128 devices in a mesh: phase: 2 (over core), dp: 64 (over x, y, z).
Axes of the slice: x: 4, y: 4, z: 4, core: 2. Of those that a mesh axis runs over, the one named last changes fastest.
Arguments:
- tokens: bfloat16 [32768, 768], P('dp'), may hold values from -6 to 6
- cotangent: bfloat16 [32768, 768], P('dp'), may hold values from -6 to 6
- lengths: int32 [128, 6], P('dp'), may hold values from 1 to 128, 256 in all within a row
- kernel_choice: int32 [128], P('dp'), may hold values from 0 to 2
- qkv_weight: float32 [768, 2304], P(('phase', 'dp')), may hold values from -0.21875 to 0.21875
- out_weight: float32 [768, 768], P(('phase', 'dp')), may hold values from -0.875 to 0.875
- ffn_in: float32 [768, 3072], P(('phase', 'dp')), may hold values from -0.21875 to 0.21875
- ffn_bias: float32 [3072], P(('phase', 'dp')), may hold values from -1.8 to 1.8
- ffn_out: float32 [3072, 768], P(('phase', 'dp')), may hold values from -0.109375 to 0.109375
- conv_in: float32 [768, 768], P(('phase', 'dp')), may hold values from -0.21875 to 0.21875
- conv_taps: float32 [15, 768], P(None, ('phase', 'dp')), may hold values from -3 to 3
- conv_out: float32 [768, 768], P(('phase', 'dp')), may hold values from -0.21875 to 0.21875
- biases: float32 [9, 768], P(None, ('phase', 'dp')), may hold values from -1.8 to 1.8
- gains: float32 [3, 768], P(None, ('phase', 'dp')), may hold values from 0.5 to 1.5
Outputs:
- block_outputs: bfloat16 [2, 32768, 768], P('phase', 'dp')
- input_grads: bfloat16 [2, 32768, 768], P('phase', 'dp')
- qkv_weight_grad: float32 [768, 2304], P(('phase', 'dp'))
- out_weight_grad: float32 [768, 768], P(('phase', 'dp'))
- ffn_in_grad: float32 [768, 3072], P(('phase', 'dp'))
- ffn_bias_grad: float32 [3072], P(('phase', 'dp'))
- ffn_out_grad: float32 [3072, 768], P(('phase', 'dp'))
- conv_in_grad: float32 [768, 768], P(('phase', 'dp'))
- conv_taps_grad: float32 [15, 768], P(None, ('phase', 'dp'))
- conv_out_grad: float32 [768, 768], P(('phase', 'dp'))
- biases_grad: float32 [9, 768], P(None, ('phase', 'dp'))
- gains_grad: float32 [3, 768], P(None, ('phase', 'dp'))
The draws below stay inside these ranges and needn't reach their ends.
Inputs may be any that keep to these rules, and one draw needn't show every extreme that they name: Each row holds the lengths of the 6 slots of one micro-batch in order and sums to 256; the last slot is padding. `kernel_choice`: 0, 1 and 2 select the kernel of 3, 5 and 7 taps.
All inputs are finite; a program needn't handle non-finite values.
Results may differ from the reference program's by a relative error of at most 0.018.
Values may be sent and summed in bfloat16 or wider, within the bound.
No kernel may reach another device: no remote copies, remote signals or barrier semaphores. Data moves between devices by JAX's collectives and lax.ppermute only.
A program may use at most 256 MiB of HBM per device.

```python
import math
import jax
import jax.numpy as jnp
import numpy as np
from jax import lax

D = 768
FF = 3072
HEAD_DIM = 64
MB_ROWS = 256
SEQS = 6
BLOCKS = 128
TOKENS = 32768


def plant(entries, stream_key, least, largest):
    extent = entries.shape
    place = [jax.random.randint(jax.random.fold_in(stream_key, axis), (), 0, extent[axis]) for axis in range(len(extent))]
    entries = entries.at[tuple(place)].set(least)
    longest = extent.index(max(extent))
    place[longest] = (place[longest] + 1) % extent[longest]
    return entries.at[tuple(place)].set(largest)


def block_scale(key, extent, pieces, least, largest):
    gain, own = 1.0, jax.random.fold_in(key, 6)
    for dim, shards_of in pieces:
        draws = jnp.exp(jax.random.uniform(jax.random.fold_in(own, dim), (shards_of,), jnp.float32, least / len(pieces), largest / len(pieces)))
        gain = gain * jnp.repeat(draws, extent[dim] // shards_of).reshape([-1 if axis == dim else 1 for axis in range(len(extent))])
    return gain


def split_up(count, total, bound, slope):
    weights = [(1 << 20) // math.isqrt(standing ** slope) + 1 for standing in range(2, count + 1)]
    surplus, given = total - bound - (count - 1), [1] * (count - 1)
    while surplus > 0:
        candidates = [i for i in range(count - 1) if given[i] < bound]
        whole, remaining = sum([weights[i] for i in candidates]), surplus
        for i in candidates:
            more = min(bound - given[i], max(1, remaining * weights[i] // whole), surplus)
            given[i] = given[i] + more
            surplus = surplus - more
    return np.array([bound] + given)


def ragged(rng, count, total, bound, lean):
    if count == 2:
        one = jax.random.randint(rng, (), max(1, total - bound), min(bound, total - 1) + 1)
        return jnp.stack([one, total - one])
    sizes = jnp.asarray(split_up(count, total, bound, lean), jnp.int32)
    couples = (count - 1) // 2
    donor, sink = sizes[1:1 + 2 * couples:2], sizes[2:2 + 2 * couples:2]
    margin = jnp.minimum(donor - 1, bound - sink)
    passed = jax.random.randint(jax.random.fold_in(rng, 1), (couples,), 0, 1 << 20) % (margin + 1)
    sizes = sizes.at[1:1 + 2 * couples:2].set(donor - passed).at[2:2 + 2 * couples:2].set(sink + passed)
    return sizes[jax.random.permutation(jax.random.fold_in(rng, 2), count)]


def centred(key, dims, spread, bound, shards=(), held_as=jnp.bfloat16):
    array = jax.random.normal(key, dims, jnp.float32) * spread
    if len(shards) > 0:
        array = block_scale(key, dims, shards, -0.22, 0.18) * array
    return jnp.clip(array, min=-bound, max=bound).astype(held_as)


def setup_inputs(seed: int = 0) -> dict:
    streams_of = jax.random.split(jax.random.key(seed), 15)
    return {
        "tokens": centred(streams_of[0], (TOKENS, D), 1.0, 6.0, ((0, 64),)),
        "cotangent": centred(streams_of[1], (TOKENS, D), 1.0, 6.0, ((0, 64),)),
        "lengths": jax.vmap(lambda own: ragged(own, SEQS, MB_ROWS, MB_ROWS // 2, 2))(jax.random.split(streams_of[2], BLOCKS)).reshape((BLOCKS, SEQS)).astype(jnp.int32),
        "kernel_choice": plant(jax.random.randint(streams_of[3], (BLOCKS,), 0, 3), jax.random.fold_in(streams_of[3], 1), 0, 2).astype(jnp.int32),
        "qkv_weight": centred(streams_of[4], (D, 3 * D), D ** -0.5, 0.21875, ((0, 128),), jnp.float32),
        "out_weight": centred(streams_of[5], (D, D), (D // 16) ** -0.5, 0.875, ((0, 128),), jnp.float32),
        "ffn_in": centred(streams_of[6], (D, FF), D ** -0.5, 0.21875, ((0, 128),), jnp.float32),
        "ffn_bias": centred(streams_of[7], (FF,), 0.3, 1.8, ((0, 128),), jnp.float32),
        "ffn_out": centred(streams_of[8], (FF, D), FF ** -0.5, 0.109375, ((0, 128),), jnp.float32),
        "conv_in": centred(streams_of[9], (D, D), D ** -0.5, 0.21875, ((0, 128),), jnp.float32),
        "conv_taps": centred(streams_of[10], (15, D), 4 ** -0.5, 3.0, ((1, 128),), jnp.float32),
        "conv_out": centred(streams_of[11], (D, D), D ** -0.5, 0.21875, ((0, 128),), jnp.float32),
        "biases": centred(streams_of[12], (9, D), 0.3, 1.8, ((1, 128),), jnp.float32),
        "gains": jnp.clip(1.0 + 0.1 * jax.random.normal(streams_of[13], (3, D), jnp.float32), 0.5, 1.5),
    }


@jax.custom_vjp
def low(v):
    return lax.optimization_barrier(v.astype(jnp.bfloat16)).astype(jnp.float32)

@jax.custom_vjp
def low_back(v):
    return v

def low_keep(v):
    return (low(v), None)

def low_pass(kept, grad):
    return (grad,)

def back_keep(v):
    return (v, None)

def back_low(kept, grad):
    return (low(grad),)
low.defvjp(low_keep, low_pass)
low_back.defvjp(back_keep, back_low)
EPSILON = 1e-05
PRECISE = lax.Precision.HIGHEST

def matmul(left_side, right_side):
    return jnp.dot(left_side, right_side, preferred_element_type=jnp.float32, precision=PRECISE)

def layer_norm(residual, gain_row, shift_row):
    centered = residual - lax.optimization_barrier(jnp.mean(residual, axis=-1, keepdims=True))
    variance = lax.optimization_barrier(jnp.mean(centered * centered, axis=-1, keepdims=True))
    return centered * lax.rsqrt(variance + EPSILON) * gain_row + shift_row

def gelu_exact(operand):
    return jax.nn.gelu(operand, approximate=False)

def tap_table():
    choice_ids = jnp.arange(3, dtype=jnp.int32)[:, None, None]
    offsets = jnp.arange(7, dtype=jnp.int32)[None, :, None] - 3
    tap_index = jnp.arange(15, dtype=jnp.int32)[None, None, :]
    radius = choice_ids + 1
    first_tap = choice_ids * choice_ids + 2 * choice_ids
    tap_hit = (jnp.abs(offsets) <= radius) & (tap_index == first_tap + offsets + radius)
    return tap_hit.astype(jnp.float32)

def segment_ids(lengths, row_count):
    slot_ends = jnp.cumsum(lengths, axis=-1).astype(jnp.int32)
    position = jnp.arange(row_count, dtype=jnp.int32)
    segment = lax.optimization_barrier(jnp.sum((position[:, None] >= slot_ends[..., None, :]).astype(jnp.int32), axis=-1)).astype(jnp.int32)
    return (segment, segment < lengths.shape[-1] - 1)

def depthwise(operand, segment, tap_rows):
    row_count = operand.shape[-2]
    pad_width = [(0, 0)] * (operand.ndim - 2) + [(3, 3), (0, 0)]
    padded = jnp.pad(operand, pad_width)
    slot_pad = jnp.pad(segment, [(0, 0)] * (segment.ndim - 1) + [(3, 3)], constant_values=-1)
    summed = jnp.zeros_like(operand)
    for offset in range(7):
        shifted = padded[..., offset:offset + row_count, :]
        inside = (slot_pad[..., offset:offset + row_count] == segment)[..., None]
        summed = summed + jnp.where(inside, shifted, 0.0) * tap_rows[..., offset:offset + 1, :]
    return summed

def forward(tokens, qkv_weight, out_weight, ffn_in, ffn_bias, ffn_out, conv_in, conv_taps, conv_out, biases, gains, zero_probe, segment, valid_rows, selection):
    model_width = tokens.shape[1]
    head_count = model_width // HEAD_DIM
    bias_rows = low(biases)
    gain_rows = low(gains)
    qkv_proj = matmul(tokens, low(qkv_weight))
    queries = low_back(low(qkv_proj[:, :model_width] + bias_rows[0]))
    key_rows = low_back(low(qkv_proj[:, model_width:2 * model_width]))
    value_rows = low_back(low(qkv_proj[:, 2 * model_width:] + bias_rows[1]))
    four_dims = (BLOCKS, MB_ROWS, head_count, HEAD_DIM)
    score_scale = HEAD_DIM ** (-0.5)
    scores = jnp.einsum('brhe,bshe->bhrs', queries.reshape(four_dims), key_rows.reshape(four_dims), precision=PRECISE) * score_scale
    diagonal = jnp.eye(MB_ROWS, dtype=jnp.bool_)
    allowed = (segment[:, :, None] == segment[:, None, :]) & (valid_rows[:, None, :] | diagonal[None])
    scores = low_back(jnp.where(allowed[:, None], scores, -1000000000.0))
    soft_weights = jax.nn.softmax(scores, axis=-1)
    attended = jnp.einsum('bhrs,bshe->brhe', low(soft_weights), value_rows.reshape(four_dims), precision=PRECISE)
    attended = low_back(low(attended.reshape(TOKENS, model_width)))
    branch = low_back(matmul(attended, low(out_weight)) + bias_rows[2])
    hidden = low(layer_norm(tokens + branch, gain_rows[0], bias_rows[3]))
    up_proj = low_back(matmul(hidden, low(ffn_in)) + low(ffn_bias))
    activated = low(gelu_exact(up_proj))
    ffn_branch = low_back(matmul(activated, low(ffn_out)) + bias_rows[4])
    phase_one = layer_norm(hidden + ffn_branch, gain_rows[1], bias_rows[5])
    sent_rows = low_back(low(phase_one) + zero_probe)
    mixed_in = low_back(matmul(sent_rows, low(conv_in)) + bias_rows[6])
    tap_rows = jnp.einsum('bjt,td->bjd', selection, low(conv_taps), precision=PRECISE)
    convolved = depthwise(mixed_in.reshape(BLOCKS, MB_ROWS, model_width), segment, tap_rows).reshape(TOKENS, model_width)
    gated_rows = low(gelu_exact(convolved))
    conv_branch = low_back(matmul(gated_rows, low(conv_out)) + bias_rows[7])
    result = layer_norm(sent_rows + conv_branch, gain_rows[2], bias_rows[8])
    return (result, sent_rows)

def reference(tokens, cotangent, lengths, kernel_choice, qkv_weight, out_weight, ffn_in, ffn_bias, ffn_out, conv_in, conv_taps, conv_out, biases, gains):
    segment, valid_rows = segment_ids(lengths, MB_ROWS)
    selection = tap_table()[kernel_choice]
    model_width = tokens.shape[1]
    zero_probe = jnp.zeros((TOKENS, model_width), jnp.float32)

    def wrapped(*weights):
        return forward(*weights, segment, valid_rows, selection)
    primals = (tokens.astype(jnp.float32), qkv_weight, out_weight, ffn_in, ffn_bias, ffn_out, conv_in, conv_taps, conv_out, biases, gains, zero_probe)
    result, pullback, sent_rows = jax.vjp(wrapped, *primals, has_aux=True)
    valid_cols = valid_rows.reshape(TOKENS, 1).astype(jnp.float32)
    gradients = pullback(cotangent.astype(jnp.float32) * valid_cols)
    block_outputs = jnp.stack([sent_rows, result]).astype(jnp.bfloat16)
    input_grads = jnp.stack([gradients[0], gradients[11]]).astype(jnp.bfloat16)
    return (block_outputs, input_grads, gradients[1], gradients[2], gradients[3], gradients[4], gradients[5], gradients[6], gradients[7], gradients[8], gradients[9], gradients[10])
```

```python
import jax
import jax.numpy as jnp
from jax import lax
from jax.sharding import PartitionSpec as P

HEAD_DIM = 64
EPSILON = 1e-05
BOTH = ("phase", "dp")
STRIDE = {"x": 16, "y": 4, "z": 1}
LANES = 384
SWAP = [(0, 1), (1, 0)]
BF = jnp.bfloat16
F32 = jnp.float32


def partners(axis, step):
    pairs = []
    for core in range(2):
        mask = (1, 3)[(core + step) % 2]
        for chip in range(64):
            coordinate = (chip // STRIDE[axis]) % 4
            target = chip + ((coordinate ^ mask) - coordinate) * STRIDE[axis]
            pairs.append((core * 64 + chip, core * 64 + target))
    return pairs


def masks():
    core = lax.axis_index("phase")
    return (jnp.where(core == 0, 1, 3), jnp.where(core == 0, 3, 1))


def coordinate_of(axis):
    return (lax.axis_index("dp") // STRIDE[axis]) % 4


def pick(stack, index):
    return lax.dynamic_index_in_dim(stack, index, 0, keepdims=False)


def gather_axis(own, axis):
    first = lax.ppermute(own, BOTH, partners(axis, 0))
    two = jnp.stack([own, first])
    far = lax.ppermute(two, BOTH, partners(axis, 1))
    here = coordinate_of(axis)
    mask_one, mask_two = masks()
    four = jnp.concatenate([two, far], axis=0)
    placed = []
    for unit in range(4):
        apart = here ^ unit
        place = jnp.where(
            apart == 0, 0, jnp.where(apart == mask_one, 1, jnp.where(apart == mask_two, 2, 3))
        )
        placed.append(pick(four, place))
    return jnp.stack(placed)


def scatter_axis(units, axis):
    here = coordinate_of(axis)
    mask_one, mask_two = masks()
    away = jnp.stack([pick(units, here ^ mask_two), pick(units, here ^ 2)]).astype(BF)
    first = lax.ppermute(away, BOTH, partners(axis, 1))
    beside = (pick(units, here ^ mask_one) + first[1].astype(F32)).astype(BF)
    second = lax.ppermute(beside, BOTH, partners(axis, 0))
    return pick(units, here) + first[0].astype(F32) + second.astype(F32)


def in_blocks(matrix):
    count = matrix.shape[-1] // LANES
    return jnp.stack([matrix[..., i * LANES : (i + 1) * LANES] for i in range(count)])


def side_by_side(blocks):
    return jnp.concatenate([blocks[i] for i in range(blocks.shape[0])], axis=-1)


def layer_norm(residual, gain_row, shift_row):
    centered = residual - jnp.mean(residual, axis=-1, keepdims=True)
    variance = jnp.mean(centered * centered, axis=-1, keepdims=True)
    inverse = lax.rsqrt(variance + EPSILON)
    normed = centered * inverse
    return (normed * gain_row + shift_row, normed, inverse)


def layer_norm_back(grad, normed, inverse, gain_row):
    scaled = grad * gain_row
    return inverse * (
        scaled
        - jnp.mean(scaled, axis=-1, keepdims=True)
        - normed * jnp.mean(scaled * normed, axis=-1, keepdims=True)
    )


def gelu(operand):
    return operand * 0.5 * (1.0 + lax.erf(operand * (0.5**0.5)))


def gelu_slope(operand):
    return 0.5 * (1.0 + lax.erf(operand * (0.5**0.5))) + operand * jnp.exp(
        -0.5 * operand * operand
    ) * (0.5 / jnp.pi) ** 0.5


def segment_ids(lengths, row_count):
    slot_ends = jnp.cumsum(lengths, axis=-1)
    position = jnp.arange(row_count, dtype=jnp.int32)
    segment = jnp.sum((position[:, None] >= slot_ends[..., None, :]).astype(jnp.int32), axis=-1)
    return (segment, segment < lengths.shape[-1] - 1)


def product(left_side, right_side):
    return jnp.dot(left_side, right_side, preferred_element_type=F32)


def product_left(left_side, right_side):
    return lax.dot_general(
        left_side, right_side, (((0,), (0,)), ((), ())), preferred_element_type=F32
    )


def product_right(left_side, right_side):
    return lax.dot_general(
        left_side, right_side, (((1,), (1,)), ((), ())), preferred_element_type=F32
    )


def column_sum(operand):
    return jnp.sum(operand.astype(F32), axis=0)


def shifted(operand, offset):
    if offset == 0:
        return operand
    pad = jnp.zeros_like(operand[:, : abs(offset)])
    if offset > 0:
        return jnp.concatenate([operand[:, offset:], pad], axis=1)
    return jnp.concatenate([pad, operand[:, :offset]], axis=1)


def core_sum(partial):
    sent = partial.astype(BF)
    return partial + lax.ppermute(sent, "phase", SWAP).astype(F32)


def gather_weights(masters):
    (qkv, out, ffn_in, ffn_bias, ffn_out, conv_in, conv_taps, conv_out, biases, gains) = masters
    core = lax.axis_index("phase")
    width = qkv.shape[1] // 3
    half, wide = width // 2, ffn_in.shape[1] // 2
    small = jnp.concatenate(
        [biases.T, gains.T, conv_taps.T, ffn_bias.reshape(4, -1).T], axis=1
    )

    def columns_of(which):
        pieces = [qkv[:, i * width + which * half : i * width + (which + 1) * half] for i in range(3)]
        pieces.append(ffn_in[:, which * wide : (which + 1) * wide])
        pieces.append(conv_in[:, which * half : (which + 1) * half])
        return in_blocks(jnp.concatenate(pieces, axis=1))

    low, high = columns_of(0), columns_of(1)
    small_pad = jnp.pad(small, ((0, 0), (0, LANES - small.shape[1])))[None]
    mine = jnp.where(core == 0, low, high)
    theirs = jnp.where(core == 0, high, low)
    arrived = lax.ppermute(jnp.concatenate([theirs, small_pad]), "phase", SWAP)
    upper, lower = jnp.where(core == 0, mine, arrived[:8]), jnp.where(core == 0, arrived[:8], mine)
    deep = jnp.stack([upper, lower], axis=1)
    both_small = jnp.concatenate(
        [small, arrived[8, :, : small.shape[1]], small_pad[0, :, : LANES - 2 * small.shape[1]]], axis=1
    )
    payload = jnp.concatenate(
        [
            deep[:3].reshape(6, 6, LANES),
            in_blocks(out),
            in_blocks(conv_out),
            deep[3:].reshape(10, 6, LANES),
            both_small[None],
        ]
    )
    along_z = gather_axis(payload, "z")
    along_z = jnp.swapaxes(along_z, 0, 1).reshape(21, 24, LANES)
    part_a, part_b, part_c = along_z[:10], along_z[10:], in_blocks(ffn_out)
    part_a = gather_axis(part_a, "x")
    part_b = gather_axis(part_b, "y")
    part_c = gather_axis(part_c, "x")
    part_a = gather_axis(part_a, "y")
    part_b = gather_axis(part_b, "x")
    part_c = gather_axis(part_c, "y")
    part_c = gather_axis(part_c, "z")
    part_a = jnp.swapaxes(part_a, 0, 1)

    def tall(part, first, blocks):
        chosen = part[:, :, first : first + blocks]
        return jnp.transpose(chosen, (0, 1, 3, 2, 4)).reshape(-1, blocks * LANES)

    def deep_of(part, first, blocks):
        chosen = part[:, :, first : first + 2 * blocks].reshape(4, 4, blocks, 2, 24, LANES)
        return jnp.transpose(chosen, (3, 0, 1, 4, 2, 5)).reshape(-1, blocks * LANES)

    full_qkv = deep_of(part_a, 0, 3)
    full_out = tall(part_a, 6, 2)
    full_conv_out = tall(part_a, 8, 2)
    full_ffn_in = deep_of(part_b, 0, 4)
    full_conv_in = deep_of(part_b, 8, 1)
    smalls = tall(part_b, 10, 1)
    full_ffn_out = jnp.transpose(part_c, (2, 1, 0, 4, 3, 5)).reshape(-1, 2 * LANES)
    mine_small = smalls[:, : small.shape[1]].astype(F32).T
    their_small = smalls[:, small.shape[1] : 2 * small.shape[1]].astype(F32).T
    row_sets = jnp.where(
        core == 0,
        jnp.concatenate([mine_small[:12], their_small[:12]], axis=1),
        jnp.concatenate([their_small[:12], mine_small[:12]], axis=1),
    )
    bias_full = mine_small[27:].reshape(4, 64, 6).transpose(1, 0, 2).reshape(-1)
    return (
        full_qkv,
        full_out,
        full_ffn_in,
        full_ffn_out,
        full_conv_in,
        full_conv_out,
        row_sets[:9],
        row_sets[9:],
        mine_small[:2],
        mine_small[12:27],
        bias_full,
    )


def scatter_gradients(qkv, out, ffn_in, ffn_out, conv_in, conv_out, small):
    def tall(matrix):
        return in_blocks(matrix.reshape(4, 4, 24, -1)).transpose(1, 2, 0, 3, 4)

    def deep(matrix):
        blocks = in_blocks(matrix.reshape(2, 4, 4, 24, -1))
        return blocks.transpose(2, 3, 0, 1, 4, 5).reshape(4, 4, -1, 24, LANES)

    small_tall = jnp.pad(small.T, ((0, 0), (0, LANES - small.shape[0])))
    part_a = jnp.concatenate([deep(qkv), tall(out), tall(conv_out)], axis=2)
    part_b = jnp.concatenate([deep(ffn_in), deep(conv_in), tall(small_tall)], axis=2)
    part_c = in_blocks(ffn_out.reshape(4, 4, 4, 24, -1)).transpose(3, 2, 1, 0, 4, 5)
    part_c = scatter_axis(part_c, "z")
    part_b = scatter_axis(part_b, "x")
    part_a = scatter_axis(jnp.swapaxes(part_a, 0, 1), "y")
    part_c = scatter_axis(part_c, "y")
    part_b = scatter_axis(part_b, "y")
    part_a = scatter_axis(part_a, "x")
    part_c = scatter_axis(part_c, "x")
    both = jnp.concatenate([part_a, part_b]).reshape(-1, 4, 6, LANES)
    mine = scatter_axis(jnp.swapaxes(both, 0, 1), "z")
    core = lax.axis_index("phase")
    grads = jnp.concatenate([mine[:6], mine[10:20]]).reshape(8, 2, 6, LANES)
    sent = jnp.where(core == 0, grads[:, 1], grads[:, 0])
    kept = jnp.where(core == 0, grads[:, 0], grads[:, 1])
    arrived = lax.ppermute(sent.astype(BF), "phase", SWAP).astype(F32)
    low, high = jnp.where(core == 0, kept, arrived), jnp.where(core == 0, arrived, kept)
    qkv_share = jnp.concatenate(
        [piece for i in range(3) for piece in (low[i], high[i])], axis=1
    )
    ffn_in_share = jnp.concatenate([side_by_side(low[3:7]), side_by_side(high[3:7])], axis=1)
    conv_in_share = jnp.concatenate([low[7], high[7]], axis=1)
    out_share = side_by_side(mine[6:8])
    conv_out_share = side_by_side(mine[8:10])
    small_share = mine[20, :, : small.shape[0]].T
    return (
        qkv_share,
        out_share,
        ffn_in_share,
        small_share[27:].reshape(-1),
        side_by_side(part_c),
        conv_in_share,
        small_share[12:27],
        conv_out_share,
        small_share[:9],
        small_share[9:12],
    )


def shards(
    tokens,
    cotangent,
    lengths,
    kernel_choice,
    *masters,
):
    core = lax.axis_index("phase")
    leading = core == 0
    batches = lengths.shape[0]
    rows, width = tokens.shape
    per_batch = rows // batches
    half = width // 2
    heads = half // HEAD_DIM
    gathered = gather_weights(tuple(piece.astype(BF) for piece in masters))
    (qkv_w, out_w, ffn_in, ffn_out, conv_in, conv_out, bias, gain, own_bias, taps, ffn_bias) = gathered
    segment, valid = segment_ids(lengths, per_batch)
    diagonal = jnp.eye(per_batch, dtype=jnp.bool_)
    allowed = (segment[:, :, None] == segment[:, None, :]) & (valid[:, None, :] | diagonal[None])
    scale = HEAD_DIM ** (-0.5)

    qkv = product(tokens, qkv_w)
    shape = (batches, per_batch, heads, HEAD_DIM)
    queries = (qkv[:, :half] + own_bias[0]).astype(BF).reshape(shape)
    keys = qkv[:, half : 2 * half].astype(BF).reshape(shape)
    values = (qkv[:, 2 * half :] + own_bias[1]).astype(BF).reshape(shape)
    scores = jnp.einsum("brhe,bshe->bhrs", queries, keys, preferred_element_type=F32) * scale
    scores = jnp.where(allowed[:, None], scores, -1e9)
    exponent = jnp.exp(scores - jnp.max(scores, axis=-1, keepdims=True))
    soft = exponent / jnp.sum(exponent, axis=-1, keepdims=True)
    soft_low = soft.astype(BF)
    attended = jnp.einsum("bhrs,bshe->brhe", soft_low, values, preferred_element_type=F32)
    attended = attended.reshape(rows, half).astype(BF)
    resid_one = tokens.astype(F32) + core_sum(product(attended, out_w)) + bias[2]
    hidden, norm_one, inverse_one = layer_norm(resid_one, gain[0], bias[3])
    hidden = hidden.astype(BF)
    up = product(hidden, ffn_in) + ffn_bias
    activated = gelu(up).astype(BF)
    resid_two = hidden.astype(F32) + core_sum(product(activated, ffn_out)) + bias[4]
    phase_one, norm_two, inverse_two = layer_norm(resid_two, gain[1], bias[5])
    phase_one = phase_one.astype(BF)

    own_conv_bias = lax.dynamic_slice_in_dim(bias[6], core * half, half)
    mixed = (product(phase_one, conv_in) + own_conv_bias).reshape(batches, per_batch, half)
    tap_rows = []
    inside = []
    for offset in range(-3, 4):
        choices = []
        for choice in range(3):
            radius = choice + 1
            first = choice * choice + 2 * choice
            if abs(offset) <= radius:
                choices.append(taps[first + offset + radius])
            else:
                choices.append(jnp.zeros((half,), F32))
        tap_rows.append(jnp.stack(choices)[kernel_choice])
        position = jnp.arange(per_batch) + offset
        there = (position >= 0) & (position < per_batch)
        inside.append(there[None] & (segment == jnp.roll(segment, -offset, axis=1)))
    convolved = jnp.zeros_like(mixed)
    for place in range(7):
        term = jnp.where(inside[place][:, :, None], shifted(mixed, place - 3), 0.0)
        convolved = convolved + term * tap_rows[place][:, None]
    gated = gelu(convolved).astype(BF).reshape(rows, half)
    resid_three = phase_one.astype(F32) + core_sum(product(gated, conv_out)) + bias[7]
    result, norm_three, inverse_three = layer_norm(resid_three, gain[2], bias[8])
    block_outputs = jnp.where(leading, phase_one, result.astype(BF))

    masked = cotangent.astype(F32) * valid.reshape(rows, 1).astype(F32)
    grad_three = layer_norm_back(masked, norm_three, inverse_three, gain[2])
    grad_branch_two = grad_three.astype(BF)
    d_conv_out = product_left(gated, grad_branch_two)
    grad_convolved = product_right(grad_branch_two, conv_out).reshape(mixed.shape) * gelu_slope(convolved)
    grad_mixed = jnp.zeros_like(mixed)
    tap_sums = []
    for place in range(7):
        there = inside[place][:, :, None]
        tap_sums.append(
            jnp.sum(jnp.where(there, grad_convolved * shifted(mixed, place - 3), 0.0), axis=1)
        )
        back = jnp.where(there, grad_convolved, 0.0)
        grad_mixed = grad_mixed + shifted(back, 3 - place) * tap_rows[place][:, None]
    d_taps = []
    for choice in range(3):
        radius = choice + 1
        chosen = (kernel_choice == choice)[:, None]
        for offset in range(-radius, radius + 1):
            d_taps.append(jnp.sum(jnp.where(chosen, tap_sums[offset + 3], 0.0), axis=0))
    grad_mixed = grad_mixed.astype(BF).reshape(rows, half)
    d_conv_in = product_left(phase_one, grad_mixed)
    grad_phase_one = (grad_three + core_sum(product_right(grad_mixed, conv_in))).astype(BF)

    arriving = grad_phase_one.astype(F32)
    grad_two = layer_norm_back(arriving, norm_two, inverse_two, gain[1])
    grad_ffn = grad_two.astype(BF)
    d_ffn_out = product_left(activated, grad_ffn)
    grad_up = (product_right(grad_ffn, ffn_out) * gelu_slope(up)).astype(BF)
    d_ffn_in = product_left(hidden, grad_up)
    grad_hidden = grad_two + core_sum(product_right(grad_up, ffn_in))
    grad_one = layer_norm_back(grad_hidden, norm_one, inverse_one, gain[0])
    grad_branch = grad_one.astype(BF)
    d_out = product_left(attended, grad_branch)
    grad_attended = product_right(grad_branch, out_w).astype(BF).reshape(shape)
    grad_soft = jnp.einsum("brhe,bshe->bhrs", grad_attended, values, preferred_element_type=F32)
    grad_values = jnp.einsum("bhrs,brhe->bshe", soft_low, grad_attended, preferred_element_type=F32)
    grad_scores = soft * (grad_soft - jnp.sum(grad_soft * soft, axis=-1, keepdims=True))
    grad_scores = grad_scores.astype(BF)
    grad_queries = jnp.einsum("bhrs,bshe->brhe", grad_scores, keys, preferred_element_type=F32) * scale
    grad_keys = jnp.einsum("bhrs,brhe->bshe", grad_scores, queries, preferred_element_type=F32) * scale
    grad_qkv = jnp.concatenate(
        [piece.astype(BF).reshape(rows, half) for piece in (grad_queries, grad_keys, grad_values)], axis=1
    )
    d_qkv = product_left(tokens, grad_qkv)
    grad_tokens = (grad_one + core_sum(product_right(grad_qkv, qkv_w))).astype(BF)
    input_grads = jnp.where(leading, grad_tokens, grad_phase_one)

    def own_half(row):
        return lax.dynamic_slice_in_dim(row, core * half, half)

    small = jnp.stack(
        [
            column_sum(grad_qkv[:, :half]),
            column_sum(grad_qkv[:, 2 * half :]),
            own_half(column_sum(grad_branch)),
            own_half(column_sum(grad_hidden)),
            own_half(column_sum(grad_ffn)),
            own_half(column_sum(arriving)),
            column_sum(grad_mixed),
            own_half(column_sum(grad_branch_two)),
            own_half(column_sum(masked)),
            own_half(column_sum(grad_hidden * norm_one)),
            own_half(column_sum(arriving * norm_two)),
            own_half(column_sum(masked * norm_three)),
        ]
        + d_taps
    )
    d_ffn_bias = column_sum(grad_up).reshape(64, 4, 6).transpose(1, 0, 2).reshape(4, half)
    shares = scatter_gradients(
        d_qkv, d_out, d_ffn_in, d_ffn_out, d_conv_in, d_conv_out, jnp.concatenate([small, d_ffn_bias])
    )
    return (block_outputs[None], input_grads[None], *shares)


def solution(mesh):
    sharded, columns = P(BOTH, None), P(None, BOTH)
    weights = (sharded, sharded, sharded, P(BOTH), sharded, sharded, columns, sharded, columns, columns)
    return jax.shard_map(
        shards,
        mesh=mesh,
        in_specs=(P("dp", None), P("dp", None), P("dp", None), P("dp"), *weights),
        out_specs=(P("phase", "dp", None), P("phase", "dp", None), *weights),
        check_vma=False,
    )
```

```python
import math

import jax
import jax.numpy as jnp
from jax import lax
from jax.experimental import pallas as pl
from jax.experimental.pallas import tpu as pltpu
from jax.sharding import PartitionSpec as P

HEAD_DIM = 64
EPSILON = 1e-05
BOTH = ("phase", "dp")
STRIDE = {"x": 16, "y": 4, "z": 1}
AXES = "xyz"
LANES = 384
SLOTS = 6
MEMORY = 16 * 1024 * 1024
SWAP = [(0, 1), (1, 0)]
BF = jnp.bfloat16
F32 = jnp.float32


def partners(axis, step):
    pairs = []
    for core in range(2):
        mask = (1, 3)[(core + step) % 2]
        for chip in range(64):
            coordinate = (chip // STRIDE[axis]) % 4
            target = chip + ((coordinate ^ mask) - coordinate) * STRIDE[axis]
            pairs.append((core * 64 + chip, core * 64 + target))
    return pairs


def line_groups():
    return [
        [core * 64 + line * 4 + z for core in range(2) for z in range(4)] for line in range(16)
    ]


def grown(held, axis, step):
    return jnp.concatenate([held, lax.ppermute(held, BOTH, partners(axis, step))])


def shrunk(kept, sent, axis, step):
    total = (kept.astype(F32) + lax.ppermute(sent, BOTH, partners(axis, step)).astype(F32)).astype(BF)
    count = total.shape[0] // 2
    return (total[:count], total[count:])


def swap(part):
    return lax.ppermute(part, "phase", SWAP)


def info_of(lengths, kernel_choice):
    core = lax.axis_index("phase").astype(jnp.int32)
    chip = lax.axis_index("dp").astype(jnp.int32)
    return jnp.concatenate(
        [
            core[None],
            kernel_choice,
            jnp.zeros((3 - kernel_choice.shape[0],), jnp.int32),
            jnp.cumsum(lengths, axis=-1).reshape(-1),
            jnp.stack([(chip // STRIDE[axis]) % 4 for axis in AXES]),
            jnp.stack([1 + 2 * core, 3 - 2 * core]),
        ]
    )


def coordinate_at(info, axis, index):
    here = info[16 + AXES.index(axis)]
    return here ^ (0, info[19], info[20], 2)[index]


def index_at(info, axis, coordinate):
    apart = info[16 + AXES.index(axis)] ^ coordinate
    return jnp.where(
        apart == 0, 0, jnp.where(apart == info[19], 1, jnp.where(apart == info[20], 2, 3))
    )


def outer_inner(order, indices):
    place = 0
    for axis in order:
        place = place * 4 + indices[axis]
    return place


def tall_rows(info, part, order, block, x):
    pieces = []
    for y in range(4):
        place = outer_inner(order, {"x": index_at(info, "x", x), "y": index_at(info, "y", y)})
        pieces.append(part[place, block].astype(F32))
    return jnp.concatenate(pieces, axis=0)


def pack_rows(info, source, order, block, kept, sent, first_row):
    for outer in range(4):
        for inner in range(4):
            place = {order[0]: coordinate_at(info, order[0], outer)}
            place[order[1]] = coordinate_at(info, order[1], inner)
            row = pl.multiple_of(first_row + 96 * place["x"] + 24 * place["y"], 8)
            piece = source[pl.ds(row, 24), :].astype(BF)
            (kept if outer < 2 else sent)[(outer % 2) * 4 + inner, block] = piece


def send_weights_kernel(
    qkv, out, ffn_in, ffn_bias, ffn_out, conv_in, conv_taps, conv_out, biases, gains,
    payload, part_c, turned,
):
    width = out.shape[1]
    half, wide = width // 2, ffn_in.shape[1] // 2
    turned[...] = jnp.zeros_like(turned)
    turned[0:9, 0:6] = biases[...]
    turned[9:12, 0:6] = gains[...]
    turned[12:27, 0:6] = conv_taps[...]
    turned[27:31, 0:6] = ffn_bias[...]
    small = jnp.transpose(turned[...])[0:6, :]
    blank = jnp.zeros((6, LANES - 128), F32)
    small = jnp.concatenate([small, blank], axis=1).astype(BF)
    for core in range(2):
        blocks = [qkv[:, third * width + core * half : third * width + (core + 1) * half] for third in range(3)]
        blocks += [out[:, i * LANES : (i + 1) * LANES] for i in range(2)]
        blocks += [conv_out[:, i * LANES : (i + 1) * LANES] for i in range(2)]
        blocks += [ffn_in[:, core * wide + i * LANES : core * wide + (i + 1) * LANES] for i in range(4)]
        blocks.append(conv_in[:, core * half : (core + 1) * half])
        blocks = [block.astype(BF) for block in blocks] + [small]
        for z in range(4):
            for place, block in enumerate(blocks):
                payload[core * 4 + z, place] = block
    for block in range(2):
        part_c[0, block] = ffn_out[:, block * LANES : (block + 1) * LANES].astype(BF)


def line_weights_kernel(info, arrived, part_a, part_b, rows):
    core = info[0]

    def whole(source, place):
        for z in range(4):
            rows[6 * z : 6 * z + 6, :] = arrived[source * 4 + z, place].astype(F32)
        return rows[...]

    for third in range(3):
        for half in range(2):
            part_a[0, third * 2 + half] = whole(half, third).astype(BF)
    for block in range(2):
        part_a[0, 6 + block] = whole(core, 3 + block).astype(BF)
        part_a[0, 8 + block] = whole(core, 5 + block).astype(BF)
    mine = whole(core, 12)[:, :128]
    theirs = whole(1 - core, 12)[:, :128]
    part_a[0, 10] = jnp.concatenate([mine, theirs, jnp.zeros_like(mine)], axis=1).astype(BF)
    for block in range(5):
        for half in range(2):
            part_b[0, block * 2 + half] = whole(half, 7 + block).astype(BF)


def send_sums_kernel(a_kept, a_came, b_kept, b_came, payload, rows):
    def spread(kept, came, place, block, cores):
        rows[...] = kept[0, place].astype(F32) + came[0, place].astype(F32)
        for core in cores:
            for z in range(4):
                payload[core * 4 + z, block] = rows[6 * z : 6 * z + 6, :].astype(BF)

    for half in range(2):
        for third in range(3):
            spread(a_kept, a_came, third * 2 + half, third, (half,))
        for block in range(5):
            spread(b_kept, b_came, block * 2 + half, 7 + block, (half,))
    for block in range(2):
        spread(a_kept, a_came, 6 + block, 3 + block, (0, 1))
        spread(b_kept, b_came, 10 + block, 5 + block, (0, 1))
    spread(a_kept, a_came, 8, 12, (0, 1))


def shares_kernel(
    info, arrived, c_kept, c_came,
    qkv, out, ffn_in, ffn_bias, ffn_out, conv_in, conv_taps, conv_out, biases, gains, turned,
):
    width = out.shape[1]
    half, wide = width // 2, ffn_in.shape[1] // 2

    def total(source, place):
        pieces = [arrived[source * 4 + z, place].astype(F32) for z in range(4)]
        return (pieces[0] + pieces[1]) + (pieces[2] + pieces[3])

    for core in range(2):
        for third in range(3):
            first = third * width + core * half
            qkv[:, first : first + half] = total(core, third)
        for block in range(4):
            first = core * wide + block * LANES
            ffn_in[:, first : first + LANES] = total(core, 7 + block)
        conv_in[:, core * half : (core + 1) * half] = total(core, 11)
    for block in range(2):
        columns = slice(block * LANES, (block + 1) * LANES)
        out[:, columns] = total(info[0], 3 + block)
        conv_out[:, columns] = total(info[0], 5 + block)
        ffn_out[:, columns] = c_kept[0, block].astype(F32) + c_came[0, block].astype(F32)
    turned[...] = jnp.zeros_like(turned)
    turned[0:6, :] = total(info[0], 12)[:, :128]
    small = jnp.transpose(turned[...])
    biases[...] = small[0:9, 0:6]
    gains[...] = small[9:12, 0:6]
    conv_taps[...] = small[12:27, 0:6]
    ffn_bias[...] = small[27:31, 0:6]


def erf_parts(operand):
    cumulative = 0.5 * (1.0 + lax.erf(operand * (0.5**0.5)))
    density = jnp.exp(-0.5 * operand * operand) * (0.5 / math.pi) ** 0.5
    return (cumulative, density)


def dot(left_side, right_side, left_dim=1, right_dim=0):
    return lax.dot_general(
        left_side, right_side, (((left_dim,), (right_dim,)), ((), ())), preferred_element_type=F32
    )


def normed(residual):
    centered = residual - jnp.mean(residual, axis=-1, keepdims=True)
    inverse = lax.rsqrt(jnp.mean(centered * centered, axis=-1, keepdims=True) + EPSILON)
    return (centered * inverse, inverse)


def normed_back(grad, norm, inverse, gain_row):
    scaled = grad * gain_row
    return inverse * (
        scaled
        - jnp.mean(scaled, axis=-1, keepdims=True)
        - norm * jnp.mean(scaled * norm, axis=-1, keepdims=True)
    )


def each(count, size, body):
    def step(index, unused):
        body(pl.ds(pl.multiple_of(index * size, size), size))
        return unused

    lax.fori_loop(0, count, step, 0)


def slots(position, ends, batch):
    number = jnp.zeros(position.shape, jnp.int32)
    for place in range(SLOTS):
        number = number + (position >= ends[4 + SLOTS * batch + place]).astype(jnp.int32)
    return number


def attention_kernel(
    info, tokens, part_a, qkv_w, out_w, conv_out, rows, taps, ffn_bias, qkv, attended, soft, part
):
    half = out_w.shape[0]
    per_batch = soft.shape[1]
    for x in range(4):
        there = slice(96 * x, 96 * x + 96)
        for block in range(3):
            columns = slice(block * LANES, (block + 1) * LANES)
            qkv_w[there, columns] = tall_rows(info, part_a, "yx", block * 2, x).astype(BF)
            below = slice(half + 96 * x, half + 96 * x + 96)
            qkv_w[below, columns] = tall_rows(info, part_a, "yx", block * 2 + 1, x).astype(BF)
        for block in range(2):
            columns = slice(block * LANES, (block + 1) * LANES)
            out_w[there, columns] = tall_rows(info, part_a, "yx", 6 + block, x).astype(BF)
            conv_out[there, columns] = tall_rows(info, part_a, "yx", 8 + block, x).astype(BF)
    small = jnp.concatenate([tall_rows(info, part_a, "yx", 10, x) for x in range(4)], axis=0)
    mine = jnp.transpose(small[:, 0:128])
    theirs = jnp.transpose(small[:, 128:256])
    rows[...] = jnp.zeros_like(rows)
    left, right = jnp.where(info[0] == 0, mine, theirs), jnp.where(info[0] == 0, theirs, mine)
    rows[0:12, :half] = left[0:12, :]
    rows[0:12, half:] = right[0:12, :]
    rows[12:14, :half] = mine[0:2, :]
    rows[14:15, :half] = mine[6:7, :]
    taps[...] = jnp.zeros_like(taps)
    taps[0:15, :] = mine[12:27, :]
    ffn_bias[...] = mine[27:31, :]
    for third in range(3):
        columns = slice(third * half, (third + 1) * half)
        block = dot(tokens[...], qkv_w[:, columns])
        if third != 1:
            block = block + rows[12 + third // 2 : 13 + third // 2, :half]
        qkv[:, columns] = block.astype(BF)
    square = (per_batch, per_batch)
    down = lax.broadcasted_iota(jnp.int32, square, 0)
    across = lax.broadcasted_iota(jnp.int32, square, 1)
    lane = lax.broadcasted_iota(jnp.int32, (per_batch, 128), 1)
    pairs = half // 128
    for batch in range(tokens.shape[0] // per_batch):
        there = slice(batch * per_batch, (batch + 1) * per_batch)
        slot_down, slot_across = slots(down, info, batch), slots(across, info, batch)
        allowed = (slot_down == slot_across) & ((slot_across < SLOTS - 1) | (down == across))
        forbidden = jnp.where(allowed, 0.0, -1e9)
        for pair in range(pairs):
            columns = slice(pair * 128, (pair + 1) * 128)
            query = qkv[there, columns]
            key = qkv[there, half + pair * 128 : half + (pair + 1) * 128]
            value = qkv[there, 2 * half + pair * 128 : 2 * half + (pair + 1) * 128]
            result = jnp.zeros((per_batch, 128), F32)
            for side in range(2):
                mine = (lane >= HEAD_DIM) if side else (lane < HEAD_DIM)
                scores = dot(jnp.where(mine, query, jnp.zeros_like(query)), key, 1, 1)
                scores = scores * HEAD_DIM ** (-0.5) + forbidden
                exponent = jnp.exp(scores - jnp.max(scores, axis=-1, keepdims=True))
                weight = (exponent * (1.0 / jnp.sum(exponent, axis=-1, keepdims=True))).astype(BF)
                soft[(batch * pairs + pair) * 2 + side] = weight
                result = result + dot(weight, jnp.where(mine, value, jnp.zeros_like(value)))
            attended[there, columns] = result.astype(BF)
    part[...] = dot(attended[...], out_w[...]).astype(BF)


def feed_kernel(
    info, tokens, mine, theirs, rows, part_b, part_c, ffn_bias,
    ffn_in, ffn_out, conv_in, hidden, norm, inverse, activated, slope, part,
):
    half = conv_in.shape[1]
    for x in range(4):
        for side in range(2):
            there = slice(half * side + 96 * x, half * side + 96 * x + 96)
            for block in range(4):
                columns = slice(block * LANES, (block + 1) * LANES)
                ffn_in[there, columns] = tall_rows(info, part_b, "xy", block * 2 + side, x).astype(BF)
            conv_in[there, :] = tall_rows(info, part_b, "xy", 8 + side, x).astype(BF)
        for y in range(4):
            for block in range(2):
                pieces = []
                for z in range(4):
                    indices = {
                        axis: index_at(info, axis, coordinate)
                        for axis, coordinate in zip(AXES, (x, y, z))
                    }
                    pieces.append(part_c[outer_inner("zyx", indices), block].astype(F32))
                row = 384 * x + 96 * y
                ffn_out[row : row + 96, block * LANES : (block + 1) * LANES] = jnp.concatenate(
                    pieces, axis=0
                ).astype(BF)

    def first(there):
        residual = (
            tokens[there, :].astype(F32)
            + (mine[there, :].astype(F32) + theirs[there, :].astype(F32))
            + rows[2:3, :]
        )
        unit, scale = normed(residual)
        norm[there, :] = unit
        inverse[there, :] = jnp.broadcast_to(scale, (scale.shape[0], 128))
        hidden[there, :] = (unit * rows[9:10, :] + rows[3:4, :]).astype(BF)

    each(tokens.shape[0] // 64, 64, first)
    wide = ffn_in.shape[1]
    chunk = 256

    def second(index, unused):
        columns = pl.ds(pl.multiple_of(index * chunk, chunk), chunk)
        up = dot(hidden[...], ffn_in[:, columns]) + ffn_bias[0:1, columns]
        cumulative, density = erf_parts(up)
        activated[:, columns] = (up * cumulative).astype(BF)
        slope[:, columns] = (cumulative + up * density).astype(BF)
        return unused

    lax.fori_loop(0, wide // chunk, second, 0)
    part[...] = dot(activated[...], ffn_out[...]).astype(BF)


def tap_row(taps, info, batch, offset):
    choice = info[1 + batch]
    row = taps[11 + offset : 12 + offset, :]
    row = jnp.where(choice == 1, taps[5 + offset : 6 + offset, :] if abs(offset) < 3 else 0.0, row)
    return jnp.where(choice == 0, taps[1 + offset : 2 + offset, :] if abs(offset) < 2 else 0.0, row)


def fill_slots(info, padded, per_batch, batches):
    position = lax.broadcasted_iota(jnp.int32, (per_batch, 128), 0)
    outside = jnp.full((8, 128), -1, jnp.int32)
    for batch in range(batches):
        padded[batch, 0:8, :] = outside
        padded[batch, 8 : 8 + per_batch, :] = slots(position, info, batch)
        padded[batch, 8 + per_batch :, :] = outside


def clear_edges(padded, per_batch, batches):
    edge = jnp.zeros((8, padded.shape[2]), F32)
    for batch in range(batches):
        padded[batch, 0:8, :] = edge
        padded[batch, 8 + per_batch :, :] = edge


def convolution_kernel(
    info, hidden, mine, theirs, rows, conv_in, taps, conv_out,
    phase_one, norm, inverse, mixed, gated, slope, part, slot_pad, mixed_pad,
):
    batches = slot_pad.shape[0]
    per_batch = hidden.shape[0] // batches
    half = conv_in.shape[1]

    def first(there):
        residual = (
            hidden[there, :].astype(F32)
            + (mine[there, :].astype(F32) + theirs[there, :].astype(F32))
            + rows[4:5, :]
        )
        unit, scale = normed(residual)
        norm[there, :] = unit
        inverse[there, :] = jnp.broadcast_to(scale, (scale.shape[0], 128))
        phase_one[there, :] = (unit * rows[10:11, :] + rows[5:6, :]).astype(BF)

    each(hidden.shape[0] // 64, 64, first)
    fill_slots(info, slot_pad, per_batch, batches)
    clear_edges(mixed_pad, per_batch, batches)
    mixed[...] = dot(phase_one[...], conv_in[...]) + rows[14:15, :half]
    for batch in range(batches):
        there = slice(batch * per_batch, (batch + 1) * per_batch)
        mixed_pad[batch, 8 : 8 + per_batch, :] = mixed[there, :]
        for column in range(half // 128):
            columns = slice(column * 128, (column + 1) * 128)
            here = slot_pad[batch, 8 : 8 + per_batch, :]
            total = jnp.zeros((per_batch, 128), F32)
            for offset in range(-3, 4):
                same = slot_pad[batch, 8 + offset : 8 + offset + per_batch, :] == here
                moved = mixed_pad[batch, 8 + offset : 8 + offset + per_batch, columns]
                tap = tap_row(taps, info, batch, offset)[:, columns]
                total = total + jnp.where(same, moved, 0.0) * tap
            cumulative, density = erf_parts(total)
            gated[there, columns] = (total * cumulative).astype(BF)
            slope[there, columns] = cumulative + total * density
    part[...] = dot(gated[...], conv_out[...]).astype(BF)


def own(info, row):
    half = row.shape[1] // 2
    return jnp.where(info[0] == 0, row[:, :half], row[:, half:])


def convolution_back_kernel(
    info, phase_one, mine, theirs, cotangent, rows, conv_in, taps, conv_out, mixed, gated, slope,
    result, grad_three, kept, sent, part, sums, d_taps,
    slot_pad, mixed_pad, grad_pad, grad_low, grad_mixed, wide_sums, whole,
):
    batches = slot_pad.shape[0]
    per_batch = phase_one.shape[0] // batches
    half = conv_in.shape[1]
    fill_slots(info, slot_pad, per_batch, batches)
    clear_edges(mixed_pad, per_batch, batches)
    clear_edges(grad_pad, per_batch, batches)
    wide_sums[...] = jnp.zeros_like(wide_sums)
    size = 64
    for batch in range(batches):

        def first(index, unused):
            inner = pl.multiple_of(index * size, size)
            there = pl.ds(pl.multiple_of(batch * per_batch + inner, size), size)
            residual = (
                phase_one[there, :].astype(F32)
                + (mine[there, :].astype(F32) + theirs[there, :].astype(F32))
                + rows[7:8, :]
            )
            unit, scale = normed(residual)
            ended = (unit * rows[11:12, :] + rows[8:9, :]).astype(BF)
            result[there, :] = jnp.where(info[0] == 0, phase_one[there, :], ended)
            valid = slot_pad[batch, pl.ds(pl.multiple_of(8 + inner, 8), size), :][:, :1] < SLOTS - 1
            masked = jnp.where(valid, cotangent[there, :].astype(F32), 0.0)
            grad = normed_back(masked, unit, scale, rows[11:12, :])
            grad_three[there, :] = grad
            low = grad.astype(BF)
            grad_low[there, :] = low
            wide_sums[0:1, :] += jnp.sum(low.astype(F32), axis=0, keepdims=True)
            wide_sums[1:2, :] += jnp.sum(masked, axis=0, keepdims=True)
            wide_sums[2:3, :] += jnp.sum(masked * unit, axis=0, keepdims=True)
            return unused

        lax.fori_loop(0, per_batch // size, first, 0)
    for block in range(2):
        columns = slice(block * LANES, (block + 1) * LANES)
        whole[0:half, :] = dot(gated[...], grad_low[:, columns], 0, 0)
        pack_rows(info, whole, "xy", 2 + block, kept, sent, 0)
    tap_sums = [[[] for offset in range(7)] for batch in range(batches)]
    for batch in range(batches):
        there = slice(batch * per_batch, (batch + 1) * per_batch)
        grad_pad[batch, 8 : 8 + per_batch, :] = (
            dot(grad_low[there, :], conv_out[...], 1, 1) * slope[there, :]
        )
        mixed_pad[batch, 8 : 8 + per_batch, :] = mixed[there, :]
        for column in range(half // 128):
            columns = slice(column * 128, (column + 1) * 128)
            here = slot_pad[batch, 8 : 8 + per_batch, :]
            grad = grad_pad[batch, 8 : 8 + per_batch, columns]
            total = jnp.zeros((per_batch, 128), F32)
            for offset in range(-3, 4):
                away = slice(8 + offset, 8 + offset + per_batch)
                same = slot_pad[batch, away, :] == here
                tap = tap_row(taps, info, batch, -offset)[:, columns]
                total = total + jnp.where(same, grad_pad[batch, away, columns], 0.0) * tap
                term = jnp.where(same, mixed_pad[batch, away, columns], 0.0) * grad
                tap_sums[batch][offset + 3].append(jnp.sum(term, axis=0, keepdims=True))
            grad_mixed[there, columns] = total.astype(BF)
    for choice in range(3):
        for offset in range(-choice - 1, choice + 2):
            row = choice * choice + 2 * choice + offset + choice + 1
            total = jnp.zeros((1, half), F32)
            for batch in range(batches):
                joined = jnp.concatenate(tap_sums[batch][offset + 3], axis=1)
                total = total + jnp.where(info[1 + batch] == choice, joined, 0.0)
            d_taps[row : row + 1, :] = total
    d_taps[15:16, :] = jnp.zeros((1, half), F32)
    whole[...] = dot(phase_one[...], grad_mixed[...], 0, 0)
    for side in range(2):
        pack_rows(info, whole, "xy", side, kept, sent, side * half)
    part[...] = dot(grad_mixed[...], conv_in[...], 1, 1).astype(BF)
    sums[0:1, :] = jnp.sum(grad_mixed[...].astype(F32), axis=0, keepdims=True)
    for place in range(3):
        sums[place + 1 : place + 2, :] = own(info, wide_sums[place : place + 1, :])
    sums[4:8, :] = jnp.zeros((4, half), F32)


def feed_back_kernel(
    info, grad_three, mine, theirs, norm, inverse, rows, activated, slope, hidden, ffn_in, ffn_out,
    conv_kept, conv_sent,
    grad_phase_one, grad_two, b_kept, b_sent, c_kept, c_sent, part, sums, bias_sums,
    grad_low, grad_up, wide_sums, whole,
):
    wide_sums[...] = jnp.zeros_like(wide_sums)

    def first(there):
        arriving = grad_three[there, :] + (mine[there, :].astype(F32) + theirs[there, :].astype(F32))
        arriving = arriving.astype(BF)
        grad_phase_one[there, :] = arriving
        arriving = arriving.astype(F32)
        unit = norm[there, :]
        grad = normed_back(arriving, unit, inverse[there, :1], rows[10:11, :])
        grad_two[there, :] = grad
        low = grad.astype(BF)
        grad_low[there, :] = low
        wide_sums[0:1, :] += jnp.sum(low.astype(F32), axis=0, keepdims=True)
        wide_sums[1:2, :] += jnp.sum(arriving, axis=0, keepdims=True)
        wide_sums[2:3, :] += jnp.sum(arriving * unit, axis=0, keepdims=True)

    each(hidden.shape[0] // 64, 64, first)
    half = ffn_in.shape[0] // 2
    for block in range(ffn_in.shape[1] // LANES):
        columns = slice(block * LANES, (block + 1) * LANES)
        grad = dot(grad_low[...], ffn_out[columns, :], 1, 1) * slope[:, columns].astype(F32)
        low = grad.astype(BF)
        grad_up[:, columns] = low
        bias_sums[0:1, columns] = jnp.sum(low.astype(F32), axis=0, keepdims=True)
        whole[...] = dot(hidden[...], low, 0, 0)
        for side in range(2):
            pack_rows(info, whole, "xy", block * 2 + side, b_kept, b_sent, side * half)
    for place in range(8):
        for block in range(4):
            b_kept[place, 8 + block] = conv_kept[place, block]
            b_sent[place, 8 + block] = conv_sent[place, block]
    for step in range(4):
        x = coordinate_at(info, "x", step)
        there = pl.ds(pl.multiple_of(x * 384, 128), 384)
        for block in range(2):
            columns = slice(block * LANES, (block + 1) * LANES)
            whole[0:384, :] = dot(activated[:, there], grad_low[:, columns], 0, 0)
            for outer in range(4):
                for inner in range(4):
                    z, y = coordinate_at(info, "z", outer), coordinate_at(info, "y", inner)
                    piece = whole[pl.ds(pl.multiple_of(96 * y + 24 * z, 8), 24), :].astype(BF)
                    place = ((outer % 2) * 4 + inner) * 4 + step
                    (c_kept if outer < 2 else c_sent)[place, block] = piece
    part[...] = dot(grad_up[...], ffn_in[...], 1, 1).astype(BF)
    for place in range(3):
        sums[place : place + 1, :] = own(info, wide_sums[place : place + 1, :])
    sums[3:8, :] = jnp.zeros((5, sums.shape[1]), F32)


def attention_back_kernel(
    info, grad_two, mine, theirs, norm, inverse, rows, tokens, qkv, attended, soft, qkv_w, out_w,
    sums_two, sums_three, d_taps, d_ffn_bias,
    grad_one, kept, sent, part, grad_low, grad_attended, grad_qkv, wide_sums, whole, sums,
):
    half = out_w.shape[0]
    per_batch = soft.shape[1]
    wide_sums[...] = jnp.zeros_like(wide_sums)

    def first(there):
        arriving = grad_two[there, :] + (mine[there, :].astype(F32) + theirs[there, :].astype(F32))
        unit = norm[there, :]
        grad = normed_back(arriving, unit, inverse[there, :1], rows[9:10, :])
        grad_one[there, :] = grad
        low = grad.astype(BF)
        grad_low[there, :] = low
        wide_sums[0:1, :] += jnp.sum(low.astype(F32), axis=0, keepdims=True)
        wide_sums[1:2, :] += jnp.sum(arriving, axis=0, keepdims=True)
        wide_sums[2:3, :] += jnp.sum(arriving * unit, axis=0, keepdims=True)

    each(tokens.shape[0] // 64, 64, first)
    for block in range(2):
        columns = slice(block * LANES, (block + 1) * LANES)
        whole[0:half, :] = dot(attended[...], grad_low[:, columns], 0, 0)
        pack_rows(info, whole, "yx", 6 + block, kept, sent, 0)
    grad_attended[...] = dot(grad_low[...], out_w[...], 1, 1).astype(BF)
    lane = lax.broadcasted_iota(jnp.int32, (per_batch, 128), 1)
    pairs = half // 128
    scale = HEAD_DIM ** (-0.5)
    for batch in range(tokens.shape[0] // per_batch):
        there = slice(batch * per_batch, (batch + 1) * per_batch)
        for pair in range(pairs):
            columns = [
                slice(third * half + pair * 128, third * half + (pair + 1) * 128) for third in range(3)
            ]
            query, key, value = (qkv[there, columns[third]] for third in range(3))
            grad = grad_attended[there, columns[0]]
            totals = [jnp.zeros((per_batch, 128), F32) for third in range(3)]
            for side in range(2):
                mine_lanes = (lane >= HEAD_DIM) if side else (lane < HEAD_DIM)

                def only(operand):
                    return jnp.where(mine_lanes, operand, jnp.zeros_like(operand))

                weight = soft[(batch * pairs + pair) * 2 + side]
                grad_side = only(grad)
                grad_soft = dot(grad_side, value, 1, 1)
                weight_wide = weight.astype(F32)
                inner = jnp.sum(grad_soft * weight_wide, axis=-1, keepdims=True)
                grad_scores = (weight_wide * (grad_soft - inner)).astype(BF)
                totals[0] = totals[0] + dot(grad_scores, only(key))
                totals[1] = totals[1] + dot(grad_scores, only(query), 0, 0)
                totals[2] = totals[2] + dot(weight, grad_side, 0, 0)
            grad_qkv[there, columns[0]] = (totals[0] * scale).astype(BF)
            grad_qkv[there, columns[1]] = (totals[1] * scale).astype(BF)
            grad_qkv[there, columns[2]] = totals[2].astype(BF)
    part[...] = dot(grad_qkv[...], qkv_w[...], 1, 1).astype(BF)
    sums[...] = jnp.zeros_like(sums)
    for third in range(3):
        columns = slice(third * half, (third + 1) * half)
        whole[...] = dot(tokens[...], grad_qkv[:, columns], 0, 0)
        for side in range(2):
            pack_rows(info, whole, "yx", third * 2 + side, kept, sent, side * half)
        if third != 1:
            place = third // 2
            sums[place : place + 1, :] = jnp.sum(
                grad_qkv[:, columns].astype(F32), axis=0, keepdims=True
            )
    sums[2:3, :] = own(info, wide_sums[0:1, :])
    sums[3:4, :] = own(info, wide_sums[1:2, :])
    sums[4:6, :] = sums_two[0:2, :]
    sums[6:9, :] = sums_three[0:3, :]
    sums[9:10, :] = own(info, wide_sums[2:3, :])
    sums[10:11, :] = sums_two[2:3, :]
    sums[11:12, :] = sums_three[3:4, :]
    sums[12:27, :] = d_taps[0:15, :]
    sums[27:31, :] = d_ffn_bias[...]
    whole[0:half, :] = jnp.zeros((half, LANES), F32)
    whole[0:half, 0:128] = jnp.transpose(sums[...])
    pack_rows(info, whole, "yx", 8, kept, sent, 0)


def kernel_call(body, outputs, scratch, has_info, *operands):
    vmem = pl.BlockSpec(memory_space=pltpu.VMEM)
    smem = pl.BlockSpec(memory_space=pltpu.SMEM)
    return pl.pallas_call(
        body,
        out_shape=[jax.ShapeDtypeStruct(shape, dtype) for shape, dtype in outputs],
        in_specs=[smem if has_info and place == 0 else vmem for place in range(len(operands))],
        out_specs=[vmem] * len(outputs),
        scratch_shapes=[pltpu.VMEM(shape, dtype) for shape, dtype in scratch],
        compiler_params=pltpu.CompilerParams(vmem_limit_bytes=MEMORY),
    )(*operands)


def gather_weights(info, masters):
    (qkv, out, ffn_in, ffn_bias, ffn_out, conv_in, conv_taps, conv_out, biases, gains) = masters
    payload, part_c = kernel_call(
        send_weights_kernel,
        [((8, 13, 6, LANES), BF), ((1, 2, ffn_out.shape[0], LANES), BF)],
        [((128, 128), F32)],
        False,
        qkv, out, ffn_in, ffn_bias.reshape(4, -1), ffn_out, conv_in, conv_taps, conv_out, biases, gains,
    )
    for step in range(2):
        part_c = grown(part_c, "x", step)
    arrived = lax.all_to_all(payload, BOTH, 0, 0, tiled=True, axis_index_groups=line_groups())
    part_a, part_b = kernel_call(
        line_weights_kernel,
        [((1, 11, 24, LANES), BF), ((1, 10, 24, LANES), BF)],
        [((24, LANES), F32)],
        True,
        info, arrived,
    )
    for axes in ("xyy", "yxz"):
        for step in range(2):
            part_a = grown(part_a, axes[0], step)
            part_b = grown(part_b, axes[1], step)
            part_c = grown(part_c, axes[2], step)
    return (part_a, part_b, part_c)


def shards(
    tokens,
    cotangent,
    lengths,
    kernel_choice,
    *masters,
):
    batches = lengths.shape[0]
    rows, width = tokens.shape
    per_batch = rows // batches
    half = width // 2
    wide = masters[2].shape[1] // 2
    heads = half // HEAD_DIM
    info = info_of(lengths, kernel_choice)
    part_a, part_b, part_c = gather_weights(info, masters)
    low, full = ((rows, width), BF), ((rows, width), F32)
    narrow = ((rows, 128), F32)
    slot_pad = ((batches, per_batch + 16, 128), jnp.int32)
    row_pad = ((batches, per_batch + 16, half), F32)
    whole = ((width, LANES), F32)

    def halves(blocks):
        return [((8, blocks, 24, LANES), BF)] * 2

    qkv_w, out_w, conv_out, all_rows, taps, ffn_bias, qkv, attended, soft, part = kernel_call(
        attention_kernel,
        [
            ((width, 3 * half), BF), ((half, width), BF), ((half, width), BF), ((16, width), F32),
            ((16, half), F32), ((4, half), F32), ((rows, 3 * half), BF), ((rows, half), BF),
            ((batches * heads, per_batch, per_batch), BF), low,
        ],
        [],
        True,
        info, tokens, part_a,
    )
    ffn_bias = ffn_bias.reshape(4, 64, 6).transpose(1, 0, 2).reshape(1, wide)
    ffn_in, ffn_out, conv_in, hidden, norm_one, inverse_one, activated, slope_up, part_two = kernel_call(
        feed_kernel,
        [
            ((width, wide), BF), ((wide, width), BF), ((width, half), BF),
            low, full, narrow, ((rows, wide), BF), ((rows, wide), BF), low,
        ],
        [],
        True,
        info, tokens, part, swap(part), all_rows, part_b, part_c, ffn_bias,
    )
    phase_one, norm_two, inverse_two, mixed, gated, slope, part_three = kernel_call(
        convolution_kernel,
        [low, full, narrow, ((rows, half), F32), ((rows, half), BF), ((rows, half), F32), low],
        [slot_pad, row_pad],
        True,
        info, hidden, part_two, swap(part_two), all_rows, conv_in, taps, conv_out,
    )
    block_outputs, grad_three, conv_kept, conv_sent, part, sums_three, d_taps = kernel_call(
        convolution_back_kernel,
        [low, full, *halves(4), low, ((8, half), F32), ((16, half), F32)],
        [slot_pad, row_pad, row_pad, low, ((rows, half), BF), ((8, width), F32), whole],
        True,
        info, phase_one, part_three, swap(part_three), cotangent, all_rows, conv_in, taps, conv_out,
        mixed, gated, slope,
    )
    grad_phase_one, grad_two, b_kept, b_sent, c_kept, c_sent, part, sums_two, d_ffn_bias = kernel_call(
        feed_back_kernel,
        [
            low, full, *halves(12), ((32, 2, 24, LANES), BF), ((32, 2, 24, LANES), BF), low,
            ((8, half), F32), ((1, wide), F32),
        ],
        [low, ((rows, wide), BF), ((8, width), F32), whole],
        True,
        info, grad_three, part, swap(part), norm_two, inverse_two, all_rows, activated, slope_up, hidden,
        ffn_in, ffn_out, conv_kept, conv_sent,
    )
    d_ffn_bias = d_ffn_bias.reshape(64, 4, 6).transpose(1, 0, 2).reshape(4, half)
    grad_one, a_kept, a_sent, part = kernel_call(
        attention_back_kernel,
        [full, *halves(9), low],
        [low, ((rows, half), BF), ((rows, 3 * half), BF), ((8, width), F32), whole, ((128, half), F32)],
        True,
        info, grad_two, part, swap(part), norm_one, inverse_one, all_rows, tokens, qkv, attended, soft,
        qkv_w, out_w, sums_two, sums_three, d_taps, d_ffn_bias,
    )
    grad_tokens = (grad_one + (part.astype(F32) + swap(part).astype(F32))).astype(BF)
    input_grads = jnp.where(lax.axis_index("phase") == 0, grad_tokens, grad_phase_one)

    for axis in "zy":
        for step in (1, 0):
            c_kept, c_sent = shrunk(c_kept, c_sent, axis, step)
    c_kept, c_sent = shrunk(c_kept, c_sent, "x", 1)
    for step in (1, 0):
        b_kept, b_sent = shrunk(b_kept, b_sent, "x", step)
    b_kept, b_sent = shrunk(b_kept, b_sent, "y", 1)
    for step in (1, 0):
        a_kept, a_sent = shrunk(a_kept, a_sent, "y", step)
    a_kept, a_sent = shrunk(a_kept, a_sent, "x", 1)
    (payload,) = kernel_call(
        send_sums_kernel,
        [((8, 13, 6, LANES), BF)],
        [((24, LANES), F32)],
        False,
        a_kept, lax.ppermute(a_sent, BOTH, partners("x", 0)),
        b_kept, lax.ppermute(b_sent, BOTH, partners("y", 0)),
    )
    arrived = lax.all_to_all(payload, BOTH, 0, 0, tiled=True, axis_index_groups=line_groups())
    shapes = [master.shape for master in masters]
    shapes[3] = (4, shapes[3][0] // 4)
    shares = list(
        kernel_call(
            shares_kernel,
            [(shape, F32) for shape in shapes],
            [((128, 128), F32)],
            True,
            info, arrived, c_kept, lax.ppermute(c_sent, BOTH, partners("x", 0)),
        )
    )
    shares[3] = shares[3].reshape(-1)
    return (block_outputs[None], input_grads[None], *shares)


def solution(mesh):
    sharded, columns = P(BOTH, None), P(None, BOTH)
    weights = (sharded, sharded, sharded, P(BOTH), sharded, sharded, columns, sharded, columns, columns)
    return jax.shard_map(
        shards,
        mesh=mesh,
        in_specs=(P("dp", None), P("dp", None), P("dp", None), P("dp"), *weights),
        out_specs=(P("phase", "dp", None), P("phase", "dp", None), *weights),
        check_vma=False,
    )
```

```python
import math

import jax
import jax.numpy as jnp
import numpy as np
from jax import lax
from jax.experimental import pallas as pl
from jax.experimental.pallas import tpu as pltpu
from jax.sharding import PartitionSpec as P

HEAD_DIM = 64
EPSILON = 1e-05
BOTH = ("phase", "dp")
STRIDE = {"x": 16, "y": 4, "z": 1}
AXES = "xyz"
LANES = 384
SLOTS = 6
SWAP = [(0, 1), (1, 0)]
BF = jnp.bfloat16
F32 = jnp.float32


def partners(axis, step):
    pairs = []
    for core in range(2):
        mask = (1, 3)[(core + step) % 2]
        for chip in range(64):
            coordinate = (chip // STRIDE[axis]) % 4
            target = chip + ((coordinate ^ mask) - coordinate) * STRIDE[axis]
            pairs.append((core * 64 + chip, core * 64 + target))
    return pairs


def grown(held, axis, step):
    return jnp.concatenate([held, lax.ppermute(held, BOTH, partners(axis, step))])


def shrunk(kept, sent, axis, step):
    came = lax.ppermute(sent, BOTH, partners(axis, step))
    count = kept.shape[0] // 2
    return tuple(
        (kept[there].astype(F32) + came[there].astype(F32)).astype(BF)
        for there in (slice(0, count), slice(count, 2 * count))
    )


def swap(part):
    return lax.ppermute(part, "phase", SWAP)


def bias_order():
    table = np.zeros((LANES, LANES), np.float32)
    for i in range(4):
        for d in range(16):
            for j in range(6):
                table[96 * i + 6 * d + j, 24 * d + 6 * i + j] = 1.0
    return jnp.asarray(table, BF)


def info_of(lengths, kernel_choice):
    core = lax.axis_index("phase").astype(jnp.int32)
    chip = lax.axis_index("dp").astype(jnp.int32)
    return jnp.concatenate(
        [
            core[None],
            kernel_choice,
            jnp.zeros((3 - kernel_choice.shape[0],), jnp.int32),
            jnp.cumsum(lengths, axis=-1).reshape(-1),
            jnp.stack([(chip // STRIDE[axis]) % 4 for axis in AXES]),
            jnp.stack([1 + 2 * core, 3 - 2 * core]),
        ]
    )


def coordinate_at(info, axis, index):
    here = info[16 + AXES.index(axis)]
    return here ^ (0, info[19], info[20], 2)[index]


def index_at(info, axis, coordinate):
    apart = info[16 + AXES.index(axis)] ^ coordinate
    return jnp.where(
        apart == 0, 0, jnp.where(apart == info[19], 1, jnp.where(apart == info[20], 2, 3))
    )


def outer_inner(order, indices):
    place = 0
    for axis in order:
        place = place * 4 + indices[axis]
    return place


def tall_rows(info, part, order, block, x):
    pieces = []
    for y in range(4):
        place = outer_inner(order, {"x": index_at(info, "x", x), "y": index_at(info, "y", y)})
        pieces.append(part[place, block].astype(F32))
    return jnp.concatenate(pieces, axis=0)


def pack_rows(info, source, order, block, kept, sent, first_row):
    for outer in range(4):
        for inner in range(4):
            place = {order[0]: coordinate_at(info, order[0], outer)}
            place[order[1]] = coordinate_at(info, order[1], inner)
            row = pl.multiple_of(first_row + 96 * place["x"] + 24 * place["y"], 8)
            piece = source[pl.ds(row, 24), :].astype(BF)
            (kept if outer < 2 else sent)[(outer % 2) * 4 + inner, block] = piece


def send_weights_kernel(
    flow, core, qkv, out, ffn_in, ffn_bias, ffn_out, conv_in, conv_taps, conv_out, biases, gains,
    mine, theirs, part_c, turned,
):
    width = out.shape[1]
    half, wide = width // 2, ffn_in.shape[1] // 2
    turned[...] = jnp.zeros_like(turned)
    flow.arrive()
    for block in range(2):
        part_c[0, block] = ffn_out[:, block * LANES : (block + 1) * LANES].astype(BF)
    turned[9:12, 0:6] = gains[...]
    for i in range(4):
        turned[27 + i : 28 + i, 0:6] = ffn_bias[0:1, 6 * i : 6 * i + 6]
    turned[0:8, :] = jnp.transpose(turned[...])[0:8, :]
    turned[0:6, 0:9] = biases[...]
    turned[0:6, 12:27] = conv_taps[...]
    small = turned[0:6, :]
    blank = jnp.zeros((6, LANES - 128), F32)
    small = jnp.concatenate([small, blank], axis=1).astype(BF)

    def pair(source, first, apart):
        return (source[:, first : first + LANES], source[:, first + apart : first + apart + LANES])

    places = [pair(qkv, third * width, half) for third in range(3)]
    places += [pair(ffn_in, block * LANES, wide) for block in range(4)]
    places.append(pair(conv_in, 0, half))
    for place, (low, high) in enumerate(places):
        mine[0, place] = jnp.where(core[0] == 0, low, high).astype(BF)
        theirs[0, place] = jnp.where(core[0] == 0, high, low).astype(BF)
    mine[0, 8] = small
    theirs[0, 8] = small
    for block in range(2):
        columns = slice(block * LANES, (block + 1) * LANES)
        mine[0, 9 + block] = out[:, columns].astype(BF)
        mine[0, 11 + block] = conv_out[:, columns].astype(BF)


def line_weights_kernel(info, held, came, part_a, part_b, rows):
    core = info[0]

    def whole(place):
        for z in range(4):
            source = index_at(info, "z", z)
            near = held[source % 2, place].astype(F32)
            far = came[source % 2, place].astype(F32)
            rows[6 * z : 6 * z + 6, :] = jnp.where(source < 2, near, far)
        return rows[...]

    for third in range(3):
        part_a[0, third * 2 + core] = whole(third).astype(BF)
        part_a[0, third * 2 + 1 - core] = whole(13 + third).astype(BF)
    for block in range(2):
        part_a[0, 6 + block] = whole(9 + block).astype(BF)
        part_b[0, 10 + block] = whole(11 + block).astype(BF)
    mine = whole(8)[:, :128]
    theirs = whole(21)[:, :128]
    part_a[0, 8] = jnp.concatenate([mine, theirs, jnp.zeros_like(mine)], axis=1).astype(BF)
    for block in range(5):
        part_b[0, block * 2 + core] = whole(3 + block).astype(BF)
        part_b[0, block * 2 + 1 - core] = whole(16 + block).astype(BF)


def send_sums_kernel(info, a_kept, a_came, b_kept, b_came, kept, sent, rows):
    core = info[0]

    def spread(near, came, place, block):
        rows[...] = near[0, place].astype(F32) + came[0, place].astype(F32)
        pieces = [rows[6 * z : 6 * z + 6, :] for z in range(4)]
        for index in range(4):
            z = coordinate_at(info, "z", index)
            low = jnp.where(z % 2 == 0, pieces[0], pieces[1])
            high = jnp.where(z % 2 == 0, pieces[2], pieces[3])
            piece = jnp.where(z < 2, low, high).astype(BF)
            (kept if index < 2 else sent)[index % 2, block] = piece

    for side, first in ((core, 0), (1 - core, 13)):
        for third in range(3):
            spread(a_kept, a_came, third * 2 + side, first + third)
        for block in range(5):
            spread(b_kept, b_came, block * 2 + side, first + 3 + block)
    spread(a_kept, a_came, 8, 8)
    for block in range(2):
        spread(a_kept, a_came, 6 + block, 9 + block)
        spread(b_kept, b_came, 10 + block, 11 + block)


def shares_kernel(
    info, held, came, c_kept, c_came,
    qkv, out, ffn_in, ffn_bias, ffn_out, conv_in, conv_taps, conv_out, biases, gains, turned,
):
    width = out.shape[1]
    half, wide = width // 2, ffn_in.shape[1] // 2

    def put(target, first, apart, place):
        own_columns, other = held[0, place].astype(F32), came[0, place].astype(F32)
        target[:, first : first + LANES] = jnp.where(info[0] == 0, own_columns, other)
        target[:, first + apart : first + apart + LANES] = jnp.where(info[0] == 0, other, own_columns)

    for third in range(3):
        put(qkv, third * width, half, third)
    for block in range(4):
        put(ffn_in, block * LANES, wide, 3 + block)
    put(conv_in, 0, half, 7)
    for block in range(2):
        columns = slice(block * LANES, (block + 1) * LANES)
        out[:, columns] = held[0, 9 + block].astype(F32)
        conv_out[:, columns] = held[0, 11 + block].astype(F32)
        ffn_out[:, columns] = c_kept[0, block].astype(F32) + c_came[0, block].astype(F32)
    turned[...] = jnp.zeros_like(turned)
    turned[0:6, :] = held[0, 8].astype(F32)[:, :128]
    biases[...] = turned[0:6, 0:9]
    conv_taps[...] = turned[0:6, 12:27]
    small = jnp.transpose(turned[...])
    gains[...] = small[9:12, 0:6]
    for i in range(4):
        ffn_bias[0:1, 6 * i : 6 * i + 6] = small[27 + i : 28 + i, 0:6]


def erf_parts(operand):
    cumulative = 0.5 * (1.0 + lax.erf(operand * (0.5**0.5)))
    density = jnp.exp(-0.5 * operand * operand) * (0.5 / math.pi) ** 0.5
    return (cumulative, density)


def dot(left_side, right_side, left_dim=1, right_dim=0):
    return lax.dot_general(
        left_side, right_side, (((left_dim,), (right_dim,)), ((), ())), preferred_element_type=F32
    )


def normed(residual):
    centered = residual - jnp.mean(residual, axis=-1, keepdims=True)
    inverse = lax.rsqrt(jnp.mean(centered * centered, axis=-1, keepdims=True) + EPSILON)
    return (centered * inverse, inverse)


def normed_back(grad, norm, inverse, gain_row):
    scaled = grad * gain_row
    return inverse * (
        scaled
        - jnp.mean(scaled, axis=-1, keepdims=True)
        - norm * jnp.mean(scaled * norm, axis=-1, keepdims=True)
    )


def each(count, size, body):
    def step(index, unused):
        body(pl.ds(pl.multiple_of(index * size, size), size))
        return unused

    lax.fori_loop(0, count, step, 0)


def slots(position, ends, batch):
    number = jnp.zeros(position.shape, jnp.int32)
    for place in range(SLOTS):
        number = number + (position >= ends[4 + SLOTS * batch + place]).astype(jnp.int32)
    return number


def attention_kernel(
    flow, info, tokens, part_a, order, qkv_w, out_w, rows, taps, ffn_bias, qkv, attended, soft, part
):
    half = out_w.shape[0]
    per_batch = soft.shape[1]
    flow.arrive()
    for x in range(4):
        there = slice(96 * x, 96 * x + 96)
        for block in range(3):
            columns = slice(block * LANES, (block + 1) * LANES)
            qkv_w[there, columns] = tall_rows(info, part_a, "yx", block * 2, x).astype(BF)
            below = slice(half + 96 * x, half + 96 * x + 96)
            qkv_w[below, columns] = tall_rows(info, part_a, "yx", block * 2 + 1, x).astype(BF)
        for block in range(2):
            columns = slice(block * LANES, (block + 1) * LANES)
            out_w[there, columns] = tall_rows(info, part_a, "yx", 6 + block, x).astype(BF)
    flow.leave(0, 1)
    small = jnp.concatenate([tall_rows(info, part_a, "yx", 8, x) for x in range(4)], axis=0)
    mine = jnp.transpose(small[:, 0:128])
    theirs = jnp.transpose(small[:, 128:256])
    rows[...] = jnp.zeros_like(rows)
    left, right = jnp.where(info[0] == 0, mine, theirs), jnp.where(info[0] == 0, theirs, mine)
    rows[0:12, :half] = left[0:12, :]
    rows[0:12, half:] = right[0:12, :]
    rows[12:14, :half] = mine[0:2, :]
    rows[14:15, :half] = mine[6:7, :]
    taps[...] = jnp.zeros_like(taps)
    taps[0:15, :] = mine[12:27, :]
    spread = jnp.concatenate(
        [
            jnp.concatenate([mine[27 + i : 28 + i, 96 * x : 96 * x + 96] for i in range(4)], axis=1)
            for x in range(4)
        ]
        + [jnp.zeros((4, half), F32)],
        axis=0,
    )
    spread = dot(spread.astype(BF), order[...])
    for x in range(4):
        ffn_bias[0:1, x * LANES : (x + 1) * LANES] = spread[x : x + 1, :]
    for third in range(3):
        columns = slice(third * half, (third + 1) * half)
        block = dot(tokens[...], qkv_w[:, columns])
        if third != 1:
            block = block + rows[12 + third // 2 : 13 + third // 2, :half]
        qkv[:, columns] = block.astype(BF)
    square = (per_batch, per_batch)
    down = lax.broadcasted_iota(jnp.int32, square, 0)
    across = lax.broadcasted_iota(jnp.int32, square, 1)
    lane = lax.broadcasted_iota(jnp.int32, (per_batch, 128), 1)
    pairs = half // 128
    for batch in range(tokens.shape[0] // per_batch):
        there = slice(batch * per_batch, (batch + 1) * per_batch)
        slot_down, slot_across = slots(down, info, batch), slots(across, info, batch)
        allowed = (slot_down == slot_across) & ((slot_across < SLOTS - 1) | (down == across))
        forbidden = jnp.where(allowed, 0.0, -1e9)
        for pair in range(pairs):
            columns = slice(pair * 128, (pair + 1) * 128)
            query = qkv[there, columns]
            key = qkv[there, half + pair * 128 : half + (pair + 1) * 128]
            value = qkv[there, 2 * half + pair * 128 : 2 * half + (pair + 1) * 128]
            result = jnp.zeros((per_batch, 128), F32)
            for side in range(2):
                mine = (lane >= HEAD_DIM) if side else (lane < HEAD_DIM)
                scores = dot(jnp.where(mine, query, jnp.zeros_like(query)), key, 1, 1)
                scores = scores * HEAD_DIM ** (-0.5) + forbidden
                exponent = jnp.exp(scores - jnp.max(scores, axis=-1, keepdims=True))
                weight = (exponent * (1.0 / jnp.sum(exponent, axis=-1, keepdims=True))).astype(BF)
                soft[(batch * pairs + pair) * 2 + side] = weight
                result = result + dot(weight, jnp.where(mine, value, jnp.zeros_like(value)))
            attended[there, columns] = result.astype(BF)
    flow.leave(5, 6, 7)
    part[...] = dot(attended[...], out_w[...]).astype(BF)


def feed_kernel(
    flow, info, tokens, mine, theirs, rows, part_b, part_c, ffn_bias,
    ffn_in, ffn_out, conv_in, conv_out, hidden, norm, inverse, activated, slope, part,
):
    half = conv_in.shape[1]

    def first(there):
        residual = (
            tokens[there, :].astype(F32)
            + (mine[there, :].astype(F32) + theirs[there, :].astype(F32))
            + rows[2:3, :]
        )
        unit, scale = normed(residual)
        norm[there, :] = unit
        inverse[there, :] = jnp.broadcast_to(scale, (scale.shape[0], 128))
        hidden[there, :] = (unit * rows[9:10, :] + rows[3:4, :]).astype(BF)

    each(tokens.shape[0] // 64, 64, first)
    flow.leave(5, 6)
    flow.arrive(5)
    for x in range(4):
        for side in range(2):
            there = slice(half * side + 96 * x, half * side + 96 * x + 96)
            for block in range(4):
                columns = slice(block * LANES, (block + 1) * LANES)
                ffn_in[there, columns] = tall_rows(info, part_b, "xy", block * 2 + side, x).astype(BF)
            conv_in[there, :] = tall_rows(info, part_b, "xy", 8 + side, x).astype(BF)
        for block in range(2):
            columns = slice(block * LANES, (block + 1) * LANES)
            conv_out[96 * x : 96 * x + 96, columns] = tall_rows(info, part_b, "xy", 10 + block, x).astype(BF)
    flow.leave(0)
    wide = ffn_in.shape[1]
    chunk = 256

    def second(index, unused):
        columns = pl.ds(pl.multiple_of(index * chunk, chunk), chunk)
        up = dot(hidden[...], ffn_in[:, columns]) + ffn_bias[0:1, columns]
        cumulative, density = erf_parts(up)
        activated[:, columns] = (up * cumulative).astype(BF)
        slope[:, columns] = (cumulative + up * density).astype(BF)
        return unused

    lax.fori_loop(0, wide // chunk, second, 0)
    flow.leave(7, 8)
    flow.arrive(6)
    for x in range(4):
        for y in range(4):
            for block in range(2):
                pieces = []
                for z in range(4):
                    indices = {
                        axis: index_at(info, axis, coordinate)
                        for axis, coordinate in zip(AXES, (x, y, z))
                    }
                    pieces.append(part_c[outer_inner("zyx", indices), block].astype(F32))
                row = 384 * x + 96 * y
                ffn_out[row : row + 96, block * LANES : (block + 1) * LANES] = jnp.concatenate(
                    pieces, axis=0
                ).astype(BF)
    flow.leave(1)
    part[...] = dot(activated[...], ffn_out[...]).astype(BF)


def tap_row(taps, info, batch, offset):
    choice = info[1 + batch]
    row = taps[11 + offset : 12 + offset, :]
    row = jnp.where(choice == 1, taps[5 + offset : 6 + offset, :] if abs(offset) < 3 else 0.0, row)
    return jnp.where(choice == 0, taps[1 + offset : 2 + offset, :] if abs(offset) < 2 else 0.0, row)


def fill_slots(info, padded, per_batch, batches):
    position = lax.broadcasted_iota(jnp.int32, (per_batch, 128), 0)
    outside = jnp.full((8, 128), -1, jnp.int32)
    for batch in range(batches):
        padded[batch, 0:8, :] = outside
        padded[batch, 8 : 8 + per_batch, :] = slots(position, info, batch)
        padded[batch, 8 + per_batch :, :] = outside


def clear_edges(padded, per_batch, batches):
    edge = jnp.zeros((8, padded.shape[2]), F32)
    for batch in range(batches):
        padded[batch, 0:8, :] = edge
        padded[batch, 8 + per_batch :, :] = edge


def convolution_kernel(
    flow, info, hidden, mine, theirs, rows, conv_in, taps, conv_out,
    phase_one, norm, inverse, mixed, gated, slope, part, slot_pad, mixed_pad,
):
    batches = slot_pad.shape[0]
    per_batch = hidden.shape[0] // batches
    half = conv_in.shape[1]

    def first(there):
        residual = (
            hidden[there, :].astype(F32)
            + (mine[there, :].astype(F32) + theirs[there, :].astype(F32))
            + rows[4:5, :]
        )
        unit, scale = normed(residual)
        norm[there, :] = unit
        inverse[there, :] = jnp.broadcast_to(scale, (scale.shape[0], 128))
        phase_one[there, :] = (unit * rows[10:11, :] + rows[5:6, :]).astype(BF)

    each(hidden.shape[0] // 64, 64, first)
    flow.leave(1, 2)
    fill_slots(info, slot_pad, per_batch, batches)
    clear_edges(mixed_pad, per_batch, batches)
    mixed[...] = dot(phase_one[...], conv_in[...]) + rows[14:15, :half]
    for batch in range(batches):
        there = slice(batch * per_batch, (batch + 1) * per_batch)
        mixed_pad[batch, 8 : 8 + per_batch, :] = mixed[there, :]
        for column in range(half // 128):
            columns = slice(column * 128, (column + 1) * 128)
            here = slot_pad[batch, 8 : 8 + per_batch, :]
            total = jnp.zeros((per_batch, 128), F32)
            for offset in range(-3, 4):
                same = slot_pad[batch, 8 + offset : 8 + offset + per_batch, :] == here
                moved = mixed_pad[batch, 8 + offset : 8 + offset + per_batch, columns]
                tap = tap_row(taps, info, batch, offset)[:, columns]
                total = total + jnp.where(same, moved, 0.0) * tap
            cumulative, density = erf_parts(total)
            gated[there, columns] = (total * cumulative).astype(BF)
            slope[there, columns] = cumulative + total * density
    part[...] = dot(gated[...], conv_out[...]).astype(BF)


def own(info, row):
    half = row.shape[1] // 2
    return jnp.where(info[0] == 0, row[:, :half], row[:, half:])


def convolution_back_kernel(
    flow, info, phase_one, mine, theirs, cotangent, rows, conv_in, taps, conv_out, mixed, gated, slope,
    result, grad_three, kept, sent, part, sums, d_taps,
    slot_pad, mixed_pad, grad_pad, grad_low, grad_mixed, wide_sums, whole,
):
    batches = slot_pad.shape[0]
    per_batch = phase_one.shape[0] // batches
    half = conv_in.shape[1]
    fill_slots(info, slot_pad, per_batch, batches)
    clear_edges(mixed_pad, per_batch, batches)
    clear_edges(grad_pad, per_batch, batches)
    wide_sums[...] = jnp.zeros_like(wide_sums)
    flow.arrive()
    size = 64
    for batch in range(batches):

        def first(index, unused):
            inner = pl.multiple_of(index * size, size)
            there = pl.ds(pl.multiple_of(batch * per_batch + inner, size), size)
            residual = (
                phase_one[there, :].astype(F32)
                + (mine[there, :].astype(F32) + theirs[there, :].astype(F32))
                + rows[7:8, :]
            )
            unit, scale = normed(residual)
            ended = (unit * rows[11:12, :] + rows[8:9, :]).astype(BF)
            result[there, :] = jnp.where(info[0] == 0, phase_one[there, :], ended)
            valid = slot_pad[batch, pl.ds(pl.multiple_of(8 + inner, 8), size), :][:, :1] < SLOTS - 1
            masked = jnp.where(valid, cotangent[there, :].astype(F32), 0.0)
            grad = normed_back(masked, unit, scale, rows[11:12, :])
            grad_three[there, :] = grad
            low = grad.astype(BF)
            grad_low[there, :] = low
            wide_sums[0:1, :] += jnp.sum(low.astype(F32), axis=0, keepdims=True)
            wide_sums[1:2, :] += jnp.sum(masked, axis=0, keepdims=True)
            wide_sums[2:3, :] += jnp.sum(masked * unit, axis=0, keepdims=True)
            return unused

        lax.fori_loop(0, per_batch // size, first, 0)
    flow.leave(0)
    for block in range(2):
        columns = slice(block * LANES, (block + 1) * LANES)
        whole[0:half, :] = dot(gated[...], grad_low[:, columns], 0, 0)
        pack_rows(info, whole, "xy", 2 + block, kept, sent, 0)
    tap_sums = [[[] for offset in range(7)] for batch in range(batches)]
    for batch in range(batches):
        there = slice(batch * per_batch, (batch + 1) * per_batch)
        grad_pad[batch, 8 : 8 + per_batch, :] = (
            dot(grad_low[there, :], conv_out[...], 1, 1) * slope[there, :]
        )
        mixed_pad[batch, 8 : 8 + per_batch, :] = mixed[there, :]
        for column in range(half // 128):
            columns = slice(column * 128, (column + 1) * 128)
            here = slot_pad[batch, 8 : 8 + per_batch, :]
            grad = grad_pad[batch, 8 : 8 + per_batch, columns]
            total = jnp.zeros((per_batch, 128), F32)
            for offset in range(-3, 4):
                away = slice(8 + offset, 8 + offset + per_batch)
                same = slot_pad[batch, away, :] == here
                tap = tap_row(taps, info, batch, -offset)[:, columns]
                total = total + jnp.where(same, grad_pad[batch, away, columns], 0.0) * tap
                term = jnp.where(same, mixed_pad[batch, away, columns], 0.0) * grad
                tap_sums[batch][offset + 3].append(jnp.sum(term, axis=0, keepdims=True))
            grad_mixed[there, columns] = total.astype(BF)
    for choice in range(3):
        for offset in range(-choice - 1, choice + 2):
            row = choice * choice + 2 * choice + offset + choice + 1
            total = jnp.zeros((1, half), F32)
            for batch in range(batches):
                joined = jnp.concatenate(tap_sums[batch][offset + 3], axis=1)
                total = total + jnp.where(info[1 + batch] == choice, joined, 0.0)
            d_taps[row : row + 1, :] = total
    d_taps[15:16, :] = jnp.zeros((1, half), F32)
    whole[...] = dot(phase_one[...], grad_mixed[...], 0, 0)
    for side in range(2):
        pack_rows(info, whole, "xy", side, kept, sent, side * half)
    part[...] = dot(grad_mixed[...], conv_in[...], 1, 1).astype(BF)
    sums[0:1, :] = jnp.sum(grad_mixed[...].astype(F32), axis=0, keepdims=True)
    for place in range(3):
        sums[place + 1 : place + 2, :] = own(info, wide_sums[place : place + 1, :])
    sums[4:8, :] = jnp.zeros((4, half), F32)


def feed_back_kernel(
    flow, info, grad_three, mine, theirs, norm, inverse, rows, activated, slope, hidden, ffn_in, ffn_out,
    conv_kept, conv_sent,
    grad_phase_one, grad_two, b_kept, b_sent, c_kept, c_sent, part, sums, bias_sums,
    grad_low, grad_up, wide_sums, whole,
):
    wide_sums[...] = jnp.zeros_like(wide_sums)
    flow.arrive(4, 5)

    def first(there):
        arriving = grad_three[there, :] + (mine[there, :].astype(F32) + theirs[there, :].astype(F32))
        arriving = arriving.astype(BF)
        grad_phase_one[there, :] = arriving
        arriving = arriving.astype(F32)
        unit = norm[there, :]
        grad = normed_back(arriving, unit, inverse[there, :1], rows[10:11, :])
        grad_two[there, :] = grad
        low = grad.astype(BF)
        grad_low[there, :] = low
        wide_sums[0:1, :] += jnp.sum(low.astype(F32), axis=0, keepdims=True)
        wide_sums[1:2, :] += jnp.sum(arriving, axis=0, keepdims=True)
        wide_sums[2:3, :] += jnp.sum(arriving * unit, axis=0, keepdims=True)

    each(hidden.shape[0] // 64, 64, first)
    flow.leave(0)
    flow.arrive(7, 8, 10, 11)
    half = ffn_in.shape[0] // 2
    for block in range(ffn_in.shape[1] // LANES):
        columns = slice(block * LANES, (block + 1) * LANES)
        grad = dot(grad_low[...], ffn_out[columns, :], 1, 1) * slope[:, columns].astype(F32)
        low = grad.astype(BF)
        grad_up[:, columns] = low
        bias_sums[0:1, columns] = jnp.sum(low.astype(F32), axis=0, keepdims=True)
        whole[...] = dot(hidden[...], low, 0, 0)
        for side in range(2):
            pack_rows(info, whole, "xy", block * 2 + side, b_kept, b_sent, side * half)
    for place in range(8):
        for block in range(4):
            b_kept[place, 8 + block] = conv_kept[place, block]
            b_sent[place, 8 + block] = conv_sent[place, block]
    for step in range(4):
        x = coordinate_at(info, "x", step)
        there = pl.ds(pl.multiple_of(x * 384, 128), 384)
        for block in range(2):
            columns = slice(block * LANES, (block + 1) * LANES)
            whole[0:384, :] = dot(activated[:, there], grad_low[:, columns], 0, 0)
            for outer in range(4):
                for inner in range(4):
                    z, y = coordinate_at(info, "z", outer), coordinate_at(info, "y", inner)
                    piece = whole[pl.ds(pl.multiple_of(96 * y + 24 * z, 8), 24), :].astype(BF)
                    place = ((outer % 2) * 4 + inner) * 4 + step
                    (c_kept if outer < 2 else c_sent)[place, block] = piece
    part[...] = dot(grad_up[...], ffn_in[...], 1, 1).astype(BF)
    for place in range(3):
        sums[place : place + 1, :] = own(info, wide_sums[place : place + 1, :])
    sums[3:8, :] = jnp.zeros((5, sums.shape[1]), F32)


def attention_back_kernel(
    flow, info, grad_two, mine, theirs, norm, inverse, rows, tokens, qkv, attended, soft, qkv_w, out_w,
    sums_two, sums_three, d_taps, bias_sums, order,
    grad_one, kept, sent, part, grad_low, grad_attended, grad_qkv, wide_sums, whole, sums,
):
    flow.arrive(4, 5)
    half = out_w.shape[0]
    per_batch = soft.shape[1]
    wide_sums[...] = jnp.zeros_like(wide_sums)

    def first(there):
        arriving = grad_two[there, :] + (mine[there, :].astype(F32) + theirs[there, :].astype(F32))
        unit = norm[there, :]
        grad = normed_back(arriving, unit, inverse[there, :1], rows[9:10, :])
        grad_one[there, :] = grad
        low = grad.astype(BF)
        grad_low[there, :] = low
        wide_sums[0:1, :] += jnp.sum(low.astype(F32), axis=0, keepdims=True)
        wide_sums[1:2, :] += jnp.sum(arriving, axis=0, keepdims=True)
        wide_sums[2:3, :] += jnp.sum(arriving * unit, axis=0, keepdims=True)

    each(tokens.shape[0] // 64, 64, first)
    flow.leave(0)
    flow.arrive(7, 8, 9, 10, 11, 12)
    for block in range(2):
        columns = slice(block * LANES, (block + 1) * LANES)
        whole[0:half, :] = dot(attended[...], grad_low[:, columns], 0, 0)
        pack_rows(info, whole, "yx", 6 + block, kept, sent, 0)
    grad_attended[...] = dot(grad_low[...], out_w[...], 1, 1).astype(BF)
    lane = lax.broadcasted_iota(jnp.int32, (per_batch, 128), 1)
    pairs = half // 128
    scale = HEAD_DIM ** (-0.5)
    for batch in range(tokens.shape[0] // per_batch):
        there = slice(batch * per_batch, (batch + 1) * per_batch)
        for pair in range(pairs):
            columns = [
                slice(third * half + pair * 128, third * half + (pair + 1) * 128) for third in range(3)
            ]
            query, key, value = (qkv[there, columns[third]] for third in range(3))
            grad = grad_attended[there, columns[0]]
            totals = [jnp.zeros((per_batch, 128), F32) for third in range(3)]
            for side in range(2):
                mine_lanes = (lane >= HEAD_DIM) if side else (lane < HEAD_DIM)

                def only(operand):
                    return jnp.where(mine_lanes, operand, jnp.zeros_like(operand))

                weight = soft[(batch * pairs + pair) * 2 + side]
                grad_side = only(grad)
                grad_soft = dot(grad_side, value, 1, 1)
                weight_wide = weight.astype(F32)
                inner = jnp.sum(grad_soft * weight_wide, axis=-1, keepdims=True)
                grad_scores = (weight_wide * (grad_soft - inner)).astype(BF)
                totals[0] = totals[0] + dot(grad_scores, only(key))
                totals[1] = totals[1] + dot(grad_scores, only(query), 0, 0)
                totals[2] = totals[2] + dot(weight, grad_side, 0, 0)
            grad_qkv[there, columns[0]] = (totals[0] * scale).astype(BF)
            grad_qkv[there, columns[1]] = (totals[1] * scale).astype(BF)
            grad_qkv[there, columns[2]] = totals[2].astype(BF)
    part[...] = dot(grad_qkv[...], qkv_w[...], 1, 1).astype(BF)
    sums[...] = jnp.zeros_like(sums)
    for third in range(3):
        columns = slice(third * half, (third + 1) * half)
        whole[...] = dot(tokens[...], grad_qkv[:, columns], 0, 0)
        for side in range(2):
            pack_rows(info, whole, "yx", third * 2 + side, kept, sent, side * half)
        if third != 1:
            place = third // 2
            sums[place : place + 1, :] = jnp.sum(
                grad_qkv[:, columns].astype(F32), axis=0, keepdims=True
            )
    sums[2:3, :] = own(info, wide_sums[0:1, :])
    sums[3:4, :] = own(info, wide_sums[1:2, :])
    sums[4:6, :] = sums_two[0:2, :]
    sums[6:9, :] = sums_three[0:3, :]
    sums[9:10, :] = own(info, wide_sums[2:3, :])
    sums[10:11, :] = sums_two[2:3, :]
    sums[11:12, :] = sums_three[3:4, :]
    sums[12:27, :] = d_taps[0:15, :]
    spread = jnp.concatenate(
        [bias_sums[0:1, x * LANES : (x + 1) * LANES] for x in range(4)] + [jnp.zeros((4, half), F32)], axis=0
    )
    spread = dot(spread.astype(BF), order[...], 1, 1)
    for i in range(4):
        sums[27 + i : 28 + i, :] = jnp.concatenate(
            [spread[x : x + 1, 96 * i : 96 * i + 96] for x in range(4)], axis=1
        )
    whole[0:half, :] = jnp.zeros((half, LANES), F32)
    whole[0:half, 0:128] = jnp.transpose(sums[...])
    pack_rows(info, whole, "yx", 8, kept, sent, 0)


class Flow:
    def __init__(self):
        self.coming, self.going = {}, {}

    def arrive(self, *chosen):
        for which in chosen or tuple(self.coming):
            for copy in self.coming[which]:
                copy.wait()

    def leave(self, *chosen):
        for which in chosen:
            self.going[which].start()


def kernel_call(body, outputs, scratch, has_info, *operands, late=(), early=(), mib=4, gflop=0):
    vmem = pl.BlockSpec(memory_space=pltpu.VMEM)
    smem = pl.BlockSpec(memory_space=pltpu.SMEM)
    hbm = pl.BlockSpec(memory_space=pltpu.HBM)
    groups = [operand if isinstance(operand, tuple) else (operand,) for operand in operands]
    arrays = [array for group in groups for array in group]
    moves = sum(len(groups[which]) for which in late) + len(early)

    def with_copies(*refs):
        taken = 0
        operand_refs = []
        for group in groups:
            operand_refs.append(refs[taken : taken + len(group)])
            taken += len(group)
        output_refs = list(refs[taken : taken + len(outputs)])
        own = refs[taken + len(outputs) : taken + len(outputs) + len(scratch)]
        buffers = list(refs[taken + len(outputs) + len(scratch) : -1])
        flags, used = refs[-1], 0
        flow = Flow()
        for which in late:
            buffer = buffers.pop(0)
            first, flow.coming[which] = 0, []
            for source in operand_refs[which]:
                count = source.shape[0]
                target = buffer if len(groups[which]) == 1 else buffer.at[pl.ds(first, count)]
                copy = pltpu.make_async_copy(source, target, flags.at[used])
                copy.start()
                flow.coming[which].append(copy)
                first, used = first + count, used + 1
            operand_refs[which] = (buffer,)
        for which in early:
            buffer = buffers.pop(0)
            flow.going[which] = pltpu.make_async_copy(buffer, output_refs[which], flags.at[used])
            output_refs[which] = buffer
            used += 1
        body(flow, *(group[0] for group in operand_refs), *output_refs, *own)
        for which in early:
            flow.going[which].wait()

    specs = [smem if has_info and place == 0 else vmem for place in range(len(operands))]
    out_specs = [vmem] * len(outputs)
    memory = [pltpu.VMEM(shape, dtype) for shape, dtype in scratch]
    for which in late:
        specs[which] = hbm
        whole = sum(array.shape[0] for array in groups[which])
        memory.append(pltpu.VMEM((whole, *groups[which][0].shape[1:]), groups[which][0].dtype))
    for which in early:
        out_specs[which] = hbm
        memory.append(pltpu.VMEM(*outputs[which]))
    if moves:
        memory.append(pltpu.SemaphoreType.DMA((moves,)))
    return pl.pallas_call(
        with_copies if moves else body,
        out_shape=[jax.ShapeDtypeStruct(shape, dtype) for shape, dtype in outputs],
        in_specs=[spec for spec, group in zip(specs, groups) for array in group],
        out_specs=out_specs,
        scratch_shapes=memory,
        compiler_params=pltpu.CompilerParams(vmem_limit_bytes=mib * 1024 * 1024),
        cost_estimate=pl.CostEstimate(flops=int(gflop * 1e9), bytes_accessed=1 << 20, transcendentals=0),
    )(*arrays)


def gather_weights(info, masters):
    (qkv, out, ffn_in, ffn_bias, ffn_out, conv_in, conv_taps, conv_out, biases, gains) = masters
    mine, theirs, part_c = kernel_call(
        send_weights_kernel,
        [((1, 13, 6, LANES), BF), ((1, 9, 6, LANES), BF), ((1, 2, ffn_out.shape[0], LANES), BF)],
        [((128, 128), F32)],
        True,
        lax.axis_index("phase").astype(jnp.int32).reshape(1), qkv, out, ffn_in, ffn_bias.reshape(1, -1), ffn_out, conv_in, conv_taps.T, conv_out, biases.T,
        gains,
        late=tuple(range(1, 11)),
        mib=60,
    )

    def together(*values):
        return lax.optimization_barrier(values)

    theirs, part_c = together(swap(theirs), grown(part_c, "x", 0))
    line = jnp.concatenate([mine, theirs], axis=1)
    line, part_c = together(grown(line, "z", 0), grown(part_c, "x", 1))
    line_came, part_c = together(lax.ppermute(line, BOTH, partners("z", 1)), grown(part_c, "y", 0))
    part_a, part_b = kernel_call(
        line_weights_kernel,
        [((1, 9, 24, LANES), BF), ((1, 12, 24, LANES), BF)],
        [((24, LANES), F32)],
        True,
        info, line, line_came,
    )
    part_a, part_b, part_c = together(grown(part_a, "x", 0), grown(part_b, "y", 0), grown(part_c, "y", 1))
    part_c = grown(part_c, "z", 0)
    part_a, part_b = together(grown(part_a, "x", 1), grown(part_b, "y", 1))
    part_a, part_b, part_c = together(grown(part_a, "y", 0), grown(part_b, "x", 0), part_c)
    return (
        (part_a, lax.ppermute(part_a, BOTH, partners("y", 1))),
        (part_b, lax.ppermute(part_b, BOTH, partners("x", 1))),
        (part_c, lax.ppermute(part_c, BOTH, partners("z", 1))),
    )


def shards(
    tokens,
    cotangent,
    lengths,
    kernel_choice,
    *masters,
):
    batches = lengths.shape[0]
    rows, width = tokens.shape
    per_batch = rows // batches
    half = width // 2
    wide = masters[2].shape[1] // 2
    heads = half // HEAD_DIM
    info = info_of(lengths, kernel_choice)
    part_a, part_b, part_c = gather_weights(info, masters)
    order = bias_order()
    low, full = ((rows, width), BF), ((rows, width), F32)
    narrow = ((rows, 128), F32)
    slot_pad = ((batches, per_batch + 16, 128), jnp.int32)
    row_pad = ((batches, per_batch + 16, half), F32)
    whole = ((width, LANES), F32)

    def halves(blocks):
        return [((8, blocks, 24, LANES), BF)] * 2

    qkv_w, out_w, all_rows, taps, ffn_bias, qkv, attended, soft, part = kernel_call(
        attention_kernel,
        [
            ((width, 3 * half), BF), ((half, width), BF), ((16, width), F32),
            ((16, half), F32), ((1, wide), F32), ((rows, 3 * half), BF), ((rows, half), BF),
            ((batches * heads, per_batch, per_batch), BF), low,
        ],
        [],
        True,
        info, tokens, part_a, order,
        late=(2,),
        early=(0, 1, 5, 6, 7),
        gflop=5,
        mib=16,
    )
    ffn_in, ffn_out, conv_in, conv_out, hidden, norm_one, inverse_one, activated, slope_up, part_two = kernel_call(
        feed_kernel,
        [
            ((width, wide), BF), ((wide, width), BF), ((width, half), BF), ((half, width), BF), low, full, narrow, ((rows, wide), BF), ((rows, wide), BF), low,
        ],
        [],
        True,
        info, tokens, part, swap(part), all_rows, part_b, part_c, ffn_bias,
        late=(5, 6),
        early=(0, 1, 5, 6, 7, 8),
        gflop=8,
        mib=24,
    )
    phase_one, norm_two, inverse_two, mixed, gated, slope, part_three = kernel_call(
        convolution_kernel,
        [low, full, narrow, ((rows, half), F32), ((rows, half), BF), ((rows, half), F32), low],
        [slot_pad, row_pad],
        True,
        info, hidden, part_two, swap(part_two), all_rows, conv_in, taps, conv_out,
        early=(1, 2),
        gflop=4,
        mib=8,
    )
    block_outputs, grad_three, conv_kept, conv_sent, part, sums_three, d_taps = kernel_call(
        convolution_back_kernel,
        [low, full, *halves(4), low, ((8, half), F32), ((16, half), F32)],
        [slot_pad, row_pad, row_pad, low, ((rows, half), BF), ((8, width), F32), whole],
        True,
        info, phase_one, part_three, swap(part_three), cotangent, all_rows, conv_in, taps, conv_out,
        mixed, gated, slope,
        late=(4,),
        early=(0,),
        gflop=8,
        mib=10,
    )
    grad_phase_one, grad_two, b_kept, b_sent, c_kept, c_sent, part, sums_two, d_ffn_bias = kernel_call(
        feed_back_kernel,
        [
            low, full, *halves(12), ((32, 2, 24, LANES), BF), ((32, 2, 24, LANES), BF), low,
            ((8, half), F32), ((1, wide), F32),
        ],
        [low, ((rows, wide), BF), ((8, width), F32), whole],
        True,
        info, grad_three, part, swap(part), norm_two, inverse_two, all_rows, activated, slope_up, hidden,
        ffn_in, ffn_out, conv_kept, conv_sent,
        late=(4, 5, 7, 8, 10, 11),
        early=(0,),
        gflop=10,
        mib=20,
    )
    grad_one, a_kept, a_sent, part = kernel_call(
        attention_back_kernel,
        [full, *halves(9), low],
        [low, ((rows, half), BF), ((rows, 3 * half), BF), ((8, width), F32), whole, ((128, half), F32)],
        True,
        info, grad_two, part, swap(part), norm_one, inverse_one, all_rows, tokens, qkv, attended, soft,
        qkv_w, out_w, sums_two, sums_three, d_taps, d_ffn_bias, order,
        late=(4, 5, 7, 8, 9, 10, 11, 12),
        early=(0,),
        gflop=10,
        mib=20,
    )
    for axis in "zy":
        for step in (1, 0):
            c_kept, c_sent = shrunk(c_kept, c_sent, axis, step)
    c_kept, c_sent = shrunk(c_kept, c_sent, "x", 1)
    for step in (1, 0):
        b_kept, b_sent = shrunk(b_kept, b_sent, "x", step)
    b_kept, b_sent = shrunk(b_kept, b_sent, "y", 1)
    a_kept, a_sent = shrunk(a_kept, a_sent, "y", 1)
    a_kept, a_sent, grad_one, part, theirs = lax.optimization_barrier(
        (a_kept, a_sent, grad_one, part, swap(part))
    )
    grad_tokens = (grad_one + (part.astype(F32) + theirs.astype(F32))).astype(BF)
    input_grads = jnp.where(lax.axis_index("phase") == 0, grad_tokens, grad_phase_one)
    a_kept, a_sent = shrunk(a_kept, a_sent, "y", 0)
    a_kept, a_sent = shrunk(a_kept, a_sent, "x", 1)
    kept, sent = kernel_call(
        send_sums_kernel,
        [((2, 21, 6, LANES), BF)] * 2,
        [((24, LANES), F32)],
        True,
        info,
        a_kept, lax.ppermute(a_sent, BOTH, partners("x", 0)),
        b_kept, lax.ppermute(b_sent, BOTH, partners("y", 0)),
    )
    kept, sent = shrunk(kept, sent, "z", 1)
    came = lax.ppermute(sent, BOTH, partners("z", 0))
    held, other = (
        (kept[:, there].astype(F32) + came[:, there].astype(F32)).astype(BF)
        for there in (slice(0, 13), slice(13, 21))
    )
    shapes = [master.shape for master in masters]
    shapes[3] = (1, shapes[3][0])
    for turned in (6, 8):
        shapes[turned] = shapes[turned][::-1]
    shares = list(
        kernel_call(
            shares_kernel,
            [(shape, F32) for shape in shapes],
            [((128, 128), F32)],
            True,
            info, held, swap(other), c_kept, lax.ppermute(c_sent, BOTH, partners("x", 0)),
        )
    )
    shares[3] = shares[3].reshape(-1)
    for turned in (6, 8):
        shares[turned] = shares[turned].T
    return (block_outputs[None], input_grads[None], *shares)


def solution(mesh):
    sharded, columns = P(BOTH, None), P(None, BOTH)
    weights = (sharded, sharded, sharded, P(BOTH), sharded, sharded, columns, sharded, columns, columns)
    return jax.shard_map(
        shards,
        mesh=mesh,
        in_specs=(P("dp", None), P("dp", None), P("dp", None), P("dp"), *weights),
        out_specs=(P("phase", "dp", None), P("phase", "dp", None), *weights),
        check_vma=False,
    )
```

```python
import math

import jax
import jax.numpy as jnp
import numpy as np
from jax import lax
from jax.experimental import pallas as pl
from jax.experimental.pallas import tpu as pltpu
from jax.sharding import PartitionSpec as P

HEAD_DIM = 64
EPSILON = 1e-05
BOTH = ("phase", "dp")
STRIDE = {"x": 16, "y": 4, "z": 1}
AXES = "xyz"
LANES = 384
SLOTS = 6
SWAP = [(0, 1), (1, 0)]
BF = jnp.bfloat16
F32 = jnp.float32


def partners(axis, step):
    pairs = []
    for core in range(2):
        mask = (1, 3)[(core + step) % 2]
        for chip in range(64):
            coordinate = (chip // STRIDE[axis]) % 4
            target = chip + ((coordinate ^ mask) - coordinate) * STRIDE[axis]
            pairs.append((core * 64 + chip, core * 64 + target))
    return pairs


def across(mask):
    return [(device, device + (((device % 4) ^ mask) - device % 4)) for device in range(128)]


def grown(held, axis, step):
    return jnp.concatenate([held, lax.ppermute(held, BOTH, partners(axis, step))])


def shrunk(kept, sent, axis, step):
    came = lax.ppermute(sent, BOTH, partners(axis, step))
    count = kept.shape[0] // 2
    return tuple(
        (kept[there].astype(F32) + came[there].astype(F32)).astype(BF)
        for there in (slice(0, count), slice(count, 2 * count))
    )


def after(value, *others):
    return lax.optimization_barrier((value, *others))[0]


def swap(part):
    return lax.ppermute(part, "phase", SWAP)


def bias_order():
    table = np.zeros((LANES, LANES), np.float32)
    for i in range(4):
        for d in range(16):
            for j in range(6):
                table[96 * i + 6 * d + j, 24 * d + 6 * i + j] = 1.0
    return jnp.asarray(table, BF)


def info_of(lengths, kernel_choice):
    core = lax.axis_index("phase").astype(jnp.int32)
    chip = lax.axis_index("dp").astype(jnp.int32)
    return jnp.concatenate(
        [
            core[None],
            kernel_choice,
            jnp.zeros((3 - kernel_choice.shape[0],), jnp.int32),
            jnp.cumsum(lengths, axis=-1).reshape(-1),
            jnp.stack([(chip // STRIDE[axis]) % 4 for axis in AXES]),
            jnp.stack([1 + 2 * core, 3 - 2 * core]),
        ]
    )


def coordinate_at(info, axis, index):
    here = info[16 + AXES.index(axis)]
    return here ^ (0, info[19], info[20], 2)[index]


def index_at(info, axis, coordinate):
    apart = info[16 + AXES.index(axis)] ^ coordinate
    return jnp.where(
        apart == 0, 0, jnp.where(apart == info[19], 1, jnp.where(apart == info[20], 2, 3))
    )


def outer_inner(order, indices):
    place = 0
    for axis in order:
        place = place * 4 + indices[axis]
    return place


def tall_rows(info, part, order, block, x):
    pieces = []
    for y in range(4):
        place = outer_inner(order, {"x": index_at(info, "x", x), "y": index_at(info, "y", y)})
        pieces.append(part[place, block].astype(F32))
    return jnp.concatenate(pieces, axis=0)


def pack_rows(info, source, order, block, kept, sent, first_row):
    for outer in range(4):
        for inner in range(4):
            place = {order[0]: coordinate_at(info, order[0], outer)}
            place[order[1]] = coordinate_at(info, order[1], inner)
            row = pl.multiple_of(first_row + 96 * place["x"] + 24 * place["y"], 8)
            piece = source[pl.ds(row, 24), :].astype(BF)
            (kept if outer < 2 else sent)[(outer % 2) * 4 + inner, block] = piece


def send_weights_kernel(
    flow, core, qkv, out, ffn_in, ffn_bias, ffn_out, conv_in, conv_taps, conv_out, biases, gains,
    mine, theirs, turned,
):
    width = out.shape[1]
    half, wide = width // 2, ffn_in.shape[1] // 2
    turned[...] = jnp.zeros_like(turned)
    flow.arrive()
    turned[9:12, 0:6] = gains[...]
    for i in range(4):
        turned[27 + i : 28 + i, 0:6] = ffn_bias[0:1, 6 * i : 6 * i + 6]
    turned[0:8, :] = jnp.transpose(turned[...])[0:8, :]
    turned[0:6, 0:9] = biases[...]
    turned[0:6, 12:27] = conv_taps[...]
    small = turned[0:6, :]
    blank = jnp.zeros((6, LANES - 128), F32)
    small = jnp.concatenate([small, blank], axis=1).astype(BF)

    def pair(source, first, apart):
        return (source[:, first : first + LANES], source[:, first + apart : first + apart + LANES])

    places = [pair(qkv, third * width, half) for third in range(3)]
    places += [pair(ffn_in, block * LANES, wide) for block in range(4)]
    places.append(pair(conv_in, 0, half))
    for place, (low, high) in enumerate(places):
        mine[place] = jnp.where(core[0] == 0, low, high).astype(BF)
        theirs[place] = jnp.where(core[0] == 0, high, low).astype(BF)
    mine[8] = small
    theirs[8] = small
    for block in range(2):
        columns = slice(block * LANES, (block + 1) * LANES)
        mine[9 + block] = out[:, columns].astype(BF)
        mine[11 + block] = conv_out[:, columns].astype(BF)
        for part in range(4):
            mine[13 + block * 4 + part] = ffn_out[6 * part : 6 * part + 6, columns].astype(BF)


def line_weights_kernel(info, own_rows, first, second, third, part_a, part_b, rows):
    core = info[0]

    def piece(z, place):
        apart = info[18] ^ z
        near = jnp.where(apart == 0, own_rows[place].astype(F32), first[place].astype(F32))
        far = jnp.where(apart == 2, second[place].astype(F32), third[place].astype(F32))
        return jnp.where(apart < 2, near, far)

    def whole(place):
        for z in range(4):
            rows[6 * z : 6 * z + 6, :] = piece(z, place)
        return rows[...]

    for block in range(3):
        part_a[0, block * 2 + core] = whole(block).astype(BF)
        part_a[0, block * 2 + 1 - core] = whole(21 + block).astype(BF)
    for block in range(2):
        part_a[0, 6 + block] = whole(9 + block).astype(BF)
        part_a[0, 11 + block] = whole(11 + block).astype(BF)
    mine = whole(8)[:, :128]
    theirs = whole(29)[:, :128]
    part_a[0, 8] = jnp.concatenate([mine, theirs, jnp.zeros_like(mine)], axis=1).astype(BF)
    part_a[0, 9 + core] = whole(7).astype(BF)
    part_a[0, 10 - core] = whole(28).astype(BF)
    for block in range(4):
        part_b[0, block * 2 + core] = whole(3 + block).astype(BF)
        part_b[0, block * 2 + 1 - core] = whole(24 + block).astype(BF)
    for z in range(4):
        for block in range(2):
            for part in range(4):
                rows[6 * part : 6 * part + 6, :] = piece(z, 13 + block * 4 + part)
            if z < 3:
                part_b[0, 8 + z * 2 + block] = rows[...].astype(BF)
            else:
                part_a[0, 13 + block] = rows[...].astype(BF)


def send_sums_kernel(info, a_kept, a_came, b_kept, b_came, kept, sent, rows):
    core = info[0]

    def spread(near, came, place, block):
        rows[...] = near[0, place].astype(F32) + came[0, place].astype(F32)
        pieces = [rows[6 * z : 6 * z + 6, :] for z in range(4)]
        for index in range(4):
            z = coordinate_at(info, "z", index)
            low = jnp.where(z % 2 == 0, pieces[0], pieces[1])
            high = jnp.where(z % 2 == 0, pieces[2], pieces[3])
            piece = jnp.where(z < 2, low, high).astype(BF)
            (kept if index < 2 else sent)[index % 2, block] = piece

    for side, first in ((core, 0), (1 - core, 13)):
        for third in range(3):
            spread(a_kept, a_came, third * 2 + side, first + third)
        for block in range(5):
            spread(b_kept, b_came, block * 2 + side, first + 3 + block)
    spread(a_kept, a_came, 8, 8)
    for block in range(2):
        spread(a_kept, a_came, 6 + block, 9 + block)
        spread(b_kept, b_came, 10 + block, 11 + block)


def shares_kernel(
    info, held, came, c_kept, c_came,
    qkv, out, ffn_in, ffn_bias, ffn_out, conv_in, conv_taps, conv_out, biases, gains, turned,
):
    width = out.shape[1]
    half, wide = width // 2, ffn_in.shape[1] // 2

    def put(target, first, apart, place):
        own_columns, other = held[0, place].astype(F32), came[0, place].astype(F32)
        target[:, first : first + LANES] = jnp.where(info[0] == 0, own_columns, other)
        target[:, first + apart : first + apart + LANES] = jnp.where(info[0] == 0, other, own_columns)

    for third in range(3):
        put(qkv, third * width, half, third)
    for block in range(4):
        put(ffn_in, block * LANES, wide, 3 + block)
    put(conv_in, 0, half, 7)
    for block in range(2):
        columns = slice(block * LANES, (block + 1) * LANES)
        out[:, columns] = held[0, 9 + block].astype(F32)
        conv_out[:, columns] = held[0, 11 + block].astype(F32)
        ffn_out[:, columns] = c_kept[0, block].astype(F32) + c_came[0, block].astype(F32)
    turned[...] = jnp.zeros_like(turned)
    turned[0:6, :] = held[0, 8].astype(F32)[:, :128]
    biases[...] = turned[0:6, 0:9]
    conv_taps[...] = turned[0:6, 12:27]
    small = jnp.transpose(turned[...])
    gains[...] = small[9:12, 0:6]
    for i in range(4):
        ffn_bias[0:1, 6 * i : 6 * i + 6] = small[27 + i : 28 + i, 0:6]


def erf_parts(operand):
    cumulative = 0.5 * (1.0 + lax.erf(operand * (0.5**0.5)))
    density = jnp.exp(-0.5 * operand * operand) * (0.5 / math.pi) ** 0.5
    return (cumulative, density)


def dot(left_side, right_side, left_dim=1, right_dim=0):
    return lax.dot_general(
        left_side, right_side, (((left_dim,), (right_dim,)), ((), ())), preferred_element_type=F32
    )


def normed(residual):
    centered = residual - jnp.mean(residual, axis=-1, keepdims=True)
    inverse = lax.rsqrt(jnp.mean(centered * centered, axis=-1, keepdims=True) + EPSILON)
    return (centered * inverse, inverse)


def normed_back(grad, norm, inverse, gain_row):
    scaled = grad * gain_row
    return inverse * (
        scaled
        - jnp.mean(scaled, axis=-1, keepdims=True)
        - norm * jnp.mean(scaled * norm, axis=-1, keepdims=True)
    )


def each(count, size, body):
    def step(index, unused):
        body(pl.ds(pl.multiple_of(index * size, size), size))
        return unused

    lax.fori_loop(0, count, step, 0)


def slots(position, ends, batch):
    number = jnp.zeros(position.shape, jnp.int32)
    for place in range(SLOTS):
        number = number + (position >= ends[4 + SLOTS * batch + place]).astype(jnp.int32)
    return number


def attention_kernel(
    flow, info, tokens, part_a, order, qkv_w, out_w, rows, taps, ffn_bias, qkv, attended, soft, part
):
    half = out_w.shape[0]
    per_batch = soft.shape[1]
    flow.arrive()
    for x in range(4):
        there = slice(96 * x, 96 * x + 96)
        for block in range(3):
            columns = slice(block * LANES, (block + 1) * LANES)
            qkv_w[there, columns] = tall_rows(info, part_a, "yx", block * 2, x).astype(BF)
            below = slice(half + 96 * x, half + 96 * x + 96)
            qkv_w[below, columns] = tall_rows(info, part_a, "yx", block * 2 + 1, x).astype(BF)
        for block in range(2):
            columns = slice(block * LANES, (block + 1) * LANES)
            out_w[there, columns] = tall_rows(info, part_a, "yx", 6 + block, x).astype(BF)
    flow.leave(0, 1)
    small = jnp.concatenate([tall_rows(info, part_a, "yx", 8, x) for x in range(4)], axis=0)
    mine = jnp.transpose(small[:, 0:128])
    theirs = jnp.transpose(small[:, 128:256])
    rows[...] = jnp.zeros_like(rows)
    left, right = jnp.where(info[0] == 0, mine, theirs), jnp.where(info[0] == 0, theirs, mine)
    rows[0:12, :half] = left[0:12, :]
    rows[0:12, half:] = right[0:12, :]
    rows[12:14, :half] = mine[0:2, :]
    rows[14:15, :half] = mine[6:7, :]
    taps[...] = jnp.zeros_like(taps)
    taps[0:15, :] = mine[12:27, :]
    spread = jnp.concatenate(
        [
            jnp.concatenate([mine[27 + i : 28 + i, 96 * x : 96 * x + 96] for i in range(4)], axis=1)
            for x in range(4)
        ]
        + [jnp.zeros((4, half), F32)],
        axis=0,
    )
    spread = dot(spread.astype(BF), order[...])
    for x in range(4):
        ffn_bias[0:1, x * LANES : (x + 1) * LANES] = spread[x : x + 1, :]
    for third in range(3):
        columns = slice(third * half, (third + 1) * half)
        block = dot(tokens[...], qkv_w[:, columns])
        if third != 1:
            block = block + rows[12 + third // 2 : 13 + third // 2, :half]
        qkv[:, columns] = block.astype(BF)
    square = (per_batch, per_batch)
    down = lax.broadcasted_iota(jnp.int32, square, 0)
    across = lax.broadcasted_iota(jnp.int32, square, 1)
    lane = lax.broadcasted_iota(jnp.int32, (per_batch, 128), 1)
    pairs = half // 128
    for batch in range(tokens.shape[0] // per_batch):
        there = slice(batch * per_batch, (batch + 1) * per_batch)
        slot_down, slot_across = slots(down, info, batch), slots(across, info, batch)
        allowed = (slot_down == slot_across) & ((slot_across < SLOTS - 1) | (down == across))
        forbidden = jnp.where(allowed, 0.0, -1e9)
        for pair in range(pairs):
            columns = slice(pair * 128, (pair + 1) * 128)
            query = qkv[there, columns]
            key = qkv[there, half + pair * 128 : half + (pair + 1) * 128]
            value = qkv[there, 2 * half + pair * 128 : 2 * half + (pair + 1) * 128]
            result = jnp.zeros((per_batch, 128), F32)
            for side in range(2):
                mine = (lane >= HEAD_DIM) if side else (lane < HEAD_DIM)
                scores = dot(jnp.where(mine, query, jnp.zeros_like(query)), key, 1, 1)
                scores = scores * HEAD_DIM ** (-0.5) + forbidden
                exponent = jnp.exp(scores - jnp.max(scores, axis=-1, keepdims=True))
                weight = (exponent * (1.0 / jnp.sum(exponent, axis=-1, keepdims=True))).astype(BF)
                soft[(batch * pairs + pair) * 2 + side] = weight
                result = result + dot(weight, jnp.where(mine, value, jnp.zeros_like(value)))
            attended[there, columns] = result.astype(BF)
    flow.leave(5, 6, 7)
    part[...] = dot(attended[...], out_w[...]).astype(BF)


def feed_kernel(
    flow, info, tokens, mine, theirs, rows, part_b, part_a, ffn_bias,
    ffn_in, ffn_out, conv_in, conv_out, hidden, norm, inverse, activated, slope, part,
):
    half = conv_in.shape[1]

    def first(there):
        residual = (
            tokens[there, :].astype(F32)
            + (mine[there, :].astype(F32) + theirs[there, :].astype(F32))
            + rows[2:3, :]
        )
        unit, scale = normed(residual)
        norm[there, :] = unit
        inverse[there, :] = jnp.broadcast_to(scale, (scale.shape[0], 128))
        hidden[there, :] = (unit * rows[9:10, :] + rows[3:4, :]).astype(BF)

    each(tokens.shape[0] // 64, 64, first)
    flow.leave(5, 6)
    flow.arrive(5, 6)
    for x in range(4):
        for side in range(2):
            there = slice(half * side + 96 * x, half * side + 96 * x + 96)
            for block in range(4):
                columns = slice(block * LANES, (block + 1) * LANES)
                ffn_in[there, columns] = tall_rows(info, part_b, "xy", block * 2 + side, x).astype(BF)
            conv_in[there, :] = tall_rows(info, part_a, "yx", side, x).astype(BF)
        for block in range(2):
            columns = slice(block * LANES, (block + 1) * LANES)
            conv_out[96 * x : 96 * x + 96, columns] = tall_rows(info, part_a, "yx", 2 + block, x).astype(BF)
    flow.leave(0)
    wide = ffn_in.shape[1]
    chunk = 256

    def second(index, unused):
        columns = pl.ds(pl.multiple_of(index * chunk, chunk), chunk)
        up = dot(hidden[...], ffn_in[:, columns]) + ffn_bias[0:1, columns]
        cumulative, density = erf_parts(up)
        activated[:, columns] = (up * cumulative).astype(BF)
        slope[:, columns] = (cumulative + up * density).astype(BF)
        return unused

    lax.fori_loop(0, wide // chunk, second, 0)
    flow.leave(7, 8)
    for x in range(4):
        for y in range(4):
            for block in range(2):
                indices = {"x": index_at(info, "x", x), "y": index_at(info, "y", y)}
                place = outer_inner("xy", indices)
                pieces = [part_b[place, 8 + z * 2 + block].astype(F32) for z in range(3)]
                pieces.append(part_a[outer_inner("yx", indices), 4 + block].astype(F32))
                row = 384 * x + 96 * y
                ffn_out[row : row + 96, block * LANES : (block + 1) * LANES] = jnp.concatenate(
                    pieces, axis=0
                ).astype(BF)
    flow.leave(1)
    part[...] = dot(activated[...], ffn_out[...]).astype(BF)


def tap_row(taps, info, batch, offset):
    choice = info[1 + batch]
    row = taps[11 + offset : 12 + offset, :]
    row = jnp.where(choice == 1, taps[5 + offset : 6 + offset, :] if abs(offset) < 3 else 0.0, row)
    return jnp.where(choice == 0, taps[1 + offset : 2 + offset, :] if abs(offset) < 2 else 0.0, row)


def fill_slots(info, padded, per_batch, batches):
    position = lax.broadcasted_iota(jnp.int32, (per_batch, 128), 0)
    outside = jnp.full((8, 128), -1, jnp.int32)
    for batch in range(batches):
        padded[batch, 0:8, :] = outside
        padded[batch, 8 : 8 + per_batch, :] = slots(position, info, batch)
        padded[batch, 8 + per_batch :, :] = outside


def clear_edges(padded, per_batch, batches):
    edge = jnp.zeros((8, padded.shape[2]), F32)
    for batch in range(batches):
        padded[batch, 0:8, :] = edge
        padded[batch, 8 + per_batch :, :] = edge


def convolution_kernel(
    flow, info, hidden, mine, theirs, rows, conv_in, taps, conv_out,
    phase_one, norm, inverse, mixed, gated, slope, part, slot_pad, mixed_pad,
):
    batches = slot_pad.shape[0]
    per_batch = hidden.shape[0] // batches
    half = conv_in.shape[1]

    def first(there):
        residual = (
            hidden[there, :].astype(F32)
            + (mine[there, :].astype(F32) + theirs[there, :].astype(F32))
            + rows[4:5, :]
        )
        unit, scale = normed(residual)
        norm[there, :] = unit
        inverse[there, :] = jnp.broadcast_to(scale, (scale.shape[0], 128))
        phase_one[there, :] = (unit * rows[10:11, :] + rows[5:6, :]).astype(BF)

    each(hidden.shape[0] // 64, 64, first)
    flow.leave(1, 2)
    fill_slots(info, slot_pad, per_batch, batches)
    clear_edges(mixed_pad, per_batch, batches)
    mixed[...] = dot(phase_one[...], conv_in[...]) + rows[14:15, :half]
    for batch in range(batches):
        there = slice(batch * per_batch, (batch + 1) * per_batch)
        mixed_pad[batch, 8 : 8 + per_batch, :] = mixed[there, :]
        for column in range(half // 128):
            columns = slice(column * 128, (column + 1) * 128)
            here = slot_pad[batch, 8 : 8 + per_batch, :]
            total = jnp.zeros((per_batch, 128), F32)
            for offset in range(-3, 4):
                same = slot_pad[batch, 8 + offset : 8 + offset + per_batch, :] == here
                moved = mixed_pad[batch, 8 + offset : 8 + offset + per_batch, columns]
                tap = tap_row(taps, info, batch, offset)[:, columns]
                total = total + jnp.where(same, moved, 0.0) * tap
            cumulative, density = erf_parts(total)
            gated[there, columns] = (total * cumulative).astype(BF)
            slope[there, columns] = cumulative + total * density
    part[...] = dot(gated[...], conv_out[...]).astype(BF)


def own(info, row):
    half = row.shape[1] // 2
    return jnp.where(info[0] == 0, row[:, :half], row[:, half:])


def convolution_back_kernel(
    flow, info, phase_one, mine, theirs, cotangent, rows, conv_in, taps, conv_out, mixed, gated, slope,
    result, grad_three, kept, sent, part, sums, d_taps,
    slot_pad, mixed_pad, grad_pad, grad_low, grad_mixed, wide_sums, whole,
):
    batches = slot_pad.shape[0]
    per_batch = phase_one.shape[0] // batches
    half = conv_in.shape[1]
    fill_slots(info, slot_pad, per_batch, batches)
    clear_edges(mixed_pad, per_batch, batches)
    clear_edges(grad_pad, per_batch, batches)
    wide_sums[...] = jnp.zeros_like(wide_sums)
    flow.arrive()
    size = 64
    for batch in range(batches):

        def first(index, unused):
            inner = pl.multiple_of(index * size, size)
            there = pl.ds(pl.multiple_of(batch * per_batch + inner, size), size)
            residual = (
                phase_one[there, :].astype(F32)
                + (mine[there, :].astype(F32) + theirs[there, :].astype(F32))
                + rows[7:8, :]
            )
            unit, scale = normed(residual)
            ended = (unit * rows[11:12, :] + rows[8:9, :]).astype(BF)
            result[there, :] = jnp.where(info[0] == 0, phase_one[there, :], ended)
            valid = slot_pad[batch, pl.ds(pl.multiple_of(8 + inner, 8), size), :][:, :1] < SLOTS - 1
            masked = jnp.where(valid, cotangent[there, :].astype(F32), 0.0)
            grad = normed_back(masked, unit, scale, rows[11:12, :])
            grad_three[there, :] = grad
            low = grad.astype(BF)
            grad_low[there, :] = low
            wide_sums[0:1, :] += jnp.sum(low.astype(F32), axis=0, keepdims=True)
            wide_sums[1:2, :] += jnp.sum(masked, axis=0, keepdims=True)
            wide_sums[2:3, :] += jnp.sum(masked * unit, axis=0, keepdims=True)
            return unused

        lax.fori_loop(0, per_batch // size, first, 0)
    flow.leave(0)
    for block in range(2):
        columns = slice(block * LANES, (block + 1) * LANES)
        whole[0:half, :] = dot(gated[...], grad_low[:, columns], 0, 0)
        pack_rows(info, whole, "xy", 2 + block, kept, sent, 0)
    tap_sums = [[[] for offset in range(7)] for batch in range(batches)]
    for batch in range(batches):
        there = slice(batch * per_batch, (batch + 1) * per_batch)
        grad_pad[batch, 8 : 8 + per_batch, :] = (
            dot(grad_low[there, :], conv_out[...], 1, 1) * slope[there, :]
        )
        mixed_pad[batch, 8 : 8 + per_batch, :] = mixed[there, :]
        for column in range(half // 128):
            columns = slice(column * 128, (column + 1) * 128)
            here = slot_pad[batch, 8 : 8 + per_batch, :]
            grad = grad_pad[batch, 8 : 8 + per_batch, columns]
            total = jnp.zeros((per_batch, 128), F32)
            for offset in range(-3, 4):
                away = slice(8 + offset, 8 + offset + per_batch)
                same = slot_pad[batch, away, :] == here
                tap = tap_row(taps, info, batch, -offset)[:, columns]
                total = total + jnp.where(same, grad_pad[batch, away, columns], 0.0) * tap
                term = jnp.where(same, mixed_pad[batch, away, columns], 0.0) * grad
                tap_sums[batch][offset + 3].append(jnp.sum(term, axis=0, keepdims=True))
            grad_mixed[there, columns] = total.astype(BF)
    for choice in range(3):
        for offset in range(-choice - 1, choice + 2):
            row = choice * choice + 2 * choice + offset + choice + 1
            total = jnp.zeros((1, half), F32)
            for batch in range(batches):
                joined = jnp.concatenate(tap_sums[batch][offset + 3], axis=1)
                total = total + jnp.where(info[1 + batch] == choice, joined, 0.0)
            d_taps[row : row + 1, :] = total
    d_taps[15:16, :] = jnp.zeros((1, half), F32)
    whole[...] = dot(phase_one[...], grad_mixed[...], 0, 0)
    for side in range(2):
        pack_rows(info, whole, "xy", side, kept, sent, side * half)
    part[...] = dot(grad_mixed[...], conv_in[...], 1, 1).astype(BF)
    sums[0:1, :] = jnp.sum(grad_mixed[...].astype(F32), axis=0, keepdims=True)
    for place in range(3):
        sums[place + 1 : place + 2, :] = own(info, wide_sums[place : place + 1, :])
    sums[4:8, :] = jnp.zeros((4, half), F32)


def feed_back_kernel(
    flow, info, grad_three, mine, theirs, norm, inverse, rows, activated, slope, hidden, ffn_in, ffn_out,
    conv_kept, conv_sent,
    grad_phase_one, grad_two, b_kept, b_sent, c_kept, c_sent, part, sums, bias_sums,
    grad_low, grad_up, wide_sums, whole,
):
    wide_sums[...] = jnp.zeros_like(wide_sums)
    flow.arrive(4, 5)

    def first(there):
        arriving = grad_three[there, :] + (mine[there, :].astype(F32) + theirs[there, :].astype(F32))
        arriving = arriving.astype(BF)
        grad_phase_one[there, :] = arriving
        arriving = arriving.astype(F32)
        unit = norm[there, :]
        grad = normed_back(arriving, unit, inverse[there, :1], rows[10:11, :])
        grad_two[there, :] = grad
        low = grad.astype(BF)
        grad_low[there, :] = low
        wide_sums[0:1, :] += jnp.sum(low.astype(F32), axis=0, keepdims=True)
        wide_sums[1:2, :] += jnp.sum(arriving, axis=0, keepdims=True)
        wide_sums[2:3, :] += jnp.sum(arriving * unit, axis=0, keepdims=True)

    each(hidden.shape[0] // 64, 64, first)
    flow.leave(0)
    flow.arrive(7, 8, 10, 11)
    half = ffn_in.shape[0] // 2
    for block in range(ffn_in.shape[1] // LANES):
        columns = slice(block * LANES, (block + 1) * LANES)
        grad = dot(grad_low[...], ffn_out[columns, :], 1, 1) * slope[:, columns].astype(F32)
        low = grad.astype(BF)
        grad_up[:, columns] = low
        bias_sums[0:1, columns] = jnp.sum(low.astype(F32), axis=0, keepdims=True)
        whole[...] = dot(hidden[...], low, 0, 0)
        for side in range(2):
            pack_rows(info, whole, "xy", block * 2 + side, b_kept, b_sent, side * half)
    for place in range(8):
        for block in range(4):
            b_kept[place, 8 + block] = conv_kept[place, block]
            b_sent[place, 8 + block] = conv_sent[place, block]
    for step in range(4):
        x = coordinate_at(info, "x", step)
        there = pl.ds(pl.multiple_of(x * 384, 128), 384)
        for block in range(2):
            columns = slice(block * LANES, (block + 1) * LANES)
            whole[0:384, :] = dot(activated[:, there], grad_low[:, columns], 0, 0)
            for outer in range(4):
                for inner in range(4):
                    z, y = coordinate_at(info, "z", outer), coordinate_at(info, "y", inner)
                    piece = whole[pl.ds(pl.multiple_of(96 * y + 24 * z, 8), 24), :].astype(BF)
                    place = ((outer % 2) * 4 + step) * 4 + inner
                    (c_kept if outer < 2 else c_sent)[place, block] = piece
    part[...] = dot(grad_up[...], ffn_in[...], 1, 1).astype(BF)
    for place in range(3):
        sums[place : place + 1, :] = own(info, wide_sums[place : place + 1, :])
    sums[3:8, :] = jnp.zeros((5, sums.shape[1]), F32)


def attention_back_kernel(
    flow, info, grad_two, mine, theirs, norm, inverse, rows, tokens, qkv, attended, soft, qkv_w, out_w,
    sums_two, sums_three, d_taps, bias_sums, order,
    grad_one, kept, sent, part, grad_low, grad_attended, grad_qkv, wide_sums, whole, sums,
):
    flow.arrive(4, 5)
    half = out_w.shape[0]
    per_batch = soft.shape[1]
    wide_sums[...] = jnp.zeros_like(wide_sums)

    def first(there):
        arriving = grad_two[there, :] + (mine[there, :].astype(F32) + theirs[there, :].astype(F32))
        unit = norm[there, :]
        grad = normed_back(arriving, unit, inverse[there, :1], rows[9:10, :])
        grad_one[there, :] = grad
        low = grad.astype(BF)
        grad_low[there, :] = low
        wide_sums[0:1, :] += jnp.sum(low.astype(F32), axis=0, keepdims=True)
        wide_sums[1:2, :] += jnp.sum(arriving, axis=0, keepdims=True)
        wide_sums[2:3, :] += jnp.sum(arriving * unit, axis=0, keepdims=True)

    each(tokens.shape[0] // 64, 64, first)
    flow.leave(0)
    flow.arrive(7, 8, 9, 10, 11, 12)
    for block in range(2):
        columns = slice(block * LANES, (block + 1) * LANES)
        whole[0:half, :] = dot(attended[...], grad_low[:, columns], 0, 0)
        pack_rows(info, whole, "yx", 6 + block, kept, sent, 0)
    grad_attended[...] = dot(grad_low[...], out_w[...], 1, 1).astype(BF)
    lane = lax.broadcasted_iota(jnp.int32, (per_batch, 128), 1)
    pairs = half // 128
    scale = HEAD_DIM ** (-0.5)
    for batch in range(tokens.shape[0] // per_batch):
        there = slice(batch * per_batch, (batch + 1) * per_batch)
        for pair in range(pairs):
            columns = [
                slice(third * half + pair * 128, third * half + (pair + 1) * 128) for third in range(3)
            ]
            query, key, value = (qkv[there, columns[third]] for third in range(3))
            grad = grad_attended[there, columns[0]]
            totals = [jnp.zeros((per_batch, 128), F32) for third in range(3)]
            for side in range(2):
                mine_lanes = (lane >= HEAD_DIM) if side else (lane < HEAD_DIM)

                def only(operand):
                    return jnp.where(mine_lanes, operand, jnp.zeros_like(operand))

                weight = soft[(batch * pairs + pair) * 2 + side]
                grad_side = only(grad)
                grad_soft = dot(grad_side, value, 1, 1)
                weight_wide = weight.astype(F32)
                inner = jnp.sum(grad_soft * weight_wide, axis=-1, keepdims=True)
                grad_scores = (weight_wide * (grad_soft - inner)).astype(BF)
                totals[0] = totals[0] + dot(grad_scores, only(key))
                totals[1] = totals[1] + dot(grad_scores, only(query), 0, 0)
                totals[2] = totals[2] + dot(weight, grad_side, 0, 0)
            grad_qkv[there, columns[0]] = (totals[0] * scale).astype(BF)
            grad_qkv[there, columns[1]] = (totals[1] * scale).astype(BF)
            grad_qkv[there, columns[2]] = totals[2].astype(BF)
    part[...] = dot(grad_qkv[...], qkv_w[...], 1, 1).astype(BF)
    sums[...] = jnp.zeros_like(sums)
    for third in range(3):
        columns = slice(third * half, (third + 1) * half)
        whole[...] = dot(tokens[...], grad_qkv[:, columns], 0, 0)
        for side in range(2):
            pack_rows(info, whole, "yx", third * 2 + side, kept, sent, side * half)
        if third != 1:
            place = third // 2
            sums[place : place + 1, :] = jnp.sum(
                grad_qkv[:, columns].astype(F32), axis=0, keepdims=True
            )
    sums[2:3, :] = own(info, wide_sums[0:1, :])
    sums[3:4, :] = own(info, wide_sums[1:2, :])
    sums[4:6, :] = sums_two[0:2, :]
    sums[6:9, :] = sums_three[0:3, :]
    sums[9:10, :] = own(info, wide_sums[2:3, :])
    sums[10:11, :] = sums_two[2:3, :]
    sums[11:12, :] = sums_three[3:4, :]
    sums[12:27, :] = d_taps[0:15, :]
    spread = jnp.concatenate(
        [bias_sums[0:1, x * LANES : (x + 1) * LANES] for x in range(4)] + [jnp.zeros((4, half), F32)], axis=0
    )
    spread = dot(spread.astype(BF), order[...], 1, 1)
    for i in range(4):
        sums[27 + i : 28 + i, :] = jnp.concatenate(
            [spread[x : x + 1, 96 * i : 96 * i + 96] for x in range(4)], axis=1
        )
    whole[0:half, :] = jnp.zeros((half, LANES), F32)
    whole[0:half, 0:128] = jnp.transpose(sums[...])
    pack_rows(info, whole, "yx", 8, kept, sent, 0)


class Flow:
    def __init__(self):
        self.coming, self.going = {}, {}

    def arrive(self, *chosen):
        for which in chosen or tuple(self.coming):
            for copy in self.coming[which]:
                copy.wait()

    def leave(self, *chosen):
        for which in chosen:
            self.going[which].start()


def kernel_call(body, outputs, scratch, has_info, *operands, late=(), early=(), mib=4, gflop=0):
    vmem = pl.BlockSpec(memory_space=pltpu.VMEM)
    smem = pl.BlockSpec(memory_space=pltpu.SMEM)
    hbm = pl.BlockSpec(memory_space=pltpu.HBM)
    groups = [operand if isinstance(operand, tuple) else (operand,) for operand in operands]
    arrays = [array for group in groups for array in group]
    moves = sum(len(groups[which]) for which in late) + len(early)

    def with_copies(*refs):
        taken = 0
        operand_refs = []
        for group in groups:
            operand_refs.append(refs[taken : taken + len(group)])
            taken += len(group)
        output_refs = list(refs[taken : taken + len(outputs)])
        own = refs[taken + len(outputs) : taken + len(outputs) + len(scratch)]
        buffers = list(refs[taken + len(outputs) + len(scratch) : -1])
        flags, used = refs[-1], 0
        flow = Flow()
        for which in late:
            buffer = buffers.pop(0)
            first, flow.coming[which] = 0, []
            for source in operand_refs[which]:
                count = source.shape[0]
                target = buffer if len(groups[which]) == 1 else buffer.at[pl.ds(first, count)]
                copy = pltpu.make_async_copy(source, target, flags.at[used])
                copy.start()
                flow.coming[which].append(copy)
                first, used = first + count, used + 1
            operand_refs[which] = (buffer,)
        for which in early:
            buffer = buffers.pop(0)
            flow.going[which] = pltpu.make_async_copy(buffer, output_refs[which], flags.at[used])
            output_refs[which] = buffer
            used += 1
        body(flow, *(group[0] for group in operand_refs), *output_refs, *own)
        for which in early:
            flow.going[which].wait()

    specs = [smem if has_info and place == 0 else vmem for place in range(len(operands))]
    out_specs = [vmem] * len(outputs)
    memory = [pltpu.VMEM(shape, dtype) for shape, dtype in scratch]
    for which in late:
        specs[which] = hbm
        whole = sum(array.shape[0] for array in groups[which])
        memory.append(pltpu.VMEM((whole, *groups[which][0].shape[1:]), groups[which][0].dtype))
    for which in early:
        out_specs[which] = hbm
        memory.append(pltpu.VMEM(*outputs[which]))
    if moves:
        memory.append(pltpu.SemaphoreType.DMA((moves,)))
    return pl.pallas_call(
        with_copies if moves else body,
        out_shape=[jax.ShapeDtypeStruct(shape, dtype) for shape, dtype in outputs],
        in_specs=[spec for spec, group in zip(specs, groups) for array in group],
        out_specs=out_specs,
        scratch_shapes=memory,
        compiler_params=pltpu.CompilerParams(vmem_limit_bytes=mib * 1024 * 1024),
        cost_estimate=pl.CostEstimate(flops=int(gflop * 1e9), bytes_accessed=1 << 20, transcendentals=0),
    )(*arrays)


def gather_weights(info, masters):
    (qkv, out, ffn_in, ffn_bias, ffn_out, conv_in, conv_taps, conv_out, biases, gains) = masters
    mine, theirs = kernel_call(
        send_weights_kernel,
        [((21, 6, LANES), BF), ((9, 6, LANES), BF)],
        [((128, 128), F32)],
        True,
        lax.axis_index("phase").astype(jnp.int32).reshape(1), qkv, out, ffn_in, ffn_bias.reshape(1, -1), ffn_out,
        conv_in, conv_taps.T, conv_out, biases.T, gains,
        late=tuple(range(1, 11)),
        mib=60,
    )

    def together(*values):
        return lax.optimization_barrier(values)

    line = jnp.concatenate([mine, swap(theirs)])
    part_a, part_b = kernel_call(
        line_weights_kernel,
        [((1, 15, 24, LANES), BF), ((1, 14, 24, LANES), BF)],
        [((24, LANES), F32)],
        True,
        info, line, *(lax.ppermute(line, BOTH, across(mask)) for mask in (1, 2, 3)),
    )
    for step in range(2):
        part_a, part_b = together(grown(part_a, "x", step), grown(part_b, "y", step))
    came = lax.ppermute(part_a, BOTH, partners("y", 0))
    early, late, part_b = together(
        jnp.concatenate([part_a[:, :9], came[:, :9]]),
        jnp.concatenate([part_a[:, 9:], came[:, 9:]]),
        grown(part_b, "x", 0),
    )
    return (
        (early, lax.ppermute(early, BOTH, partners("y", 1))),
        (late, lax.ppermute(late, BOTH, partners("y", 1))),
        (part_b, lax.ppermute(part_b, BOTH, partners("x", 1))),
    )


def shards(
    tokens,
    cotangent,
    lengths,
    kernel_choice,
    *masters,
):
    batches = lengths.shape[0]
    rows, width = tokens.shape
    per_batch = rows // batches
    half = width // 2
    wide = masters[2].shape[1] // 2
    heads = half // HEAD_DIM
    info = info_of(lengths, kernel_choice)
    part_a, rest, part_b = gather_weights(info, masters)
    order = bias_order()
    low, full = ((rows, width), BF), ((rows, width), F32)
    narrow = ((rows, 128), F32)
    slot_pad = ((batches, per_batch + 16, 128), jnp.int32)
    row_pad = ((batches, per_batch + 16, half), F32)
    whole = ((width, LANES), F32)

    def halves(blocks):
        return [((8, blocks, 24, LANES), BF)] * 2

    qkv_w, out_w, all_rows, taps, ffn_bias, qkv, attended, soft, part = kernel_call(
        attention_kernel,
        [
            ((width, 3 * half), BF), ((half, width), BF), ((16, width), F32),
            ((16, half), F32), ((1, wide), F32), ((rows, 3 * half), BF), ((rows, half), BF),
            ((batches * heads, per_batch, per_batch), BF), low,
        ],
        [],
        True,
        info, tokens, part_a, order,
        late=(2,),
        early=(0, 1, 5, 6, 7),
        gflop=5,
        mib=16,
    )
    ffn_in, ffn_out, conv_in, conv_out, hidden, norm_one, inverse_one, activated, slope_up, part_two = kernel_call(
        feed_kernel,
        [
            ((width, wide), BF), ((wide, width), BF), ((width, half), BF), ((half, width), BF), low, full, narrow, ((rows, wide), BF), ((rows, wide), BF), low,
        ],
        [],
        True,
        info, tokens, part, swap(part), all_rows, part_b, rest, ffn_bias,
        late=(5, 6),
        early=(0, 1, 5, 6, 7, 8),
        gflop=8,
        mib=24,
    )
    phase_one, norm_two, inverse_two, mixed, gated, slope, part_three = kernel_call(
        convolution_kernel,
        [low, full, narrow, ((rows, half), F32), ((rows, half), BF), ((rows, half), F32), low],
        [slot_pad, row_pad],
        True,
        info, hidden, part_two, swap(part_two), all_rows, conv_in, taps, conv_out,
        early=(1, 2),
        gflop=4,
        mib=8,
    )
    block_outputs, grad_three, conv_kept, conv_sent, part, sums_three, d_taps = kernel_call(
        convolution_back_kernel,
        [low, full, *halves(4), low, ((8, half), F32), ((16, half), F32)],
        [slot_pad, row_pad, row_pad, low, ((rows, half), BF), ((8, width), F32), whole],
        True,
        info, phase_one, part_three, swap(part_three), cotangent, all_rows, conv_in, taps, conv_out,
        mixed, gated, slope,
        late=(4,),
        early=(0,),
        gflop=8,
        mib=10,
    )
    grad_phase_one, grad_two, b_kept, b_sent, c_kept, c_sent, part, sums_two, d_ffn_bias = kernel_call(
        feed_back_kernel,
        [
            low, full, *halves(12), ((32, 2, 24, LANES), BF), ((32, 2, 24, LANES), BF), low,
            ((8, half), F32), ((1, wide), F32),
        ],
        [low, ((rows, wide), BF), ((8, width), F32), whole],
        True,
        info, grad_three, part, swap(part), norm_two, inverse_two, all_rows, activated, slope_up, hidden,
        ffn_in, ffn_out, conv_kept, conv_sent,
        late=(4, 5, 7, 8, 10, 11),
        early=(0,),
        gflop=10,
        mib=20,
    )
    grad_one, a_kept, a_sent, part = kernel_call(
        attention_back_kernel,
        [full, *halves(9), low],
        [low, ((rows, half), BF), ((rows, 3 * half), BF), ((8, width), F32), whole, ((128, half), F32)],
        True,
        info, grad_two, part, swap(part), norm_one, inverse_one, all_rows, tokens, qkv, attended, soft,
        qkv_w, out_w, sums_two, sums_three, d_taps, d_ffn_bias, order,
        late=(4, 5, 7, 8, 9, 10, 11, 12),
        early=(0,),
        gflop=10,
        mib=20,
    )
    b_kept, b_sent = shrunk(b_kept, b_sent, "x", 1)
    c_kept, c_sent = shrunk(c_kept, c_sent, "z", 1)
    a_kept, a_sent = shrunk(after(a_kept, b_sent, c_sent), a_sent, "y", 1)
    b_kept, b_sent = shrunk(b_kept, b_sent, "x", 0)
    c_kept, c_sent = shrunk(c_kept, c_sent, "z", 0)
    a_kept, a_sent = shrunk(after(a_kept, b_sent, c_sent), a_sent, "y", 0)
    b_kept, b_sent = shrunk(after(b_kept, a_sent), b_sent, "y", 1)
    c_kept, c_sent = shrunk(after(c_kept, a_sent), c_sent, "x", 1)
    a_kept, a_sent = shrunk(after(a_kept, b_sent, c_sent), a_sent, "x", 1)
    c_kept, c_sent = shrunk(after(c_kept, a_sent), c_sent, "x", 0)
    kept, sent = kernel_call(
        send_sums_kernel,
        [((2, 21, 6, LANES), BF)] * 2,
        [((24, LANES), F32)],
        True,
        info,
        a_kept, lax.ppermute(a_sent, BOTH, partners("x", 0)),
        b_kept, lax.ppermute(b_sent, BOTH, partners("y", 0)),
    )
    c_kept, c_sent = shrunk(after(c_kept, sent), c_sent, "y", 1)
    grad_one = after(grad_one, sent)
    kept, sent = shrunk(kept, sent, "z", 1)
    came = lax.ppermute(sent, BOTH, partners("z", 0))
    held, other = (
        (kept[:, there].astype(F32) + came[:, there].astype(F32)).astype(BF)
        for there in (slice(0, 13), slice(13, 21))
    )
    shapes = [master.shape for master in masters]
    shapes[3] = (1, shapes[3][0])
    for turned in (6, 8):
        shapes[turned] = shapes[turned][::-1]
    shares = list(
        kernel_call(
            shares_kernel,
            [(shape, F32) for shape in shapes],
            [((128, 128), F32)],
            True,
            info, held, swap(other), c_kept, lax.ppermute(c_sent, BOTH, partners("y", 0)),
        )
    )
    shares[3] = shares[3].reshape(-1)
    for turned in (6, 8):
        shares[turned] = shares[turned].T
    grad_tokens = (grad_one + (part.astype(F32) + swap(part).astype(F32))).astype(BF)
    input_grads = jnp.where(lax.axis_index("phase") == 0, grad_tokens, grad_phase_one)
    return (block_outputs[None], input_grads[None], *shares)


def solution(mesh):
    sharded, columns = P(BOTH, None), P(None, BOTH)
    weights = (sharded, sharded, sharded, P(BOTH), sharded, sharded, columns, sharded, columns, columns)
    return jax.shard_map(
        shards,
        mesh=mesh,
        in_specs=(P("dp", None), P("dp", None), P("dp", None), P("dp"), *weights),
        out_specs=(P("phase", "dp", None), P("phase", "dp", None), *weights),
        check_vma=False,
    )
```

```python
import math

import jax
import jax.numpy as jnp
import numpy as np
from jax import lax
from jax.experimental import pallas as pl
from jax.experimental.pallas import tpu as pltpu
from jax.sharding import PartitionSpec as P

HEAD_DIM = 64
EPSILON = 1e-05
BOTH = ("phase", "dp")
STRIDE = {"x": 16, "y": 4, "z": 1}
AXES = "xyz"
LANES = 384
SLOTS = 6
SWAP = [(0, 1), (1, 0)]
BF = jnp.bfloat16
F32 = jnp.float32


def partners(axis, step):
    pairs = []
    for core in range(2):
        mask = (1, 3)[(core + step) % 2]
        for chip in range(64):
            coordinate = (chip // STRIDE[axis]) % 4
            target = chip + ((coordinate ^ mask) - coordinate) * STRIDE[axis]
            pairs.append((core * 64 + chip, core * 64 + target))
    return pairs


def across(mask):
    return [(device, device + (((device % 4) ^ mask) - device % 4)) for device in range(128)]


def grown(held, axis, step):
    return jnp.concatenate([held, lax.ppermute(held, BOTH, partners(axis, step))])


def exchanged(sent, axis, step):
    return lax.ppermute(sent, BOTH, partners(axis, step))


def halved(kept, came):
    count = kept.shape[0] // 2
    return tuple(
        (kept[there].astype(F32) + came[there].astype(F32)).astype(BF)
        for there in (slice(0, count), slice(count, 2 * count))
    )


def after(value, *others):
    return lax.optimization_barrier((value, *others))[0]


def swap(part):
    return lax.ppermute(part, "phase", SWAP)


def bias_order():
    table = np.zeros((LANES, LANES), np.float32)
    for i in range(4):
        for d in range(16):
            for j in range(6):
                table[96 * i + 6 * d + j, 24 * d + 6 * i + j] = 1.0
    return jnp.asarray(table, BF)


def info_of(lengths, kernel_choice):
    core = lax.axis_index("phase").astype(jnp.int32)
    chip = lax.axis_index("dp").astype(jnp.int32)
    return jnp.concatenate(
        [
            core[None],
            kernel_choice,
            jnp.zeros((3 - kernel_choice.shape[0],), jnp.int32),
            jnp.cumsum(lengths, axis=-1).reshape(-1),
            jnp.stack([(chip // STRIDE[axis]) % 4 for axis in AXES]),
            jnp.stack([1 + 2 * core, 3 - 2 * core]),
        ]
    )


def coordinate_at(info, axis, index):
    here = info[16 + AXES.index(axis)]
    return here ^ (0, info[19], info[20], 2)[index]


def index_at(info, axis, coordinate):
    apart = info[16 + AXES.index(axis)] ^ coordinate
    return jnp.where(
        apart == 0, 0, jnp.where(apart == info[19], 1, jnp.where(apart == info[20], 2, 3))
    )


def outer_inner(order, indices):
    place = 0
    for axis in order:
        place = place * 4 + indices[axis]
    return place


def tall_rows(info, part, order, block, x):
    pieces = []
    for y in range(4):
        place = outer_inner(order, {"x": index_at(info, "x", x), "y": index_at(info, "y", y)})
        pieces.append(part[place, block].astype(F32))
    return jnp.concatenate(pieces, axis=0)


def pack_rows(info, source, order, block, kept, sent, first_row):
    for outer in range(4):
        for inner in range(4):
            place = {order[0]: coordinate_at(info, order[0], outer)}
            place[order[1]] = coordinate_at(info, order[1], inner)
            row = pl.multiple_of(first_row + 96 * place["x"] + 24 * place["y"], 8)
            piece = source[pl.ds(row, 24), :].astype(BF)
            (kept if outer < 2 else sent)[(outer % 2) * 4 + inner, block] = piece


def send_weights_kernel(
    flow, core, qkv, out, ffn_in, ffn_bias, ffn_out, conv_in, conv_taps, conv_out, biases, gains,
    mine, theirs, turned, mine_rows, their_rows,
):
    width = out.shape[1]
    half, wide = width // 2, ffn_in.shape[1] // 2
    turned[...] = jnp.zeros_like(turned)
    flow.arrive()
    turned[9:12, 0:6] = gains[...]
    for i in range(4):
        turned[27 + i : 28 + i, 0:6] = ffn_bias[0:1, 6 * i : 6 * i + 6]
    turned[0:8, :] = jnp.transpose(turned[...])[0:8, :]
    turned[0:6, 0:9] = biases[...]
    turned[0:6, 12:27] = conv_taps[...]
    small = turned[0:6, :]
    blank = jnp.zeros((6, LANES - 128), F32)
    small = jnp.concatenate([small, blank], axis=1)
    mine_rows[120:128, :] = jnp.zeros((8, LANES), F32)
    their_rows[48:56, :] = jnp.zeros((8, LANES), F32)

    def put(target, place, block):
        target[6 * place : 6 * place + 6, :] = block

    def pair(source, first, apart):
        return (source[:, first : first + LANES], source[:, first + apart : first + apart + LANES])

    places = [pair(qkv, third * width, half) for third in range(3)]
    places += [pair(ffn_in, block * LANES, wide) for block in range(4)]
    places.append(pair(conv_in, 0, half))
    for place, (low, high) in enumerate(places):
        put(mine_rows, place, jnp.where(core[0] == 0, low, high))
        put(their_rows, place, jnp.where(core[0] == 0, high, low))
    put(mine_rows, 8, small)
    put(their_rows, 8, small)
    for block in range(2):
        columns = slice(block * LANES, (block + 1) * LANES)
        put(mine_rows, 9 + block, out[:, columns])
        put(mine_rows, 11 + block, conv_out[:, columns])
        for part in range(4):
            put(mine_rows, 13 + block * 4 + part, ffn_out[6 * part : 6 * part + 6, columns])
    mine[...] = mine_rows[...].astype(BF)
    theirs[...] = their_rows[...].astype(BF)


def line_weights_kernel(info, own_rows, first, second, third, part_a, part_b, rows, lines):
    core = info[0]

    for mask, source in enumerate((own_rows, first, second, third)):
        lines[mask] = source[...].astype(F32)

    def piece(z, place):
        row = 6 * place if place < 21 else 128 + 6 * (place - 21)
        return lines[info[18] ^ z, row : row + 6, :]

    def whole(place):
        for z in range(4):
            rows[6 * z : 6 * z + 6, :] = piece(z, place)
        return rows[...]

    for block in range(3):
        part_a[0, block * 2 + core] = whole(block).astype(BF)
        part_a[0, block * 2 + 1 - core] = whole(21 + block).astype(BF)
    for block in range(2):
        part_a[0, 6 + block] = whole(9 + block).astype(BF)
        part_a[0, 11 + block] = whole(11 + block).astype(BF)
    mine = whole(8)[:, :128]
    theirs = whole(29)[:, :128]
    part_a[0, 8] = jnp.concatenate([mine, theirs, jnp.zeros_like(mine)], axis=1).astype(BF)
    part_a[0, 9 + core] = whole(7).astype(BF)
    part_a[0, 10 - core] = whole(28).astype(BF)
    for block in range(4):
        part_b[0, block * 2 + core] = whole(3 + block).astype(BF)
        part_b[0, block * 2 + 1 - core] = whole(24 + block).astype(BF)
    for z in range(4):
        for block in range(2):
            for part in range(4):
                rows[6 * part : 6 * part + 6, :] = piece(z, 13 + block * 4 + part)
            if z < 3:
                part_b[0, 8 + z * 2 + block] = rows[...].astype(BF)
            else:
                part_a[0, 13 + block] = rows[...].astype(BF)


def send_sums_kernel(
    info, a_kept, a_came, b_kept, b_came, kept, first, second, third, ffn_out, rows, lines
):
    core = info[0]
    lines[:, 120:128, :] = jnp.zeros((4, 8, LANES), F32)

    def spread(near, came, place, block):
        rows[...] = near[0, place].astype(F32) + came[0, place].astype(F32)
        pieces = [rows[6 * z : 6 * z + 6, :] for z in range(4)]
        for mask in range(4):
            z = info[18] ^ mask
            low = jnp.where(z % 2 == 0, pieces[0], pieces[1])
            high = jnp.where(z % 2 == 0, pieces[2], pieces[3])
            lines[mask, 6 * block : 6 * block + 6, :] = jnp.where(z < 2, low, high)

    for side, place in ((core, 0), (1 - core, 13)):
        for block in range(3):
            spread(a_kept, a_came, block * 2 + side, place + block)
        for block in range(5):
            spread(b_kept, b_came, block * 2 + side, place + 3 + block)
    spread(a_kept, a_came, 8, 8)
    for block in range(2):
        spread(a_kept, a_came, 6 + block, 9 + block)
        spread(b_kept, b_came, 10 + block, 11 + block)
        ffn_out[:, block * LANES : (block + 1) * LANES] = (
            b_kept[0, 12 + block].astype(F32) + b_came[0, 12 + block].astype(F32)
        )
    for mask, target in enumerate((kept, first, second, third)):
        target[...] = lines[mask].astype(BF)


def join_sums_kernel(
    info, kept, first, second, third,
    held, other, out, ffn_bias, conv_taps, conv_out, biases, gains, turned, lines,
):
    pieces = [source[...].astype(F32) for source in (kept, first, second, third)]
    lines[...] = (pieces[0] + pieces[1]) + (pieces[2] + pieces[3])

    def total(place):
        return lines[6 * place : 6 * place + 6, :]

    for place in range(8):
        held[place] = total(place)
        other[place] = total(13 + place).astype(BF)
    for block in range(2):
        columns = slice(block * LANES, (block + 1) * LANES)
        out[:, columns] = total(9 + block)
        conv_out[:, columns] = total(11 + block)
    turned[...] = jnp.zeros_like(turned)
    turned[0:6, :] = total(8)[:, :128]
    biases[...] = turned[0:6, 0:9]
    conv_taps[...] = turned[0:6, 12:27]
    small = jnp.transpose(turned[...])
    gains[...] = small[9:12, 0:6]
    for i in range(4):
        ffn_bias[0:1, 6 * i : 6 * i + 6] = small[27 + i : 28 + i, 0:6]


def shares_kernel(info, held, came, qkv, ffn_in, conv_in):
    width = conv_in.shape[1]
    half, wide = width // 2, ffn_in.shape[1] // 2

    def put(target, first, apart, place):
        own_columns, other = held[place], came[place].astype(F32)
        target[:, first : first + LANES] = jnp.where(info[0] == 0, own_columns, other)
        target[:, first + apart : first + apart + LANES] = jnp.where(info[0] == 0, other, own_columns)

    for third in range(3):
        put(qkv, third * width, half, third)
    for block in range(4):
        put(ffn_in, block * LANES, wide, 3 + block)
    put(conv_in, 0, half, 7)


def erf_parts(operand):
    cumulative = 0.5 * (1.0 + lax.erf(operand * (0.5**0.5)))
    density = jnp.exp(-0.5 * operand * operand) * (0.5 / math.pi) ** 0.5
    return (cumulative, density)


def dot(left_side, right_side, left_dim=1, right_dim=0):
    return lax.dot_general(
        left_side, right_side, (((left_dim,), (right_dim,)), ((), ())), preferred_element_type=F32
    )


def normed(residual):
    centered = residual - jnp.mean(residual, axis=-1, keepdims=True)
    inverse = lax.rsqrt(jnp.mean(centered * centered, axis=-1, keepdims=True) + EPSILON)
    return (centered * inverse, inverse)


def normed_back(grad, norm, inverse, gain_row):
    scaled = grad * gain_row
    return inverse * (
        scaled
        - jnp.mean(scaled, axis=-1, keepdims=True)
        - norm * jnp.mean(scaled * norm, axis=-1, keepdims=True)
    )


def each(count, size, body):
    def step(index, unused):
        body(pl.ds(pl.multiple_of(index * size, size), size))
        return unused

    lax.fori_loop(0, count, step, 0)


def slots(position, ends, batch):
    number = jnp.zeros(position.shape, jnp.int32)
    for place in range(SLOTS):
        number = number + (position >= ends[4 + SLOTS * batch + place]).astype(jnp.int32)
    return number


def attention_kernel(
    flow, info, tokens, part_a, order, qkv_w, out_w, rows, taps, ffn_bias, qkv, attended, soft, part
):
    half = out_w.shape[0]
    per_batch = soft.shape[1]
    flow.arrive()
    for x in range(4):
        there = slice(96 * x, 96 * x + 96)
        for block in range(3):
            columns = slice(block * LANES, (block + 1) * LANES)
            qkv_w[there, columns] = tall_rows(info, part_a, "yx", block * 2, x).astype(BF)
            below = slice(half + 96 * x, half + 96 * x + 96)
            qkv_w[below, columns] = tall_rows(info, part_a, "yx", block * 2 + 1, x).astype(BF)
        for block in range(2):
            columns = slice(block * LANES, (block + 1) * LANES)
            out_w[there, columns] = tall_rows(info, part_a, "yx", 6 + block, x).astype(BF)
    flow.leave(0)
    small = jnp.concatenate([tall_rows(info, part_a, "yx", 8, x) for x in range(4)], axis=0)
    mine = jnp.transpose(small[:, 0:128])
    theirs = jnp.transpose(small[:, 128:256])
    rows[...] = jnp.zeros_like(rows)
    left, right = jnp.where(info[0] == 0, mine, theirs), jnp.where(info[0] == 0, theirs, mine)
    rows[0:12, :half] = left[0:12, :]
    rows[0:12, half:] = right[0:12, :]
    rows[12:14, :half] = mine[0:2, :]
    rows[14:15, :half] = mine[6:7, :]
    taps[...] = jnp.zeros_like(taps)
    taps[0:15, :] = mine[12:27, :]
    spread = jnp.concatenate(
        [
            jnp.concatenate([mine[27 + i : 28 + i, 96 * x : 96 * x + 96] for i in range(4)], axis=1)
            for x in range(4)
        ]
        + [jnp.zeros((4, half), F32)],
        axis=0,
    )
    spread = dot(spread.astype(BF), order[...])
    for x in range(4):
        ffn_bias[0:1, x * LANES : (x + 1) * LANES] = spread[x : x + 1, :]
    for third in range(3):
        columns = slice(third * half, (third + 1) * half)
        block = dot(tokens[...], qkv_w[:, columns])
        if third != 1:
            block = block + rows[12 + third // 2 : 13 + third // 2, :half]
        qkv[:, columns] = block.astype(BF)
    square = (per_batch, per_batch)
    down = lax.broadcasted_iota(jnp.int32, square, 0)
    across = lax.broadcasted_iota(jnp.int32, square, 1)
    lane = lax.broadcasted_iota(jnp.int32, (per_batch, 128), 1)
    pairs = half // 128
    for batch in range(tokens.shape[0] // per_batch):
        there = slice(batch * per_batch, (batch + 1) * per_batch)
        slot_down, slot_across = slots(down, info, batch), slots(across, info, batch)
        allowed = (slot_down == slot_across) & ((slot_across < SLOTS - 1) | (down == across))
        forbidden = jnp.where(allowed, 0.0, -1e9)
        for pair in range(pairs):
            columns = slice(pair * 128, (pair + 1) * 128)
            query = qkv[there, columns]
            key = qkv[there, half + pair * 128 : half + (pair + 1) * 128]
            value = qkv[there, 2 * half + pair * 128 : 2 * half + (pair + 1) * 128]
            result = jnp.zeros((per_batch, 128), F32)
            for side in range(2):
                mine = (lane >= HEAD_DIM) if side else (lane < HEAD_DIM)
                scores = dot(jnp.where(mine, query, jnp.zeros_like(query)), key, 1, 1)
                scores = scores * HEAD_DIM ** (-0.5) + forbidden
                exponent = jnp.exp(scores - jnp.max(scores, axis=-1, keepdims=True))
                weight = (exponent * (1.0 / jnp.sum(exponent, axis=-1, keepdims=True))).astype(BF)
                soft[(batch * pairs + pair) * 2 + side] = weight
                result = result + dot(weight, jnp.where(mine, value, jnp.zeros_like(value)))
            attended[there, columns] = result.astype(BF)
    flow.leave(5, 6, 7)
    part[...] = dot(attended[...], out_w[...]).astype(BF)


def feed_kernel(
    flow, info, tokens, mine, theirs, rows, part_b, part_a, ffn_bias,
    ffn_in, ffn_out, conv_in, conv_out, hidden, norm, inverse, activated, slope, part,
):
    half = conv_in.shape[1]

    def first(there):
        residual = (
            tokens[there, :].astype(F32)
            + (mine[there, :].astype(F32) + theirs[there, :].astype(F32))
            + rows[2:3, :]
        )
        unit, scale = normed(residual)
        norm[there, :] = unit
        inverse[there, :] = jnp.broadcast_to(scale, (scale.shape[0], 128))
        hidden[there, :] = (unit * rows[9:10, :] + rows[3:4, :]).astype(BF)

    each(tokens.shape[0] // 64, 64, first)
    flow.leave(5, 6)
    flow.arrive(5, 6)
    for x in range(4):
        for side in range(2):
            there = slice(half * side + 96 * x, half * side + 96 * x + 96)
            for block in range(4):
                columns = slice(block * LANES, (block + 1) * LANES)
                ffn_in[there, columns] = tall_rows(info, part_b, "xy", block * 2 + side, x).astype(BF)
            conv_in[there, :] = tall_rows(info, part_a, "yx", side, x).astype(BF)
        for block in range(2):
            columns = slice(block * LANES, (block + 1) * LANES)
            conv_out[96 * x : 96 * x + 96, columns] = tall_rows(info, part_a, "yx", 2 + block, x).astype(BF)
    flow.leave(0)
    wide = ffn_in.shape[1]
    chunk = 256

    def second(index, unused):
        columns = pl.ds(pl.multiple_of(index * chunk, chunk), chunk)
        up = dot(hidden[...], ffn_in[:, columns]) + ffn_bias[0:1, columns]
        cumulative, density = erf_parts(up)
        activated[:, columns] = (up * cumulative).astype(BF)
        slope[:, columns] = (cumulative + up * density).astype(BF)
        return unused

    lax.fori_loop(0, wide // chunk, second, 0)
    flow.leave(7, 8)
    for x in range(4):
        for y in range(4):
            for block in range(2):
                indices = {"x": index_at(info, "x", x), "y": index_at(info, "y", y)}
                place = outer_inner("xy", indices)
                pieces = [part_b[place, 8 + z * 2 + block].astype(F32) for z in range(3)]
                pieces.append(part_a[outer_inner("yx", indices), 4 + block].astype(F32))
                row = 384 * x + 96 * y
                ffn_out[row : row + 96, block * LANES : (block + 1) * LANES] = jnp.concatenate(
                    pieces, axis=0
                ).astype(BF)
    flow.leave(1)
    part[...] = dot(activated[...], ffn_out[...]).astype(BF)


def tap_row(taps, info, batch, offset):
    choice = info[1 + batch]
    row = taps[11 + offset : 12 + offset, :]
    row = jnp.where(choice == 1, taps[5 + offset : 6 + offset, :] if abs(offset) < 3 else 0.0, row)
    return jnp.where(choice == 0, taps[1 + offset : 2 + offset, :] if abs(offset) < 2 else 0.0, row)


def fill_slots(info, padded, per_batch, batches):
    position = lax.broadcasted_iota(jnp.int32, (per_batch, 128), 0)
    outside = jnp.full((8, 128), -1, jnp.int32)
    for batch in range(batches):
        padded[batch, 0:8, :] = outside
        padded[batch, 8 : 8 + per_batch, :] = slots(position, info, batch)
        padded[batch, 8 + per_batch :, :] = outside


def clear_edges(padded, per_batch, batches):
    edge = jnp.zeros((8, padded.shape[2]), F32)
    for batch in range(batches):
        padded[batch, 0:8, :] = edge
        padded[batch, 8 + per_batch :, :] = edge


def convolution_kernel(
    flow, info, hidden, mine, theirs, rows, conv_in, taps, conv_out,
    phase_one, norm, inverse, mixed, gated, slope, part, slot_pad, mixed_pad,
):
    batches = slot_pad.shape[0]
    per_batch = hidden.shape[0] // batches
    half = conv_in.shape[1]

    def first(there):
        residual = (
            hidden[there, :].astype(F32)
            + (mine[there, :].astype(F32) + theirs[there, :].astype(F32))
            + rows[4:5, :]
        )
        unit, scale = normed(residual)
        norm[there, :] = unit
        inverse[there, :] = jnp.broadcast_to(scale, (scale.shape[0], 128))
        phase_one[there, :] = (unit * rows[10:11, :] + rows[5:6, :]).astype(BF)

    each(hidden.shape[0] // 64, 64, first)
    flow.leave(1, 2)
    fill_slots(info, slot_pad, per_batch, batches)
    clear_edges(mixed_pad, per_batch, batches)
    mixed[...] = dot(phase_one[...], conv_in[...]) + rows[14:15, :half]
    for batch in range(batches):
        there = slice(batch * per_batch, (batch + 1) * per_batch)
        mixed_pad[batch, 8 : 8 + per_batch, :] = mixed[there, :]
        for column in range(half // 128):
            columns = slice(column * 128, (column + 1) * 128)
            here = slot_pad[batch, 8 : 8 + per_batch, :]
            total = jnp.zeros((per_batch, 128), F32)
            for offset in range(-3, 4):
                same = slot_pad[batch, 8 + offset : 8 + offset + per_batch, :] == here
                moved = mixed_pad[batch, 8 + offset : 8 + offset + per_batch, columns]
                tap = tap_row(taps, info, batch, offset)[:, columns]
                total = total + jnp.where(same, moved, 0.0) * tap
            cumulative, density = erf_parts(total)
            gated[there, columns] = (total * cumulative).astype(BF)
            slope[there, columns] = cumulative + total * density
    part[...] = dot(gated[...], conv_out[...]).astype(BF)


def own(info, row):
    half = row.shape[1] // 2
    return jnp.where(info[0] == 0, row[:, :half], row[:, half:])


def convolution_back_kernel(
    flow, info, phase_one, mine, theirs, cotangent, rows, conv_in, taps, conv_out, mixed, gated, slope,
    result, grad_three, grad_low, grad_mixed, part, sums, d_taps,
    slot_pad, mixed_pad, grad_pad, wide_sums,
):
    batches = slot_pad.shape[0]
    per_batch = phase_one.shape[0] // batches
    half = conv_in.shape[1]
    fill_slots(info, slot_pad, per_batch, batches)
    clear_edges(mixed_pad, per_batch, batches)
    clear_edges(grad_pad, per_batch, batches)
    wide_sums[...] = jnp.zeros_like(wide_sums)
    flow.arrive()
    size = 64
    for batch in range(batches):

        def first(index, unused):
            inner = pl.multiple_of(index * size, size)
            there = pl.ds(pl.multiple_of(batch * per_batch + inner, size), size)
            residual = (
                phase_one[there, :].astype(F32)
                + (mine[there, :].astype(F32) + theirs[there, :].astype(F32))
                + rows[7:8, :]
            )
            unit, scale = normed(residual)
            ended = (unit * rows[11:12, :] + rows[8:9, :]).astype(BF)
            result[there, :] = jnp.where(info[0] == 0, phase_one[there, :], ended)
            valid = slot_pad[batch, pl.ds(pl.multiple_of(8 + inner, 8), size), :][:, :1] < SLOTS - 1
            masked = jnp.where(valid, cotangent[there, :].astype(F32), 0.0)
            grad = normed_back(masked, unit, scale, rows[11:12, :])
            grad_three[there, :] = grad
            low = grad.astype(BF)
            grad_low[there, :] = low
            wide_sums[0:1, :] += jnp.sum(low.astype(F32), axis=0, keepdims=True)
            wide_sums[1:2, :] += jnp.sum(masked, axis=0, keepdims=True)
            wide_sums[2:3, :] += jnp.sum(masked * unit, axis=0, keepdims=True)
            return unused

        lax.fori_loop(0, per_batch // size, first, 0)
    flow.leave(0)
    tap_sums = [[[] for offset in range(7)] for batch in range(batches)]
    for batch in range(batches):
        there = slice(batch * per_batch, (batch + 1) * per_batch)
        grad_pad[batch, 8 : 8 + per_batch, :] = (
            dot(grad_low[there, :], conv_out[...], 1, 1) * slope[there, :]
        )
        mixed_pad[batch, 8 : 8 + per_batch, :] = mixed[there, :]
        for column in range(half // 128):
            columns = slice(column * 128, (column + 1) * 128)
            here = slot_pad[batch, 8 : 8 + per_batch, :]
            grad = grad_pad[batch, 8 : 8 + per_batch, columns]
            total = jnp.zeros((per_batch, 128), F32)
            for offset in range(-3, 4):
                away = slice(8 + offset, 8 + offset + per_batch)
                same = slot_pad[batch, away, :] == here
                tap = tap_row(taps, info, batch, -offset)[:, columns]
                total = total + jnp.where(same, grad_pad[batch, away, columns], 0.0) * tap
                term = jnp.where(same, mixed_pad[batch, away, columns], 0.0) * grad
                tap_sums[batch][offset + 3].append(jnp.sum(term, axis=0, keepdims=True))
            grad_mixed[there, columns] = total.astype(BF)
    for choice in range(3):
        for offset in range(-choice - 1, choice + 2):
            row = choice * choice + 2 * choice + offset + choice + 1
            total = jnp.zeros((1, half), F32)
            for batch in range(batches):
                joined = jnp.concatenate(tap_sums[batch][offset + 3], axis=1)
                total = total + jnp.where(info[1 + batch] == choice, joined, 0.0)
            d_taps[row : row + 1, :] = total
    d_taps[15:16, :] = jnp.zeros((1, half), F32)
    part[...] = dot(grad_mixed[...], conv_in[...], 1, 1).astype(BF)
    sums[0:1, :] = jnp.sum(grad_mixed[...].astype(F32), axis=0, keepdims=True)
    for place in range(3):
        sums[place + 1 : place + 2, :] = own(info, wide_sums[place : place + 1, :])
    sums[4:8, :] = jnp.zeros((4, half), F32)


def convolution_sums_kernel(info, phase_one, gated, grad_low, grad_mixed, kept, sent, whole):
    half = gated.shape[1]
    for block in range(2):
        columns = slice(block * LANES, (block + 1) * LANES)
        whole[0:half, :] = dot(gated[...], grad_low[:, columns], 0, 0)
        pack_rows(info, whole, "xy", 2 + block, kept, sent, 0)
    whole[...] = dot(phase_one[...], grad_mixed[...], 0, 0)
    for side in range(2):
        pack_rows(info, whole, "xy", side, kept, sent, side * half)


def feed_back_kernel(
    flow, info, grad_three, mine, theirs, norm, inverse, rows, activated, slope, hidden, ffn_in, ffn_out,
    conv_kept, conv_sent,
    grad_phase_one, grad_two, b_kept, b_sent, c_kept, c_sent, part, sums, bias_sums,
    grad_low, grad_up, wide_sums, whole,
):
    wide_sums[...] = jnp.zeros_like(wide_sums)
    flow.arrive(4, 5)

    def first(there):
        arriving = grad_three[there, :] + (mine[there, :].astype(F32) + theirs[there, :].astype(F32))
        arriving = arriving.astype(BF)
        grad_phase_one[there, :] = arriving
        arriving = arriving.astype(F32)
        unit = norm[there, :]
        grad = normed_back(arriving, unit, inverse[there, :1], rows[10:11, :])
        grad_two[there, :] = grad
        low = grad.astype(BF)
        grad_low[there, :] = low
        wide_sums[0:1, :] += jnp.sum(low.astype(F32), axis=0, keepdims=True)
        wide_sums[1:2, :] += jnp.sum(arriving, axis=0, keepdims=True)
        wide_sums[2:3, :] += jnp.sum(arriving * unit, axis=0, keepdims=True)

    each(hidden.shape[0] // 64, 64, first)
    flow.leave(0)
    flow.arrive(7, 8, 10, 11)
    half = ffn_in.shape[0] // 2
    for block in range(ffn_in.shape[1] // LANES):
        columns = slice(block * LANES, (block + 1) * LANES)
        grad = dot(grad_low[...], ffn_out[columns, :], 1, 1) * slope[:, columns].astype(F32)
        low = grad.astype(BF)
        grad_up[:, columns] = low
        bias_sums[0:1, columns] = jnp.sum(low.astype(F32), axis=0, keepdims=True)
        whole[...] = dot(hidden[...], low, 0, 0)
        for side in range(2):
            pack_rows(info, whole, "xy", block * 2 + side, b_kept, b_sent, side * half)
    for place in range(8):
        for block in range(4):
            b_kept[place, 8 + block] = conv_kept[place, block]
            b_sent[place, 8 + block] = conv_sent[place, block]
    for step in range(4):
        x = coordinate_at(info, "x", step)
        there = pl.ds(pl.multiple_of(x * 384, 128), 384)
        for block in range(2):
            columns = slice(block * LANES, (block + 1) * LANES)
            whole[0:384, :] = dot(activated[:, there], grad_low[:, columns], 0, 0)
            for outer in range(4):
                for inner in range(4):
                    z, y = coordinate_at(info, "z", outer), coordinate_at(info, "y", inner)
                    piece = whole[pl.ds(pl.multiple_of(96 * y + 24 * z, 8), 24), :].astype(BF)
                    place = ((outer % 2) * 4 + step) * 4 + inner
                    (c_kept if outer < 2 else c_sent)[place, block] = piece
    part[...] = dot(grad_up[...], ffn_in[...], 1, 1).astype(BF)
    for place in range(3):
        sums[place : place + 1, :] = own(info, wide_sums[place : place + 1, :])
    sums[3:8, :] = jnp.zeros((5, sums.shape[1]), F32)


def attention_back_kernel(
    flow, info, grad_two, mine, theirs, norm, inverse, rows, tokens, qkv, attended, soft, out_w,
    sums_two, sums_three, d_taps, bias_sums, order,
    grad_one, kept, sent, grad_qkv, grad_low, grad_attended, wide_sums, whole, sums,
):
    flow.arrive(4, 5)
    half = out_w.shape[0]
    per_batch = soft.shape[1]
    wide_sums[...] = jnp.zeros_like(wide_sums)

    def first(there):
        arriving = grad_two[there, :] + (mine[there, :].astype(F32) + theirs[there, :].astype(F32))
        unit = norm[there, :]
        grad = normed_back(arriving, unit, inverse[there, :1], rows[9:10, :])
        grad_one[there, :] = grad
        low = grad.astype(BF)
        grad_low[there, :] = low
        wide_sums[0:1, :] += jnp.sum(low.astype(F32), axis=0, keepdims=True)
        wide_sums[1:2, :] += jnp.sum(arriving, axis=0, keepdims=True)
        wide_sums[2:3, :] += jnp.sum(arriving * unit, axis=0, keepdims=True)

    each(tokens.shape[0] // 64, 64, first)
    flow.leave(0)
    flow.arrive(7, 8, 9, 10)
    for block in range(2):
        columns = slice(block * LANES, (block + 1) * LANES)
        whole[0:half, :] = dot(attended[...], grad_low[:, columns], 0, 0)
        pack_rows(info, whole, "yx", 6 + block, kept, sent, 0)
    grad_attended[...] = dot(grad_low[...], out_w[...], 1, 1).astype(BF)
    lane = lax.broadcasted_iota(jnp.int32, (per_batch, 128), 1)
    pairs = half // 128
    scale = HEAD_DIM ** (-0.5)
    for batch in range(tokens.shape[0] // per_batch):
        there = slice(batch * per_batch, (batch + 1) * per_batch)
        for pair in range(pairs):
            columns = [
                slice(third * half + pair * 128, third * half + (pair + 1) * 128) for third in range(3)
            ]
            query, key, value = (qkv[there, columns[third]] for third in range(3))
            grad = grad_attended[there, columns[0]]
            totals = [jnp.zeros((per_batch, 128), F32) for third in range(3)]
            for side in range(2):
                mine_lanes = (lane >= HEAD_DIM) if side else (lane < HEAD_DIM)

                def only(operand):
                    return jnp.where(mine_lanes, operand, jnp.zeros_like(operand))

                weight = soft[(batch * pairs + pair) * 2 + side]
                grad_side = only(grad)
                grad_soft = dot(grad_side, value, 1, 1)
                weight_wide = weight.astype(F32)
                inner = jnp.sum(grad_soft * weight_wide, axis=-1, keepdims=True)
                grad_scores = (weight_wide * (grad_soft - inner)).astype(BF)
                totals[0] = totals[0] + dot(grad_scores, only(key))
                totals[1] = totals[1] + dot(grad_scores, only(query), 0, 0)
                totals[2] = totals[2] + dot(weight, grad_side, 0, 0)
            grad_qkv[there, columns[0]] = (totals[0] * scale).astype(BF)
            grad_qkv[there, columns[1]] = (totals[1] * scale).astype(BF)
            grad_qkv[there, columns[2]] = totals[2].astype(BF)
    sums[...] = jnp.zeros_like(sums)
    for third in range(3):
        columns = slice(third * half, (third + 1) * half)
        whole[...] = dot(tokens[...], grad_qkv[:, columns], 0, 0)
        for side in range(2):
            pack_rows(info, whole, "yx", third * 2 + side, kept, sent, side * half)
        if third != 1:
            place = third // 2
            sums[place : place + 1, :] = jnp.sum(
                grad_qkv[:, columns].astype(F32), axis=0, keepdims=True
            )
    sums[2:3, :] = own(info, wide_sums[0:1, :])
    sums[3:4, :] = own(info, wide_sums[1:2, :])
    sums[4:6, :] = sums_two[0:2, :]
    sums[6:9, :] = sums_three[0:3, :]
    sums[9:10, :] = own(info, wide_sums[2:3, :])
    sums[10:11, :] = sums_two[2:3, :]
    sums[11:12, :] = sums_three[3:4, :]
    sums[12:27, :] = d_taps[0:15, :]
    spread = jnp.concatenate(
        [bias_sums[0:1, x * LANES : (x + 1) * LANES] for x in range(4)] + [jnp.zeros((4, half), F32)], axis=0
    )
    spread = dot(spread.astype(BF), order[...], 1, 1)
    for i in range(4):
        sums[27 + i : 28 + i, :] = jnp.concatenate(
            [spread[x : x + 1, 96 * i : 96 * i + 96] for x in range(4)], axis=1
        )
    whole[0:half, :] = jnp.zeros((half, LANES), F32)
    whole[0:half, 0:128] = jnp.transpose(sums[...])
    pack_rows(info, whole, "yx", 8, kept, sent, 0)


def tokens_back_kernel(flow, grad_qkv, qkv_w, part):
    flow.arrive()
    part[...] = dot(grad_qkv[...], qkv_w[...], 1, 1).astype(BF)


class Flow:
    def __init__(self):
        self.coming, self.going = {}, {}

    def arrive(self, *chosen):
        for which in chosen or tuple(self.coming):
            for copy in self.coming[which]:
                copy.wait()

    def leave(self, *chosen):
        for which in chosen:
            self.going[which].start()


def kernel_call(body, outputs, scratch, has_info, *operands, late=(), early=(), mib=4, gflop=0):
    vmem = pl.BlockSpec(memory_space=pltpu.VMEM)
    smem = pl.BlockSpec(memory_space=pltpu.SMEM)
    hbm = pl.BlockSpec(memory_space=pltpu.HBM)
    groups = [operand if isinstance(operand, tuple) else (operand,) for operand in operands]
    arrays = [array for group in groups for array in group]
    moves = sum(len(groups[which]) for which in late) + len(early)

    def with_copies(*refs):
        taken = 0
        operand_refs = []
        for group in groups:
            operand_refs.append(refs[taken : taken + len(group)])
            taken += len(group)
        output_refs = list(refs[taken : taken + len(outputs)])
        own = refs[taken + len(outputs) : taken + len(outputs) + len(scratch)]
        buffers = list(refs[taken + len(outputs) + len(scratch) : -1])
        flags, used = refs[-1], 0
        flow = Flow()
        for which in late:
            buffer = buffers.pop(0)
            first, flow.coming[which] = 0, []
            for source in operand_refs[which]:
                count = source.shape[0]
                target = buffer if len(groups[which]) == 1 else buffer.at[pl.ds(first, count)]
                copy = pltpu.make_async_copy(source, target, flags.at[used])
                copy.start()
                flow.coming[which].append(copy)
                first, used = first + count, used + 1
            operand_refs[which] = (buffer,)
        for which in early:
            buffer = buffers.pop(0)
            flow.going[which] = pltpu.make_async_copy(buffer, output_refs[which], flags.at[used])
            output_refs[which] = buffer
            used += 1
        body(flow, *(group[0] for group in operand_refs), *output_refs, *own)
        for which in early:
            flow.going[which].wait()

    specs = [smem if has_info and place == 0 else vmem for place in range(len(operands))]
    out_specs = [vmem] * len(outputs)
    memory = [pltpu.VMEM(shape, dtype) for shape, dtype in scratch]
    for which in late:
        specs[which] = hbm
        whole = sum(array.shape[0] for array in groups[which])
        memory.append(pltpu.VMEM((whole, *groups[which][0].shape[1:]), groups[which][0].dtype))
    for which in early:
        out_specs[which] = hbm
        memory.append(pltpu.VMEM(*outputs[which]))
    if moves:
        memory.append(pltpu.SemaphoreType.DMA((moves,)))
    return pl.pallas_call(
        with_copies if moves else body,
        out_shape=[jax.ShapeDtypeStruct(shape, dtype) for shape, dtype in outputs],
        in_specs=[spec for spec, group in zip(specs, groups) for array in group],
        out_specs=out_specs,
        scratch_shapes=memory,
        compiler_params=pltpu.CompilerParams(vmem_limit_bytes=mib * 1024 * 1024),
        cost_estimate=pl.CostEstimate(flops=int(gflop * 1e9), bytes_accessed=1 << 20, transcendentals=0),
    )(*arrays)


def gather_weights(info, masters):
    (qkv, out, ffn_in, ffn_bias, ffn_out, conv_in, conv_taps, conv_out, biases, gains) = masters
    mine, theirs = kernel_call(
        send_weights_kernel,
        [((128, LANES), BF), ((56, LANES), BF)],
        [((128, 128), F32), ((128, LANES), F32), ((56, LANES), F32)],
        True,
        lax.axis_index("phase").astype(jnp.int32).reshape(1), qkv, out, ffn_in, ffn_bias.reshape(1, -1), ffn_out,
        conv_in, conv_taps.T, conv_out, biases.T, gains,
        late=tuple(range(1, 11)),
        mib=60,
    )

    def together(*values):
        return lax.optimization_barrier(values)

    line = jnp.concatenate([mine, swap(theirs)])
    part_a, part_b = kernel_call(
        line_weights_kernel,
        [((1, 15, 24, LANES), BF), ((1, 14, 24, LANES), BF)],
        [((24, LANES), F32), ((4, 184, LANES), F32)],
        True,
        info, line, *(lax.ppermute(line, BOTH, across(mask)) for mask in (1, 2, 3)),
    )
    for step in range(2):
        part_a, part_b = together(grown(part_a, "x", step), grown(part_b, "y", step))
    came = lax.ppermute(part_a, BOTH, partners("y", 0))
    early, late, part_b = together(
        jnp.concatenate([part_a[:, :9], came[:, :9]]),
        jnp.concatenate([part_a[:, 9:], came[:, 9:]]),
        grown(part_b, "x", 0),
    )
    return (
        (early, lax.ppermute(early, BOTH, partners("y", 1))),
        (late, lax.ppermute(late, BOTH, partners("y", 1))),
        (part_b, lax.ppermute(part_b, BOTH, partners("x", 1))),
    )


def shards(
    tokens,
    cotangent,
    lengths,
    kernel_choice,
    *masters,
):
    batches = lengths.shape[0]
    rows, width = tokens.shape
    per_batch = rows // batches
    half = width // 2
    wide = masters[2].shape[1] // 2
    heads = half // HEAD_DIM
    info = info_of(lengths, kernel_choice)
    part_a, rest, part_b = gather_weights(info, masters)
    order = bias_order()
    low, full = ((rows, width), BF), ((rows, width), F32)
    narrow = ((rows, 128), F32)
    slot_pad = ((batches, per_batch + 16, 128), jnp.int32)
    row_pad = ((batches, per_batch + 16, half), F32)
    whole = ((width, LANES), F32)

    def halves(blocks):
        return [((8, blocks, 24, LANES), BF)] * 2

    qkv_w, out_w, all_rows, taps, ffn_bias, qkv, attended, soft, part = kernel_call(
        attention_kernel,
        [
            ((width, 3 * half), BF), ((half, width), BF), ((16, width), F32),
            ((16, half), F32), ((1, wide), F32), ((rows, 3 * half), BF), ((rows, half), BF),
            ((batches * heads, per_batch, per_batch), BF), low,
        ],
        [],
        True,
        info, tokens, part_a, order,
        late=(2,),
        early=(0, 5, 6, 7),
        gflop=5,
        mib=16,
    )
    ffn_in, ffn_out, conv_in, conv_out, hidden, norm_one, inverse_one, activated, slope_up, part_two = kernel_call(
        feed_kernel,
        [
            ((width, wide), BF), ((wide, width), BF), ((width, half), BF), ((half, width), BF), low, full, narrow, ((rows, wide), BF), ((rows, wide), BF), low,
        ],
        [],
        True,
        info, tokens, part, swap(part), all_rows, part_b, rest, ffn_bias,
        late=(5, 6),
        early=(0, 1, 5, 6, 7, 8),
        gflop=8,
        mib=24,
    )
    phase_one, norm_two, inverse_two, mixed, gated, slope, part_three = kernel_call(
        convolution_kernel,
        [low, full, narrow, ((rows, half), F32), ((rows, half), BF), ((rows, half), F32), low],
        [slot_pad, row_pad],
        True,
        info, hidden, part_two, swap(part_two), all_rows, conv_in, taps, conv_out,
        early=(1, 2),
        gflop=4,
        mib=8,
    )
    block_outputs, grad_three, grad_low, grad_mixed, part, sums_three, d_taps = kernel_call(
        convolution_back_kernel,
        [low, full, low, ((rows, half), BF), low, ((8, half), F32), ((16, half), F32)],
        [slot_pad, row_pad, row_pad, ((8, width), F32)],
        True,
        info, phase_one, part_three, swap(part_three), cotangent, all_rows, conv_in, taps, conv_out,
        mixed, gated, slope,
        late=(4,),
        early=(0,),
        gflop=8,
        mib=10,
    )
    conv_kept, conv_sent = kernel_call(
        convolution_sums_kernel,
        halves(4),
        [whole],
        True,
        info, phase_one, gated, grad_low, grad_mixed,
        gflop=2,
        mib=6,
    )
    grad_phase_one, grad_two, b_kept, b_sent, c_kept, c_sent, part, sums_two, d_ffn_bias = kernel_call(
        feed_back_kernel,
        [
            low, full, *halves(12), ((32, 2, 24, LANES), BF), ((32, 2, 24, LANES), BF), low,
            ((8, half), F32), ((1, wide), F32),
        ],
        [low, ((rows, wide), BF), ((8, width), F32), whole],
        True,
        info, grad_three, part, swap(part), norm_two, inverse_two, all_rows, activated, slope_up, hidden,
        ffn_in, ffn_out, conv_kept, conv_sent,
        late=(4, 5, 7, 8, 10, 11),
        early=(0,),
        gflop=10,
        mib=20,
    )
    grad_one, a_kept, a_sent, grad_qkv = kernel_call(
        attention_back_kernel,
        [full, *halves(9), ((rows, 3 * half), BF)],
        [low, ((rows, half), BF), ((8, width), F32), whole, ((128, half), F32)],
        True,
        info, grad_two, part, swap(part), norm_one, inverse_one, all_rows, tokens, qkv, attended, soft,
        out_w, sums_two, sums_three, d_taps, d_ffn_bias, order,
        late=(4, 5, 7, 8, 9, 10),
        early=(0,),
        gflop=10,
        mib=20,
    )
    (part,) = kernel_call(
        tokens_back_kernel, [low], [], False, grad_qkv, qkv_w, late=(1,), gflop=1, mib=8
    )
    theirs = lax.ppermute(part, "phase", [(1, 0)])
    b_kept, b_sent = halved(b_kept, exchanged(b_sent, "x", 1))
    c_kept, c_sent = halved(c_kept, exchanged(c_sent, "z", 1))
    a_kept, a_sent = halved(after(a_kept, b_sent, c_sent, theirs), exchanged(a_sent, "y", 1))
    b_came = exchanged(b_sent, "x", 0)
    c_kept, c_sent = halved(after(c_kept, b_sent), exchanged(c_sent, "z", 0))
    c_kept, c_sent = halved(c_kept, exchanged(c_sent, "x", 1))
    a_kept, a_sent = halved(after(a_kept, b_came, c_sent), exchanged(a_sent, "y", 0))
    b_kept, b_sent = halved(after(b_kept, a_sent), b_came)
    c_kept, c_sent = halved(c_kept, exchanged(c_sent, "x", 0))
    b_kept, b_sent = (jnp.concatenate(pair, axis=1) for pair in ((b_kept, c_kept), (b_sent, c_sent)))
    b_came = exchanged(b_sent, "y", 1)
    a_kept, a_sent = halved(a_kept, exchanged(a_sent, "x", 1))
    b_kept, b_sent = halved(after(b_kept, a_sent), b_came)
    *pieces, ffn_out_share = kernel_call(
        send_sums_kernel,
        [*[((128, LANES), BF)] * 4, (masters[4].shape, F32)],
        [((24, LANES), F32), ((4, 128, LANES), F32)],
        True,
        info, a_kept, exchanged(a_sent, "x", 0), b_kept, exchanged(b_sent, "y", 0),
    )
    grad_one = after(grad_one, pieces[1])
    shapes = [master.shape for master in masters]
    shapes[3] = (1, shapes[3][0])
    for turned in (6, 8):
        shapes[turned] = shapes[turned][::-1]
    joined, swapped = (1, 3, 6, 7, 8, 9), (0, 2, 5)
    held, other, *done = kernel_call(
        join_sums_kernel,
        [((8, 6, LANES), F32), ((8, 6, LANES), BF), *((shapes[place], F32) for place in joined)],
        [((128, 128), F32), ((128, LANES), F32)],
        True,
        info, pieces[0], *(lax.ppermute(pieces[mask], BOTH, across(mask)) for mask in (1, 2, 3)),
    )
    done += kernel_call(
        shares_kernel, [(shapes[place], F32) for place in swapped], [], True, info, held, swap(other)
    )
    shares = dict(zip(joined + swapped, done))
    shares[4] = ffn_out_share
    shares[3] = shares[3].reshape(-1)
    for turned in (6, 8):
        shares[turned] = shares[turned].T
    shares = [shares[place] for place in range(10)]
    grad_tokens = (grad_one + (part.astype(F32) + theirs.astype(F32))).astype(BF)
    input_grads = jnp.where(lax.axis_index("phase") == 0, grad_tokens, grad_phase_one)
    return (block_outputs[None], input_grads[None], *shares)


def solution(mesh):
    sharded, columns = P(BOTH, None), P(None, BOTH)
    weights = (sharded, sharded, sharded, P(BOTH), sharded, sharded, columns, sharded, columns, columns)
    return jax.shard_map(
        shards,
        mesh=mesh,
        in_specs=(P("dp", None), P("dp", None), P("dp", None), P("dp"), *weights),
        out_specs=(P("phase", "dp", None), P("phase", "dp", None), *weights),
        check_vma=False,
    )
```

```python
import math

import jax
import jax.numpy as jnp
import numpy as np
from jax import lax
from jax.experimental import pallas as pl
from jax.experimental.pallas import tpu as pltpu
from jax.sharding import PartitionSpec as P

HEAD_DIM = 64
EPSILON = 1e-05
BOTH = ("phase", "dp")
STRIDE = {"x": 16, "y": 4, "z": 1}
AXES = "xyz"
LANES = 384
SLOTS = 6
SWAP = [(0, 1), (1, 0)]
BF = jnp.bfloat16
F32 = jnp.float32


def partners(axis, step):
    pairs = []
    for core in range(2):
        mask = (1, 3)[(core + step) % 2]
        for chip in range(64):
            coordinate = (chip // STRIDE[axis]) % 4
            target = chip + ((coordinate ^ mask) - coordinate) * STRIDE[axis]
            pairs.append((core * 64 + chip, core * 64 + target))
    return pairs


def across(mask):
    return [(device, device + (((device % 4) ^ mask) - device % 4)) for device in range(128)]


def grown(held, axis, step):
    return jnp.concatenate([held, lax.ppermute(held, BOTH, partners(axis, step))])


def exchanged(sent, axis, step):
    return lax.ppermute(sent, BOTH, partners(axis, step))


def halved(kept, came):
    count = kept.shape[0] // 2
    return tuple(
        (kept[there].astype(F32) + came[there].astype(F32)).astype(BF)
        for there in (slice(0, count), slice(count, 2 * count))
    )


def after(value, *others):
    return lax.optimization_barrier((value, *others))[0]


def swap(part):
    return lax.ppermute(part, "phase", SWAP)


def bias_order():
    table = np.zeros((LANES, LANES), np.float32)
    for i in range(4):
        for d in range(16):
            for j in range(6):
                table[96 * i + 6 * d + j, 24 * d + 6 * i + j] = 1.0
    return jnp.asarray(table, BF)


def info_of(lengths, kernel_choice):
    core = lax.axis_index("phase").astype(jnp.int32)
    chip = lax.axis_index("dp").astype(jnp.int32)
    return jnp.concatenate(
        [
            core[None],
            kernel_choice,
            jnp.zeros((3 - kernel_choice.shape[0],), jnp.int32),
            jnp.cumsum(lengths, axis=-1).reshape(-1),
            jnp.stack([(chip // STRIDE[axis]) % 4 for axis in AXES]),
            jnp.stack([1 + 2 * core, 3 - 2 * core]),
        ]
    )


def coordinate_at(info, axis, index):
    here = info[16 + AXES.index(axis)]
    return here ^ (0, info[19], info[20], 2)[index]


def index_at(info, axis, coordinate):
    apart = info[16 + AXES.index(axis)] ^ coordinate
    return jnp.where(
        apart == 0, 0, jnp.where(apart == info[19], 1, jnp.where(apart == info[20], 2, 3))
    )


def outer_inner(order, indices):
    place = 0
    for axis in order:
        place = place * 4 + indices[axis]
    return place


def tall_rows(info, part, order, block, x):
    pieces = []
    for y in range(4):
        place = outer_inner(order, {"x": index_at(info, "x", x), "y": index_at(info, "y", y)})
        pieces.append(part[place, block].astype(F32))
    return jnp.concatenate(pieces, axis=0)


def pack_rows(info, source, order, block, kept, sent, first_row):
    for outer in range(4):
        for inner in range(4):
            place = {order[0]: coordinate_at(info, order[0], outer)}
            place[order[1]] = coordinate_at(info, order[1], inner)
            row = pl.multiple_of(first_row + 96 * place["x"] + 24 * place["y"], 8)
            piece = source[pl.ds(row, 24), :].astype(BF)
            (kept if outer < 2 else sent)[(outer % 2) * 4 + inner, block] = piece


def send_weights_kernel(
    flow, core, qkv, out, ffn_in, ffn_bias, ffn_out, conv_in, conv_taps, conv_out, biases, gains,
    mine, theirs, turned, mine_rows, their_rows,
):
    width = out.shape[1]
    half, wide = width // 2, ffn_in.shape[1] // 2
    turned[...] = jnp.zeros_like(turned)
    flow.arrive()
    turned[9:12, 0:6] = gains[...]
    for i in range(4):
        turned[27 + i : 28 + i, 0:6] = ffn_bias[0:1, 6 * i : 6 * i + 6]
    turned[0:8, :] = jnp.transpose(turned[...])[0:8, :]
    turned[0:6, 0:9] = biases[...]
    turned[0:6, 12:27] = conv_taps[...]
    small = turned[0:6, :]
    blank = jnp.zeros((6, LANES - 128), F32)
    small = jnp.concatenate([small, blank], axis=1)
    mine_rows[120:128, :] = jnp.zeros((8, LANES), F32)
    their_rows[48:56, :] = jnp.zeros((8, LANES), F32)

    def put(target, place, block):
        target[6 * place : 6 * place + 6, :] = block

    def pair(source, first, apart):
        return (source[:, first : first + LANES], source[:, first + apart : first + apart + LANES])

    places = [pair(qkv, third * width, half) for third in range(3)]
    places += [pair(ffn_in, block * LANES, wide) for block in range(4)]
    places.append(pair(conv_in, 0, half))
    for place, (low, high) in enumerate(places):
        put(mine_rows, place, jnp.where(core[0] == 0, low, high))
        put(their_rows, place, jnp.where(core[0] == 0, high, low))
    put(mine_rows, 8, small)
    put(their_rows, 8, small)
    for block in range(2):
        columns = slice(block * LANES, (block + 1) * LANES)
        put(mine_rows, 9 + block, out[:, columns])
        put(mine_rows, 11 + block, conv_out[:, columns])
        for part in range(4):
            put(mine_rows, 13 + block * 4 + part, ffn_out[6 * part : 6 * part + 6, columns])
    mine[...] = mine_rows[...].astype(BF)
    theirs[...] = their_rows[...].astype(BF)


def line_weights_kernel(info, own_rows, first, second, third, part_a, part_b, rows, lines):
    core = info[0]

    for mask, source in enumerate((own_rows, first, second, third)):
        lines[mask] = source[...].astype(F32)

    def piece(z, place):
        row = 6 * place if place < 21 else 128 + 6 * (place - 21)
        return lines[info[18] ^ z, row : row + 6, :]

    def whole(place):
        for z in range(4):
            rows[6 * z : 6 * z + 6, :] = piece(z, place)
        return rows[...]

    for block in range(3):
        part_a[0, block * 2 + core] = whole(block).astype(BF)
        part_a[0, block * 2 + 1 - core] = whole(21 + block).astype(BF)
    for block in range(2):
        part_a[0, 6 + block] = whole(9 + block).astype(BF)
        part_a[0, 11 + block] = whole(11 + block).astype(BF)
    mine = whole(8)[:, :128]
    theirs = whole(29)[:, :128]
    part_a[0, 8] = jnp.concatenate([mine, theirs, jnp.zeros_like(mine)], axis=1).astype(BF)
    part_a[0, 9 + core] = whole(7).astype(BF)
    part_a[0, 10 - core] = whole(28).astype(BF)
    for block in range(4):
        part_b[0, block * 2 + core] = whole(3 + block).astype(BF)
        part_b[0, block * 2 + 1 - core] = whole(24 + block).astype(BF)
    for z in range(4):
        for block in range(2):
            for part in range(4):
                rows[6 * part : 6 * part + 6, :] = piece(z, 13 + block * 4 + part)
            if z < 3:
                part_b[0, 8 + z * 2 + block] = rows[...].astype(BF)
            else:
                part_a[0, 13 + block] = rows[...].astype(BF)


def send_sums_kernel(
    info, a_kept, a_came, b_kept, b_came, kept, first, second, third, ffn_out, rows, lines
):
    core = info[0]
    lines[:, 120:128, :] = jnp.zeros((4, 8, LANES), F32)

    def spread(near, came, place, block):
        rows[...] = near[0, place].astype(F32) + came[0, place].astype(F32)
        pieces = [rows[6 * z : 6 * z + 6, :] for z in range(4)]
        for mask in range(4):
            z = info[18] ^ mask
            low = jnp.where(z % 2 == 0, pieces[0], pieces[1])
            high = jnp.where(z % 2 == 0, pieces[2], pieces[3])
            lines[mask, 6 * block : 6 * block + 6, :] = jnp.where(z < 2, low, high)

    for side, place in ((core, 0), (1 - core, 13)):
        for block in range(3):
            spread(a_kept, a_came, block * 2 + side, place + block)
        for block in range(5):
            spread(b_kept, b_came, block * 2 + side, place + 3 + block)
    spread(a_kept, a_came, 8, 8)
    for block in range(2):
        spread(a_kept, a_came, 6 + block, 9 + block)
        spread(b_kept, b_came, 10 + block, 11 + block)
        ffn_out[:, block * LANES : (block + 1) * LANES] = (
            b_kept[0, 12 + block].astype(F32) + b_came[0, 12 + block].astype(F32)
        )
    for mask, target in enumerate((kept, first, second, third)):
        target[...] = lines[mask].astype(BF)


def join_sums_kernel(
    info, kept, first, second, third,
    held, other, out, ffn_bias, conv_taps, conv_out, biases, gains, turned, lines,
):
    pieces = [source[...].astype(F32) for source in (kept, first, second, third)]
    lines[...] = (pieces[0] + pieces[1]) + (pieces[2] + pieces[3])

    def total(place):
        return lines[6 * place : 6 * place + 6, :]

    for place in range(8):
        held[place] = total(place)
        other[place] = total(13 + place).astype(BF)
    for block in range(2):
        columns = slice(block * LANES, (block + 1) * LANES)
        out[:, columns] = total(9 + block)
        conv_out[:, columns] = total(11 + block)
    turned[...] = jnp.zeros_like(turned)
    turned[0:6, :] = total(8)[:, :128]
    biases[...] = turned[0:6, 0:9]
    conv_taps[...] = turned[0:6, 12:27]
    small = jnp.transpose(turned[...])
    gains[...] = small[9:12, 0:6]
    for i in range(4):
        ffn_bias[0:1, 6 * i : 6 * i + 6] = small[27 + i : 28 + i, 0:6]


def shares_kernel(info, held, came, qkv, ffn_in, conv_in):
    width = conv_in.shape[1]
    half, wide = width // 2, ffn_in.shape[1] // 2

    def put(target, first, apart, place):
        own_columns, other = held[place], came[place].astype(F32)
        target[:, first : first + LANES] = jnp.where(info[0] == 0, own_columns, other)
        target[:, first + apart : first + apart + LANES] = jnp.where(info[0] == 0, other, own_columns)

    for third in range(3):
        put(qkv, third * width, half, third)
    for block in range(4):
        put(ffn_in, block * LANES, wide, 3 + block)
    put(conv_in, 0, half, 7)


def erf_parts(operand):
    cumulative = 0.5 * (1.0 + lax.erf(operand * (0.5**0.5)))
    density = jnp.exp(-0.5 * operand * operand) * (0.5 / math.pi) ** 0.5
    return (cumulative, density)


def dot(left_side, right_side, left_dim=1, right_dim=0):
    return lax.dot_general(
        left_side, right_side, (((left_dim,), (right_dim,)), ((), ())), preferred_element_type=F32
    )


def normed(residual):
    centered = residual - jnp.mean(residual, axis=-1, keepdims=True)
    inverse = lax.rsqrt(jnp.mean(centered * centered, axis=-1, keepdims=True) + EPSILON)
    return (centered * inverse, inverse)


def normed_back(grad, norm, inverse, gain_row):
    scaled = grad * gain_row
    return inverse * (
        scaled
        - jnp.mean(scaled, axis=-1, keepdims=True)
        - norm * jnp.mean(scaled * norm, axis=-1, keepdims=True)
    )


def each(count, size, body):
    def step(index, unused):
        body(pl.ds(pl.multiple_of(index * size, size), size))
        return unused

    lax.fori_loop(0, count, step, 0, unroll=True)


def slots(position, ends, batch):
    number = jnp.zeros(position.shape, jnp.int32)
    for place in range(SLOTS):
        number = number + (position >= ends[4 + SLOTS * batch + place]).astype(jnp.int32)
    return number


def attention_kernel(
    flow, info, tokens, part_a, order, weights, rows, taps, ffn_bias, qkv, attended, soft, part
):
    half, width = attended.shape[1], tokens.shape[1]
    per_batch = soft.shape[1]
    qkv_w, out_w = weights.at[0:width, :], weights.at[width:, 0:width]
    weights[width:, width:] = jnp.zeros((half, half), BF)
    flow.arrive()
    for x in range(4):
        there = slice(96 * x, 96 * x + 96)
        for block in range(3):
            columns = slice(block * LANES, (block + 1) * LANES)
            qkv_w[there, columns] = tall_rows(info, part_a, "yx", block * 2, x).astype(BF)
            below = slice(half + 96 * x, half + 96 * x + 96)
            qkv_w[below, columns] = tall_rows(info, part_a, "yx", block * 2 + 1, x).astype(BF)
        for block in range(2):
            columns = slice(block * LANES, (block + 1) * LANES)
            out_w[there, columns] = tall_rows(info, part_a, "yx", 6 + block, x).astype(BF)
    flow.leave(0)
    small = jnp.concatenate([tall_rows(info, part_a, "yx", 8, x) for x in range(4)], axis=0)
    mine = jnp.transpose(small[:, 0:128])
    theirs = jnp.transpose(small[:, 128:256])
    rows[...] = jnp.zeros_like(rows)
    left, right = jnp.where(info[0] == 0, mine, theirs), jnp.where(info[0] == 0, theirs, mine)
    rows[0:12, :half] = left[0:12, :]
    rows[0:12, half:] = right[0:12, :]
    rows[12:14, :half] = mine[0:2, :]
    rows[14:15, :half] = mine[6:7, :]
    taps[...] = jnp.zeros_like(taps)
    taps[0:15, :] = mine[12:27, :]
    spread = jnp.concatenate(
        [
            jnp.concatenate([mine[27 + i : 28 + i, 96 * x : 96 * x + 96] for i in range(4)], axis=1)
            for x in range(4)
        ]
        + [jnp.zeros((4, half), F32)],
        axis=0,
    )
    spread = dot(spread.astype(BF), order[...])
    for x in range(4):
        ffn_bias[0:1, x * LANES : (x + 1) * LANES] = spread[x : x + 1, :]
    for third in range(3):
        columns = slice(third * half, (third + 1) * half)
        block = dot(tokens[...], qkv_w[:, columns])
        if third != 1:
            block = block + rows[12 + third // 2 : 13 + third // 2, :half]
        qkv[:, columns] = block.astype(BF)
    square = (per_batch, per_batch)
    down = lax.broadcasted_iota(jnp.int32, square, 0)
    across = lax.broadcasted_iota(jnp.int32, square, 1)
    lane = lax.broadcasted_iota(jnp.int32, (per_batch, 128), 1)
    pairs = half // 128
    for batch in range(tokens.shape[0] // per_batch):
        there = slice(batch * per_batch, (batch + 1) * per_batch)
        slot_down, slot_across = slots(down, info, batch), slots(across, info, batch)
        allowed = (slot_down == slot_across) & ((slot_across < SLOTS - 1) | (down == across))
        forbidden = jnp.where(allowed, 0.0, -1e9)
        for pair in range(pairs):
            columns = slice(pair * 128, (pair + 1) * 128)
            query = qkv[there, columns]
            key = qkv[there, half + pair * 128 : half + (pair + 1) * 128]
            value = qkv[there, 2 * half + pair * 128 : 2 * half + (pair + 1) * 128]
            result = jnp.zeros((per_batch, 128), F32)
            for side in range(2):
                mine = (lane >= HEAD_DIM) if side else (lane < HEAD_DIM)
                scores = dot(jnp.where(mine, query, jnp.zeros_like(query)), key, 1, 1)
                scores = scores * HEAD_DIM ** (-0.5) + forbidden
                exponent = jnp.exp(scores - jnp.max(scores, axis=-1, keepdims=True))
                weight = (exponent * (1.0 / jnp.sum(exponent, axis=-1, keepdims=True))).astype(BF)
                soft[(batch * pairs + pair) * 2 + side] = weight
                result = result + dot(weight, jnp.where(mine, value, jnp.zeros_like(value)))
            attended[there, columns] = result.astype(BF)
    flow.leave(4, 5, 6)
    part[...] = dot(attended[...], out_w[...]).astype(BF)


def feed_kernel(
    flow, info, tokens, mine, theirs, rows, part_b, part_a, ffn_bias,
    ffn_in, ffn_out, conv_in, conv_out, hidden, norm, inverse, activated, slope, part,
):
    half = conv_in.shape[1]

    def first(there):
        residual = (
            tokens[there, :].astype(F32)
            + (mine[there, :].astype(F32) + theirs[there, :].astype(F32))
            + rows[2:3, :]
        )
        unit, scale = normed(residual)
        norm[there, :] = unit
        inverse[there, :] = jnp.broadcast_to(scale, (scale.shape[0], 128))
        hidden[there, :] = (unit * rows[9:10, :] + rows[3:4, :]).astype(BF)

    each(tokens.shape[0] // 64, 64, first)
    flow.leave(5, 6)
    flow.arrive(5, 6)
    for x in range(4):
        for side in range(2):
            there = slice(half * side + 96 * x, half * side + 96 * x + 96)
            for block in range(4):
                columns = slice(block * LANES, (block + 1) * LANES)
                ffn_in[there, columns] = tall_rows(info, part_b, "xy", block * 2 + side, x).astype(BF)
            conv_in[there, :] = tall_rows(info, part_a, "yx", side, x).astype(BF)
        for block in range(2):
            columns = slice(block * LANES, (block + 1) * LANES)
            conv_out[96 * x : 96 * x + 96, columns] = tall_rows(info, part_a, "yx", 2 + block, x).astype(BF)
    flow.leave(0)
    wide = ffn_in.shape[1]
    chunk = 512

    def second(index, unused):
        columns = pl.ds(pl.multiple_of(index * chunk, chunk), chunk)
        up = dot(hidden[...], ffn_in[:, columns]) + ffn_bias[0:1, columns]
        cumulative, density = erf_parts(up)
        activated[:, columns] = (up * cumulative).astype(BF)
        slope[:, columns] = (cumulative + up * density).astype(BF)
        return unused

    lax.fori_loop(0, wide // chunk, second, 0, unroll=True)
    flow.leave(7, 8)
    for x in range(4):
        for y in range(4):
            for block in range(2):
                indices = {"x": index_at(info, "x", x), "y": index_at(info, "y", y)}
                place = outer_inner("xy", indices)
                pieces = [part_b[place, 8 + z * 2 + block].astype(F32) for z in range(3)]
                pieces.append(part_a[outer_inner("yx", indices), 4 + block].astype(F32))
                row = 384 * x + 96 * y
                ffn_out[row : row + 96, block * LANES : (block + 1) * LANES] = jnp.concatenate(
                    pieces, axis=0
                ).astype(BF)
    flow.leave(1)
    part[...] = dot(activated[...], ffn_out[...]).astype(BF)


def tap_row(taps, info, batch, offset):
    choice = info[1 + batch]
    row = taps[11 + offset : 12 + offset, :]
    row = jnp.where(choice == 1, taps[5 + offset : 6 + offset, :] if abs(offset) < 3 else 0.0, row)
    return jnp.where(choice == 0, taps[1 + offset : 2 + offset, :] if abs(offset) < 2 else 0.0, row)


def fill_slots(info, padded, per_batch, batches):
    position = lax.broadcasted_iota(jnp.int32, (per_batch, 128), 0)
    outside = jnp.full((8, 128), -1, jnp.int32)
    for batch in range(batches):
        padded[batch, 0:8, :] = outside
        padded[batch, 8 : 8 + per_batch, :] = slots(position, info, batch)
        padded[batch, 8 + per_batch :, :] = outside


def clear_edges(padded, per_batch, batches):
    edge = jnp.zeros((8, padded.shape[2]), F32)
    for batch in range(batches):
        padded[batch, 0:8, :] = edge
        padded[batch, 8 + per_batch :, :] = edge


def convolution_kernel(
    flow, info, hidden, mine, theirs, rows, conv_in, taps, conv_out,
    phase_one, norm, inverse, mixed, gated, slope, part, slot_pad, mixed_pad,
):
    batches = slot_pad.shape[0]
    per_batch = hidden.shape[0] // batches
    half = conv_in.shape[1]

    def first(there):
        residual = (
            hidden[there, :].astype(F32)
            + (mine[there, :].astype(F32) + theirs[there, :].astype(F32))
            + rows[4:5, :]
        )
        unit, scale = normed(residual)
        norm[there, :] = unit
        inverse[there, :] = jnp.broadcast_to(scale, (scale.shape[0], 128))
        phase_one[there, :] = (unit * rows[10:11, :] + rows[5:6, :]).astype(BF)

    each(hidden.shape[0] // 64, 64, first)
    flow.leave(1, 2)
    fill_slots(info, slot_pad, per_batch, batches)
    clear_edges(mixed_pad, per_batch, batches)
    mixed[...] = dot(phase_one[...], conv_in[...]) + rows[14:15, :half]
    for batch in range(batches):
        there = slice(batch * per_batch, (batch + 1) * per_batch)
        mixed_pad[batch, 8 : 8 + per_batch, :] = mixed[there, :]
        for column in range(half // 128):
            columns = slice(column * 128, (column + 1) * 128)
            here = slot_pad[batch, 8 : 8 + per_batch, :]
            total = jnp.zeros((per_batch, 128), F32)
            for offset in range(-3, 4):
                same = slot_pad[batch, 8 + offset : 8 + offset + per_batch, :] == here
                moved = mixed_pad[batch, 8 + offset : 8 + offset + per_batch, columns]
                tap = tap_row(taps, info, batch, offset)[:, columns]
                total = total + jnp.where(same, moved, 0.0) * tap
            cumulative, density = erf_parts(total)
            gated[there, columns] = (total * cumulative).astype(BF)
            slope[there, columns] = cumulative + total * density
    part[...] = dot(gated[...], conv_out[...]).astype(BF)


def own(info, row):
    half = row.shape[1] // 2
    return jnp.where(info[0] == 0, row[:, :half], row[:, half:])


def convolution_back_kernel(
    flow, info, phase_one, mine, theirs, cotangent, rows, conv_in, taps, conv_out, mixed, gated, slope,
    result, grad_three, grad_low, grad_mixed, part, sums, d_taps,
    slot_pad, mixed_pad, grad_pad, wide_sums,
):
    batches = slot_pad.shape[0]
    per_batch = phase_one.shape[0] // batches
    half = conv_in.shape[1]
    fill_slots(info, slot_pad, per_batch, batches)
    clear_edges(mixed_pad, per_batch, batches)
    clear_edges(grad_pad, per_batch, batches)
    wide_sums[...] = jnp.zeros_like(wide_sums)
    flow.arrive()
    size = 64
    for batch in range(batches):

        def first(index, unused):
            inner = pl.multiple_of(index * size, size)
            there = pl.ds(pl.multiple_of(batch * per_batch + inner, size), size)
            residual = (
                phase_one[there, :].astype(F32)
                + (mine[there, :].astype(F32) + theirs[there, :].astype(F32))
                + rows[7:8, :]
            )
            unit, scale = normed(residual)
            ended = (unit * rows[11:12, :] + rows[8:9, :]).astype(BF)
            result[there, :] = jnp.where(info[0] == 0, phase_one[there, :], ended)
            valid = slot_pad[batch, pl.ds(pl.multiple_of(8 + inner, 8), size), :][:, :1] < SLOTS - 1
            masked = jnp.where(valid, cotangent[there, :].astype(F32), 0.0)
            grad = normed_back(masked, unit, scale, rows[11:12, :])
            grad_three[there, :] = grad
            low = grad.astype(BF)
            grad_low[there, :] = low
            wide_sums[0:1, :] += jnp.sum(low.astype(F32), axis=0, keepdims=True)
            wide_sums[1:2, :] += jnp.sum(masked, axis=0, keepdims=True)
            wide_sums[2:3, :] += jnp.sum(masked * unit, axis=0, keepdims=True)
            return unused

        lax.fori_loop(0, per_batch // size, first, 0, unroll=True)
    flow.leave(0)
    tap_sums = [[[] for offset in range(7)] for batch in range(batches)]
    for batch in range(batches):
        there = slice(batch * per_batch, (batch + 1) * per_batch)
        grad_pad[batch, 8 : 8 + per_batch, :] = (
            dot(grad_low[there, :], conv_out[...], 1, 1) * slope[there, :]
        )
        mixed_pad[batch, 8 : 8 + per_batch, :] = mixed[there, :]
        for column in range(half // 128):
            columns = slice(column * 128, (column + 1) * 128)
            here = slot_pad[batch, 8 : 8 + per_batch, :]
            grad = grad_pad[batch, 8 : 8 + per_batch, columns]
            total = jnp.zeros((per_batch, 128), F32)
            for offset in range(-3, 4):
                away = slice(8 + offset, 8 + offset + per_batch)
                same = slot_pad[batch, away, :] == here
                tap = tap_row(taps, info, batch, -offset)[:, columns]
                total = total + jnp.where(same, grad_pad[batch, away, columns], 0.0) * tap
                term = jnp.where(same, mixed_pad[batch, away, columns], 0.0) * grad
                tap_sums[batch][offset + 3].append(jnp.sum(term, axis=0, keepdims=True))
            grad_mixed[there, columns] = total.astype(BF)
    for choice in range(3):
        for offset in range(-choice - 1, choice + 2):
            row = choice * choice + 2 * choice + offset + choice + 1
            total = jnp.zeros((1, half), F32)
            for batch in range(batches):
                joined = jnp.concatenate(tap_sums[batch][offset + 3], axis=1)
                total = total + jnp.where(info[1 + batch] == choice, joined, 0.0)
            d_taps[row : row + 1, :] = total
    d_taps[15:16, :] = jnp.zeros((1, half), F32)
    part[...] = dot(grad_mixed[...], conv_in[...], 1, 1).astype(BF)
    sums[0:1, :] = jnp.sum(grad_mixed[...].astype(F32), axis=0, keepdims=True)
    for place in range(3):
        sums[place + 1 : place + 2, :] = own(info, wide_sums[place : place + 1, :])
    sums[4:8, :] = jnp.zeros((4, half), F32)


def convolution_sums_kernel(info, phase_one, gated, grad_low, grad_mixed, kept, sent, whole):
    half = gated.shape[1]
    for block in range(2):
        columns = slice(block * LANES, (block + 1) * LANES)
        whole[0:half, :] = dot(gated[...], grad_low[:, columns], 0, 0)
        pack_rows(info, whole, "xy", 2 + block, kept, sent, 0)
    whole[...] = dot(phase_one[...], grad_mixed[...], 0, 0)
    for side in range(2):
        pack_rows(info, whole, "xy", side, kept, sent, side * half)


def feed_back_kernel(
    flow, info, grad_three, mine, theirs, norm, inverse, rows, activated, slope, hidden, ffn_in, ffn_out,
    conv_kept, conv_sent,
    grad_phase_one, grad_two, b_kept, b_sent, c_kept, c_sent, part, sums, bias_sums,
    grad_low, grad_up, wide_sums, whole,
):
    wide_sums[...] = jnp.zeros_like(wide_sums)
    flow.arrive(4, 5)

    def first(there):
        arriving = grad_three[there, :] + (mine[there, :].astype(F32) + theirs[there, :].astype(F32))
        arriving = arriving.astype(BF)
        grad_phase_one[there, :] = arriving
        arriving = arriving.astype(F32)
        unit = norm[there, :]
        grad = normed_back(arriving, unit, inverse[there, :1], rows[10:11, :])
        grad_two[there, :] = grad
        low = grad.astype(BF)
        grad_low[there, :] = low
        wide_sums[0:1, :] += jnp.sum(low.astype(F32), axis=0, keepdims=True)
        wide_sums[1:2, :] += jnp.sum(arriving, axis=0, keepdims=True)
        wide_sums[2:3, :] += jnp.sum(arriving * unit, axis=0, keepdims=True)

    each(hidden.shape[0] // 64, 64, first)
    flow.leave(0)
    flow.arrive(7, 8, 10, 11)
    half = ffn_in.shape[0] // 2
    for block in range(ffn_in.shape[1] // LANES):
        columns = slice(block * LANES, (block + 1) * LANES)
        grad = dot(grad_low[...], ffn_out[columns, :], 1, 1) * slope[:, columns].astype(F32)
        low = grad.astype(BF)
        grad_up[:, columns] = low
        bias_sums[0:1, columns] = jnp.sum(low.astype(F32), axis=0, keepdims=True)
        whole[...] = dot(hidden[...], low, 0, 0)
        for side in range(2):
            pack_rows(info, whole, "xy", block * 2 + side, b_kept, b_sent, side * half)
    for place in range(8):
        for block in range(4):
            b_kept[place, 8 + block] = conv_kept[place, block]
            b_sent[place, 8 + block] = conv_sent[place, block]
    for step in range(4):
        x = coordinate_at(info, "x", step)
        there = pl.ds(pl.multiple_of(x * 384, 128), 384)
        for block in range(2):
            columns = slice(block * LANES, (block + 1) * LANES)
            whole[0:384, :] = dot(activated[:, there], grad_low[:, columns], 0, 0)
            for outer in range(4):
                for inner in range(4):
                    z, y = coordinate_at(info, "z", outer), coordinate_at(info, "y", inner)
                    piece = whole[pl.ds(pl.multiple_of(96 * y + 24 * z, 8), 24), :].astype(BF)
                    place = ((outer % 2) * 4 + step) * 4 + inner
                    (c_kept if outer < 2 else c_sent)[place, block] = piece
    part[...] = dot(grad_up[...], ffn_in[...], 1, 1).astype(BF)
    for place in range(3):
        sums[place : place + 1, :] = own(info, wide_sums[place : place + 1, :])
    sums[3:8, :] = jnp.zeros((5, sums.shape[1]), F32)


def attention_back_kernel(
    flow, info, grad_two, mine, theirs, norm, inverse, rows, tokens, qkv, attended, soft, weights,
    sums_two, sums_three, d_taps, bias_sums, order,
    grad_one, kept, sent, grad_qkv, grad_low, grad_attended, wide_sums, whole, sums,
):
    flow.arrive(4, 5)
    half, width = attended.shape[1], tokens.shape[1]
    out_w = weights.at[width:, 0:width]
    per_batch = soft.shape[1]
    wide_sums[...] = jnp.zeros_like(wide_sums)

    def first(there):
        arriving = grad_two[there, :] + (mine[there, :].astype(F32) + theirs[there, :].astype(F32))
        unit = norm[there, :]
        grad = normed_back(arriving, unit, inverse[there, :1], rows[9:10, :])
        grad_one[there, :] = grad
        low = grad.astype(BF)
        grad_low[there, :] = low
        wide_sums[0:1, :] += jnp.sum(low.astype(F32), axis=0, keepdims=True)
        wide_sums[1:2, :] += jnp.sum(arriving, axis=0, keepdims=True)
        wide_sums[2:3, :] += jnp.sum(arriving * unit, axis=0, keepdims=True)

    each(tokens.shape[0] // 64, 64, first)
    flow.leave(0)
    flow.arrive(7, 8, 9, 10, 11)
    for block in range(2):
        columns = slice(block * LANES, (block + 1) * LANES)
        whole[0:half, :] = dot(attended[...], grad_low[:, columns], 0, 0)
        pack_rows(info, whole, "yx", 6 + block, kept, sent, 0)
    grad_attended[...] = dot(grad_low[...], out_w[...], 1, 1).astype(BF)
    lane = lax.broadcasted_iota(jnp.int32, (per_batch, 128), 1)
    pairs = half // 128
    scale = HEAD_DIM ** (-0.5)
    for batch in range(tokens.shape[0] // per_batch):
        there = slice(batch * per_batch, (batch + 1) * per_batch)
        for pair in range(pairs):
            columns = [
                slice(third * half + pair * 128, third * half + (pair + 1) * 128) for third in range(3)
            ]
            query, key, value = (qkv[there, columns[third]] for third in range(3))
            grad = grad_attended[there, columns[0]]
            totals = [jnp.zeros((per_batch, 128), F32) for third in range(3)]
            for side in range(2):
                mine_lanes = (lane >= HEAD_DIM) if side else (lane < HEAD_DIM)

                def only(operand):
                    return jnp.where(mine_lanes, operand, jnp.zeros_like(operand))

                weight = soft[(batch * pairs + pair) * 2 + side]
                grad_side = only(grad)
                grad_soft = dot(grad_side, value, 1, 1)
                weight_wide = weight.astype(F32)
                inner = jnp.sum(grad_soft * weight_wide, axis=-1, keepdims=True)
                grad_scores = (weight_wide * (grad_soft - inner)).astype(BF)
                totals[0] = totals[0] + dot(grad_scores, only(key))
                totals[1] = totals[1] + dot(grad_scores, only(query), 0, 0)
                totals[2] = totals[2] + dot(weight, grad_side, 0, 0)
            grad_qkv[there, columns[0]] = (totals[0] * scale).astype(BF)
            grad_qkv[there, columns[1]] = (totals[1] * scale).astype(BF)
            grad_qkv[there, columns[2]] = totals[2].astype(BF)
    sums[...] = jnp.zeros_like(sums)
    for third in range(3):
        columns = slice(third * half, (third + 1) * half)
        whole[...] = dot(tokens[...], grad_qkv[:, columns], 0, 0)
        for side in range(2):
            pack_rows(info, whole, "yx", third * 2 + side, kept, sent, side * half)
        if third != 1:
            place = third // 2
            sums[place : place + 1, :] = jnp.sum(
                grad_qkv[:, columns].astype(F32), axis=0, keepdims=True
            )
    sums[2:3, :] = own(info, wide_sums[0:1, :])
    sums[3:4, :] = own(info, wide_sums[1:2, :])
    sums[4:6, :] = sums_two[0:2, :]
    sums[6:9, :] = sums_three[0:3, :]
    sums[9:10, :] = own(info, wide_sums[2:3, :])
    sums[10:11, :] = sums_two[2:3, :]
    sums[11:12, :] = sums_three[3:4, :]
    sums[12:27, :] = d_taps[0:15, :]
    spread = jnp.concatenate(
        [bias_sums[0:1, x * LANES : (x + 1) * LANES] for x in range(4)] + [jnp.zeros((4, half), F32)], axis=0
    )
    spread = dot(spread.astype(BF), order[...], 1, 1)
    for i in range(4):
        sums[27 + i : 28 + i, :] = jnp.concatenate(
            [spread[x : x + 1, 96 * i : 96 * i + 96] for x in range(4)], axis=1
        )
    whole[0:half, :] = jnp.zeros((half, LANES), F32)
    whole[0:half, 0:128] = jnp.transpose(sums[...])
    pack_rows(info, whole, "yx", 8, kept, sent, 0)


def tokens_back_kernel(flow, grad_qkv, weights, part):
    flow.arrive()
    part[...] = dot(grad_qkv[...], weights[0 : part.shape[1], :], 1, 1).astype(BF)


class Flow:
    def __init__(self):
        self.coming, self.going = {}, {}

    def arrive(self, *chosen):
        for which in chosen or tuple(self.coming):
            for copy in self.coming[which]:
                copy.wait()

    def leave(self, *chosen):
        for which in chosen:
            self.going[which].start()


def kernel_call(body, outputs, scratch, has_info, *operands, late=(), early=(), mib=4, gflop=0):
    vmem = pl.BlockSpec(memory_space=pltpu.VMEM)
    smem = pl.BlockSpec(memory_space=pltpu.SMEM)
    hbm = pl.BlockSpec(memory_space=pltpu.HBM)
    groups = [operand if isinstance(operand, tuple) else (operand,) for operand in operands]
    arrays = [array for group in groups for array in group]
    moves = sum(len(groups[which]) for which in late) + len(early)

    def with_copies(*refs):
        taken = 0
        operand_refs = []
        for group in groups:
            operand_refs.append(refs[taken : taken + len(group)])
            taken += len(group)
        output_refs = list(refs[taken : taken + len(outputs)])
        own = refs[taken + len(outputs) : taken + len(outputs) + len(scratch)]
        buffers = list(refs[taken + len(outputs) + len(scratch) : -1])
        flags, used = refs[-1], 0
        flow = Flow()
        for which in late:
            buffer = buffers.pop(0)
            first, flow.coming[which] = 0, []
            for source in operand_refs[which]:
                count = source.shape[0]
                target = buffer if len(groups[which]) == 1 else buffer.at[pl.ds(first, count)]
                copy = pltpu.make_async_copy(source, target, flags.at[used])
                copy.start()
                flow.coming[which].append(copy)
                first, used = first + count, used + 1
            operand_refs[which] = (buffer,)
        for which in early:
            buffer = buffers.pop(0)
            flow.going[which] = pltpu.make_async_copy(buffer, output_refs[which], flags.at[used])
            output_refs[which] = buffer
            used += 1
        body(flow, *(group[0] for group in operand_refs), *output_refs, *own)
        for which in early:
            flow.going[which].wait()

    specs = [smem if has_info and place == 0 else vmem for place in range(len(operands))]
    out_specs = [vmem] * len(outputs)
    memory = [pltpu.VMEM(shape, dtype) for shape, dtype in scratch]
    for which in late:
        specs[which] = hbm
        whole = sum(array.shape[0] for array in groups[which])
        memory.append(pltpu.VMEM((whole, *groups[which][0].shape[1:]), groups[which][0].dtype))
    for which in early:
        out_specs[which] = hbm
        memory.append(pltpu.VMEM(*outputs[which]))
    if moves:
        memory.append(pltpu.SemaphoreType.DMA((moves,)))
    return pl.pallas_call(
        with_copies if moves else body,
        out_shape=[jax.ShapeDtypeStruct(shape, dtype) for shape, dtype in outputs],
        in_specs=[spec for spec, group in zip(specs, groups) for array in group],
        out_specs=out_specs,
        scratch_shapes=memory,
        compiler_params=pltpu.CompilerParams(vmem_limit_bytes=mib * 1024 * 1024),
        cost_estimate=pl.CostEstimate(flops=int(gflop * 1e9), bytes_accessed=1 << 20, transcendentals=0),
    )(*arrays)


def gather_weights(info, masters):
    (qkv, out, ffn_in, ffn_bias, ffn_out, conv_in, conv_taps, conv_out, biases, gains) = masters
    mine, theirs = kernel_call(
        send_weights_kernel,
        [((128, LANES), BF), ((56, LANES), BF)],
        [((128, 128), F32), ((128, LANES), F32), ((56, LANES), F32)],
        True,
        lax.axis_index("phase").astype(jnp.int32).reshape(1), qkv, out, ffn_in, ffn_bias.reshape(1, -1), ffn_out,
        conv_in, conv_taps.T, conv_out, biases.T, gains,
        late=tuple(range(1, 11)),
        mib=60,
    )

    def together(*values):
        return lax.optimization_barrier(values)

    line = jnp.concatenate([mine, swap(theirs)])
    part_a, part_b = kernel_call(
        line_weights_kernel,
        [((1, 15, 24, LANES), BF), ((1, 14, 24, LANES), BF)],
        [((24, LANES), F32), ((4, 184, LANES), F32)],
        True,
        info, line, *(lax.ppermute(line, BOTH, across(mask)) for mask in (1, 2, 3)),
    )
    for step in range(2):
        part_a, part_b = together(grown(part_a, "x", step), grown(part_b, "y", step))
    came = lax.ppermute(part_a, BOTH, partners("y", 0))
    early, late, part_b = together(
        jnp.concatenate([part_a[:, :9], came[:, :9]]),
        jnp.concatenate([part_a[:, 9:], came[:, 9:]]),
        grown(part_b, "x", 0),
    )
    return (
        (early, lax.ppermute(early, BOTH, partners("y", 1))),
        (late, lax.ppermute(late, BOTH, partners("y", 1))),
        (part_b, lax.ppermute(part_b, BOTH, partners("x", 1))),
    )


def shards(
    tokens,
    cotangent,
    lengths,
    kernel_choice,
    *masters,
):
    batches = lengths.shape[0]
    rows, width = tokens.shape
    per_batch = rows // batches
    half = width // 2
    wide = masters[2].shape[1] // 2
    heads = half // HEAD_DIM
    info = info_of(lengths, kernel_choice)
    part_a, rest, part_b = gather_weights(info, masters)
    order = bias_order()
    low, full = ((rows, width), BF), ((rows, width), F32)
    narrow = ((rows, 128), F32)
    slot_pad = ((batches, per_batch + 16, 128), jnp.int32)
    row_pad = ((batches, per_batch + 16, half), F32)
    whole = ((width, LANES), F32)

    def halves(blocks):
        return [((8, blocks, 24, LANES), BF)] * 2

    weights, all_rows, taps, ffn_bias, qkv, attended, soft, part = kernel_call(
        attention_kernel,
        [
            ((width + half, 3 * half), BF), ((16, width), F32),
            ((16, half), F32), ((1, wide), F32), ((rows, 3 * half), BF), ((rows, half), BF),
            ((batches * heads, per_batch, per_batch), BF), low,
        ],
        [],
        True,
        info, tokens, part_a, order,
        late=(2,),
        early=(0, 4, 5, 6),
        gflop=5,
        mib=16,
    )
    ffn_in, ffn_out, conv_in, conv_out, hidden, norm_one, inverse_one, activated, slope_up, part_two = kernel_call(
        feed_kernel,
        [
            ((width, wide), BF), ((wide, width), BF), ((width, half), BF), ((half, width), BF), low, full, narrow, ((rows, wide), BF), ((rows, wide), BF), low,
        ],
        [],
        True,
        info, tokens, part, swap(part), all_rows, part_b, rest, ffn_bias,
        late=(5, 6),
        early=(0, 1, 5, 6, 7, 8),
        gflop=8,
        mib=24,
    )
    phase_one, norm_two, inverse_two, mixed, gated, slope, part_three = kernel_call(
        convolution_kernel,
        [low, full, narrow, ((rows, half), F32), ((rows, half), BF), ((rows, half), F32), low],
        [slot_pad, row_pad],
        True,
        info, hidden, part_two, swap(part_two), all_rows, conv_in, taps, conv_out,
        early=(1, 2),
        gflop=4,
        mib=8,
    )
    block_outputs, grad_three, grad_low, grad_mixed, part, sums_three, d_taps = kernel_call(
        convolution_back_kernel,
        [low, full, low, ((rows, half), BF), low, ((8, half), F32), ((16, half), F32)],
        [slot_pad, row_pad, row_pad, ((8, width), F32)],
        True,
        info, phase_one, part_three, swap(part_three), cotangent, all_rows, conv_in, taps, conv_out,
        mixed, gated, slope,
        late=(4,),
        early=(0,),
        gflop=8,
        mib=10,
    )
    conv_kept, conv_sent = kernel_call(
        convolution_sums_kernel,
        halves(4),
        [whole],
        True,
        info, phase_one, gated, grad_low, grad_mixed,
        gflop=2,
        mib=6,
    )
    grad_phase_one, grad_two, b_kept, b_sent, c_kept, c_sent, part, sums_two, d_ffn_bias = kernel_call(
        feed_back_kernel,
        [
            low, full, *halves(12), ((32, 2, 24, LANES), BF), ((32, 2, 24, LANES), BF), low,
            ((8, half), F32), ((1, wide), F32),
        ],
        [low, ((rows, wide), BF), ((8, width), F32), whole],
        True,
        info, grad_three, part, swap(part), norm_two, inverse_two, all_rows, activated, slope_up, hidden,
        ffn_in, ffn_out, conv_kept, conv_sent,
        late=(4, 5, 7, 8, 10, 11),
        early=(0,),
        gflop=10,
        mib=20,
    )
    grad_one, a_kept, a_sent, grad_qkv = kernel_call(
        attention_back_kernel,
        [full, *halves(9), ((rows, 3 * half), BF)],
        [low, ((rows, half), BF), ((8, width), F32), whole, ((128, half), F32)],
        True,
        info, grad_two, part, swap(part), norm_one, inverse_one, all_rows, tokens, qkv, attended, soft,
        weights, sums_two, sums_three, d_taps, d_ffn_bias, order,
        late=(4, 5, 7, 8, 9, 10, 11),
        early=(0,),
        gflop=10,
        mib=20,
    )
    (part,) = kernel_call(
        tokens_back_kernel, [low], [], False, grad_qkv, weights, late=(1,), gflop=1, mib=8
    )
    theirs = lax.ppermute(part, "phase", [(1, 0)])
    b_kept, b_sent = halved(b_kept, exchanged(b_sent, "x", 1))
    c_kept, c_sent = halved(c_kept, exchanged(c_sent, "z", 1))
    a_kept, a_sent = halved(after(a_kept, b_sent, c_sent, theirs), exchanged(a_sent, "y", 1))
    b_came = exchanged(b_sent, "x", 0)
    c_kept, c_sent = halved(after(c_kept, b_sent), exchanged(c_sent, "z", 0))
    c_kept, c_sent = halved(c_kept, exchanged(c_sent, "x", 1))
    a_kept, a_sent = halved(after(a_kept, b_came, c_sent), exchanged(a_sent, "y", 0))
    b_kept, b_sent = halved(after(b_kept, a_sent), b_came)
    c_kept, c_sent = halved(c_kept, exchanged(c_sent, "x", 0))
    b_kept, b_sent = (jnp.concatenate(pair, axis=1) for pair in ((b_kept, c_kept), (b_sent, c_sent)))
    b_came = exchanged(b_sent, "y", 1)
    a_kept, a_sent = halved(a_kept, exchanged(a_sent, "x", 1))
    b_kept, b_sent = halved(after(b_kept, a_sent), b_came)
    *pieces, ffn_out_share = kernel_call(
        send_sums_kernel,
        [*[((128, LANES), BF)] * 4, (masters[4].shape, F32)],
        [((24, LANES), F32), ((4, 128, LANES), F32)],
        True,
        info, a_kept, exchanged(a_sent, "x", 0), b_kept, exchanged(b_sent, "y", 0),
    )
    grad_one = after(grad_one, pieces[1])
    shapes = [master.shape for master in masters]
    shapes[3] = (1, shapes[3][0])
    for turned in (6, 8):
        shapes[turned] = shapes[turned][::-1]
    joined, swapped = (1, 3, 6, 7, 8, 9), (0, 2, 5)
    held, other, *done = kernel_call(
        join_sums_kernel,
        [((8, 6, LANES), F32), ((8, 6, LANES), BF), *((shapes[place], F32) for place in joined)],
        [((128, 128), F32), ((128, LANES), F32)],
        True,
        info, pieces[0], *(lax.ppermute(pieces[mask], BOTH, across(mask)) for mask in (1, 2, 3)),
    )
    done += kernel_call(
        shares_kernel, [(shapes[place], F32) for place in swapped], [], True, info, held, swap(other)
    )
    shares = dict(zip(joined + swapped, done))
    shares[4] = ffn_out_share
    shares[3] = shares[3].reshape(-1)
    for turned in (6, 8):
        shares[turned] = shares[turned].T
    shares = [shares[place] for place in range(10)]
    grad_tokens = (grad_one + (part.astype(F32) + theirs.astype(F32))).astype(BF)
    input_grads = jnp.where(lax.axis_index("phase") == 0, grad_tokens, grad_phase_one)
    return (block_outputs[None], input_grads[None], *shares)


def solution(mesh):
    sharded, columns = P(BOTH, None), P(None, BOTH)
    weights = (sharded, sharded, sharded, P(BOTH), sharded, sharded, columns, sharded, columns, columns)
    return jax.shard_map(
        shards,
        mesh=mesh,
        in_specs=(P("dp", None), P("dp", None), P("dp", None), P("dp"), *weights),
        out_specs=(P("phase", "dp", None), P("phase", "dp", None), *weights),
        check_vma=False,
    )
```

```python
import math

import jax
import jax.numpy as jnp
import numpy as np
from jax import lax
from jax.experimental import pallas as pl
from jax.experimental.pallas import tpu as pltpu
from jax.sharding import PartitionSpec as P

HEAD_DIM = 64
EPSILON = 1e-05
BOTH = ("phase", "dp")
STRIDE = {"x": 16, "y": 4, "z": 1}
AXES = "xyz"
LANES = 384
SLOTS = 6
SWAP = [(0, 1), (1, 0)]
BF = jnp.bfloat16
F32 = jnp.float32


def partners(axis, step):
    pairs = []
    for core in range(2):
        mask = (1, 3)[(core + step) % 2]
        for chip in range(64):
            coordinate = (chip // STRIDE[axis]) % 4
            target = chip + ((coordinate ^ mask) - coordinate) * STRIDE[axis]
            pairs.append((core * 64 + chip, core * 64 + target))
    return pairs


def across(mask):
    return [(device, device + (((device % 4) ^ mask) - device % 4)) for device in range(128)]


def grown(held, axis, step):
    return jnp.concatenate([held, lax.ppermute(held, BOTH, partners(axis, step))])


def exchanged(sent, axis, step):
    return lax.ppermute(sent, BOTH, partners(axis, step))


def halved(kept, came):
    count = kept.shape[0] // 2
    return tuple(
        (kept[there].astype(F32) + came[there].astype(F32)).astype(BF)
        for there in (slice(0, count), slice(count, 2 * count))
    )


def after(value, *others):
    return lax.optimization_barrier((value, *others))[0]


def swap(part):
    return lax.ppermute(part, "phase", SWAP)


def bias_order():
    table = np.zeros((LANES, LANES), np.float32)
    for i in range(4):
        for d in range(16):
            for j in range(6):
                table[96 * i + 6 * d + j, 24 * d + 6 * i + j] = 1.0
    return jnp.asarray(table, BF)


def info_of(lengths, kernel_choice):
    core = lax.axis_index("phase").astype(jnp.int32)
    chip = lax.axis_index("dp").astype(jnp.int32)
    return jnp.concatenate(
        [
            core[None],
            kernel_choice,
            jnp.zeros((3 - kernel_choice.shape[0],), jnp.int32),
            jnp.cumsum(lengths, axis=-1).reshape(-1),
            jnp.stack([(chip // STRIDE[axis]) % 4 for axis in AXES]),
            jnp.stack([1 + 2 * core, 3 - 2 * core]),
        ]
    )


def coordinate_at(info, axis, index):
    here = info[16 + AXES.index(axis)]
    return here ^ (0, info[19], info[20], 2)[index]


def index_at(info, axis, coordinate):
    apart = info[16 + AXES.index(axis)] ^ coordinate
    return jnp.where(
        apart == 0, 0, jnp.where(apart == info[19], 1, jnp.where(apart == info[20], 2, 3))
    )


def outer_inner(order, indices):
    place = 0
    for axis in order:
        place = place * 4 + indices[axis]
    return place


def tall_rows(info, part, order, block, x):
    pieces = []
    for y in range(4):
        place = outer_inner(order, {"x": index_at(info, "x", x), "y": index_at(info, "y", y)})
        pieces.append(part[place, block].astype(F32))
    return jnp.concatenate(pieces, axis=0)


def pack_rows(info, source, order, block, kept, sent, first_row):
    for outer in range(4):
        for inner in range(4):
            place = {order[0]: coordinate_at(info, order[0], outer)}
            place[order[1]] = coordinate_at(info, order[1], inner)
            row = pl.multiple_of(first_row + 96 * place["x"] + 24 * place["y"], 8)
            piece = source[pl.ds(row, 24), :].astype(BF)
            (kept if outer < 2 else sent)[(outer % 2) * 4 + inner, block] = piece


def send_weights_kernel(
    flow, core, qkv, out, ffn_in, ffn_bias, ffn_out, conv_in, conv_taps, conv_out, biases, gains,
    mine, theirs, turned, mine_rows, their_rows,
):
    width = out.shape[1]
    half, wide = width // 2, ffn_in.shape[1] // 2
    turned[...] = jnp.zeros_like(turned)
    flow.arrive()
    turned[9:12, 0:6] = gains[...]
    for i in range(4):
        turned[27 + i : 28 + i, 0:6] = ffn_bias[0:1, 6 * i : 6 * i + 6]
    turned[0:8, :] = jnp.transpose(turned[...])[0:8, :]
    turned[0:6, 0:9] = biases[...]
    turned[0:6, 12:27] = conv_taps[...]
    small = turned[0:6, :]
    blank = jnp.zeros((6, LANES - 128), F32)
    small = jnp.concatenate([small, blank], axis=1)
    mine_rows[120:128, :] = jnp.zeros((8, LANES), F32)
    their_rows[48:56, :] = jnp.zeros((8, LANES), F32)

    def put(target, place, block):
        target[6 * place : 6 * place + 6, :] = block

    def pair(source, first, apart):
        return (source[:, first : first + LANES], source[:, first + apart : first + apart + LANES])

    places = [pair(qkv, third * width, half) for third in range(3)]
    places += [pair(ffn_in, block * LANES, wide) for block in range(4)]
    places.append(pair(conv_in, 0, half))
    for place, (low, high) in enumerate(places):
        put(mine_rows, place, jnp.where(core[0] == 0, low, high))
        put(their_rows, place, jnp.where(core[0] == 0, high, low))
    put(mine_rows, 8, small)
    put(their_rows, 8, small)
    for block in range(2):
        columns = slice(block * LANES, (block + 1) * LANES)
        put(mine_rows, 9 + block, out[:, columns])
        put(mine_rows, 11 + block, conv_out[:, columns])
        for part in range(4):
            put(mine_rows, 13 + block * 4 + part, ffn_out[6 * part : 6 * part + 6, columns])
    mine[...] = mine_rows[...].astype(BF)
    theirs[...] = their_rows[...].astype(BF)


def line_weights_kernel(info, own_rows, first, second, third, part_a, part_b, rows, lines):
    core = info[0]

    for mask, source in enumerate((own_rows, first, second, third)):
        lines[mask] = source[...].astype(F32)

    def piece(z, place):
        row = 6 * place if place < 21 else 128 + 6 * (place - 21)
        return lines[info[18] ^ z, row : row + 6, :]

    def whole(place):
        for z in range(4):
            rows[6 * z : 6 * z + 6, :] = piece(z, place)
        return rows[...]

    for block in range(3):
        part_a[0, block * 2 + core] = whole(block).astype(BF)
        part_a[0, block * 2 + 1 - core] = whole(21 + block).astype(BF)
    for block in range(2):
        part_a[0, 6 + block] = whole(9 + block).astype(BF)
        part_a[0, 11 + block] = whole(11 + block).astype(BF)
    mine = whole(8)[:, :128]
    theirs = whole(29)[:, :128]
    part_a[0, 8] = jnp.concatenate([mine, theirs, jnp.zeros_like(mine)], axis=1).astype(BF)
    part_a[0, 9 + core] = whole(7).astype(BF)
    part_a[0, 10 - core] = whole(28).astype(BF)
    for block in range(4):
        part_b[0, block * 2 + core] = whole(3 + block).astype(BF)
        part_b[0, block * 2 + 1 - core] = whole(24 + block).astype(BF)
    for z in range(4):
        for block in range(2):
            for part in range(4):
                rows[6 * part : 6 * part + 6, :] = piece(z, 13 + block * 4 + part)
            if z < 3:
                part_b[0, 8 + z * 2 + block] = rows[...].astype(BF)
            else:
                part_a[0, 13 + block] = rows[...].astype(BF)


def send_sums_kernel(
    info, a_kept, a_came, b_kept, b_came, kept, first, second, third, ffn_out, rows, lines
):
    core = info[0]
    lines[:, 120:128, :] = jnp.zeros((4, 8, LANES), F32)

    def spread(near, came, place, block):
        rows[...] = near[0, place].astype(F32) + came[0, place].astype(F32)
        pieces = [rows[6 * z : 6 * z + 6, :] for z in range(4)]
        for mask in range(4):
            z = info[18] ^ mask
            low = jnp.where(z % 2 == 0, pieces[0], pieces[1])
            high = jnp.where(z % 2 == 0, pieces[2], pieces[3])
            lines[mask, 6 * block : 6 * block + 6, :] = jnp.where(z < 2, low, high)

    for side, place in ((core, 0), (1 - core, 13)):
        for block in range(3):
            spread(a_kept, a_came, block * 2 + side, place + block)
        for block in range(5):
            spread(b_kept, b_came, block * 2 + side, place + 3 + block)
    spread(a_kept, a_came, 8, 8)
    for block in range(2):
        spread(a_kept, a_came, 6 + block, 9 + block)
        spread(b_kept, b_came, 10 + block, 11 + block)
        ffn_out[:, block * LANES : (block + 1) * LANES] = (
            b_kept[0, 12 + block].astype(F32) + b_came[0, 12 + block].astype(F32)
        )
    for mask, target in enumerate((kept, first, second, third)):
        target[...] = lines[mask].astype(BF)


def join_sums_kernel(
    info, kept, first, second, third,
    held, other, out, ffn_bias, conv_taps, conv_out, biases, gains, turned, lines,
):
    pieces = [source[...].astype(F32) for source in (kept, first, second, third)]
    lines[...] = (pieces[0] + pieces[1]) + (pieces[2] + pieces[3])

    def total(place):
        return lines[6 * place : 6 * place + 6, :]

    for place in range(8):
        held[place] = total(place)
        other[place] = total(13 + place).astype(BF)
    for block in range(2):
        columns = slice(block * LANES, (block + 1) * LANES)
        out[:, columns] = total(9 + block)
        conv_out[:, columns] = total(11 + block)
    turned[...] = jnp.zeros_like(turned)
    turned[0:6, :] = total(8)[:, :128]
    biases[...] = turned[0:6, 0:9]
    conv_taps[...] = turned[0:6, 12:27]
    small = jnp.transpose(turned[...])
    gains[...] = small[9:12, 0:6]
    for i in range(4):
        ffn_bias[0:1, 6 * i : 6 * i + 6] = small[27 + i : 28 + i, 0:6]


def shares_kernel(info, held, came, qkv, ffn_in, conv_in):
    width = conv_in.shape[1]
    half, wide = width // 2, ffn_in.shape[1] // 2

    def put(target, first, apart, place):
        own_columns, other = held[place], came[place].astype(F32)
        target[:, first : first + LANES] = jnp.where(info[0] == 0, own_columns, other)
        target[:, first + apart : first + apart + LANES] = jnp.where(info[0] == 0, other, own_columns)

    for third in range(3):
        put(qkv, third * width, half, third)
    for block in range(4):
        put(ffn_in, block * LANES, wide, 3 + block)
    put(conv_in, 0, half, 7)


def erf_parts(operand):
    cumulative = 0.5 * (1.0 + lax.erf(operand * (0.5**0.5)))
    density = jnp.exp(-0.5 * operand * operand) * (0.5 / math.pi) ** 0.5
    return (cumulative, density)


def dot(left_side, right_side, left_dim=1, right_dim=0):
    return lax.dot_general(
        left_side, right_side, (((left_dim,), (right_dim,)), ((), ())), preferred_element_type=F32
    )


def normed(residual):
    centered = residual - jnp.mean(residual, axis=-1, keepdims=True)
    inverse = lax.rsqrt(jnp.mean(centered * centered, axis=-1, keepdims=True) + EPSILON)
    return (centered * inverse, inverse)


def normed_back(grad, norm, inverse, gain_row):
    scaled = grad * gain_row
    return inverse * (
        scaled
        - jnp.mean(scaled, axis=-1, keepdims=True)
        - norm * jnp.mean(scaled * norm, axis=-1, keepdims=True)
    )


def each(count, size, body):
    def step(index, unused):
        body(pl.ds(pl.multiple_of(index * size, size), size))
        return unused

    lax.fori_loop(0, count, step, 0, unroll=True)


def slots(position, ends, batch):
    number = jnp.zeros(position.shape, jnp.int32)
    for place in range(SLOTS):
        number = number + (position >= ends[4 + SLOTS * batch + place]).astype(jnp.int32)
    return number


def attention_kernel(
    flow, info, tokens, part_a, order, weights, rows, taps, ffn_bias, qkv, attended, soft, part
):
    half, width = attended.shape[1], tokens.shape[1]
    per_batch = soft.shape[1]
    qkv_w, out_w = weights.at[0:width, :], weights.at[width:, 0:width]
    weights[width:, width:] = jnp.zeros((half, half), BF)
    flow.arrive()
    for x in range(4):
        there = slice(96 * x, 96 * x + 96)
        for block in range(3):
            columns = slice(block * LANES, (block + 1) * LANES)
            qkv_w[there, columns] = tall_rows(info, part_a, "yx", block * 2, x).astype(BF)
            below = slice(half + 96 * x, half + 96 * x + 96)
            qkv_w[below, columns] = tall_rows(info, part_a, "yx", block * 2 + 1, x).astype(BF)
        for block in range(2):
            columns = slice(block * LANES, (block + 1) * LANES)
            out_w[there, columns] = tall_rows(info, part_a, "yx", 6 + block, x).astype(BF)
    flow.leave(0)
    small = jnp.concatenate([tall_rows(info, part_a, "yx", 8, x) for x in range(4)], axis=0)
    mine = jnp.transpose(small[:, 0:128])
    theirs = jnp.transpose(small[:, 128:256])
    rows[...] = jnp.zeros_like(rows)
    left, right = jnp.where(info[0] == 0, mine, theirs), jnp.where(info[0] == 0, theirs, mine)
    rows[0:12, :half] = left[0:12, :]
    rows[0:12, half:] = right[0:12, :]
    rows[12:14, :half] = mine[0:2, :]
    rows[14:15, :half] = mine[6:7, :]
    taps[...] = jnp.zeros_like(taps)
    taps[0:15, :] = mine[12:27, :]
    spread = jnp.concatenate(
        [
            jnp.concatenate([mine[27 + i : 28 + i, 96 * x : 96 * x + 96] for i in range(4)], axis=1)
            for x in range(4)
        ]
        + [jnp.zeros((4, half), F32)],
        axis=0,
    )
    spread = dot(spread.astype(BF), order[...])
    for x in range(4):
        ffn_bias[0:1, x * LANES : (x + 1) * LANES] = spread[x : x + 1, :]
    for third in range(3):
        columns = slice(third * half, (third + 1) * half)
        block = dot(tokens[...], qkv_w[:, columns])
        if third != 1:
            block = block + rows[12 + third // 2 : 13 + third // 2, :half]
        qkv[:, columns] = block.astype(BF)
    square = (per_batch, per_batch)
    down = lax.broadcasted_iota(jnp.int32, square, 0)
    across = lax.broadcasted_iota(jnp.int32, square, 1)
    lane = lax.broadcasted_iota(jnp.int32, (per_batch, 128), 1)
    pairs = half // 128
    for batch in range(tokens.shape[0] // per_batch):
        there = slice(batch * per_batch, (batch + 1) * per_batch)
        slot_down, slot_across = slots(down, info, batch), slots(across, info, batch)
        allowed = (slot_down == slot_across) & ((slot_across < SLOTS - 1) | (down == across))
        forbidden = jnp.where(allowed, 0.0, -1e9)
        for pair in range(pairs):
            columns = slice(pair * 128, (pair + 1) * 128)
            query = qkv[there, columns]
            key = qkv[there, half + pair * 128 : half + (pair + 1) * 128]
            value = qkv[there, 2 * half + pair * 128 : 2 * half + (pair + 1) * 128]
            result = jnp.zeros((per_batch, 128), F32)
            for side in range(2):
                mine = (lane >= HEAD_DIM) if side else (lane < HEAD_DIM)
                scores = dot(jnp.where(mine, query, jnp.zeros_like(query)), key, 1, 1)
                scores = scores * HEAD_DIM ** (-0.5) + forbidden
                exponent = jnp.exp(scores - jnp.max(scores, axis=-1, keepdims=True))
                weight = (exponent * (1.0 / jnp.sum(exponent, axis=-1, keepdims=True))).astype(BF)
                soft[(batch * pairs + pair) * 2 + side] = weight
                result = result + dot(weight, jnp.where(mine, value, jnp.zeros_like(value)))
            attended[there, columns] = result.astype(BF)
    flow.leave(4, 5, 6)
    part[...] = dot(attended[...], out_w[...]).astype(BF)


def feed_kernel(
    flow, info, tokens, mine, theirs, rows, part_b, part_a, ffn_bias,
    ffn_in, ffn_out, conv_in, conv_out, hidden, norm, inverse, activated, slope, part,
):
    half = conv_in.shape[1]

    def first(there):
        residual = (
            tokens[there, :].astype(F32)
            + (mine[there, :].astype(F32) + theirs[there, :].astype(F32))
            + rows[2:3, :]
        )
        unit, scale = normed(residual)
        norm[there, :] = unit
        inverse[there, :] = jnp.broadcast_to(scale, (scale.shape[0], 128))
        hidden[there, :] = (unit * rows[9:10, :] + rows[3:4, :]).astype(BF)

    each(tokens.shape[0] // 64, 64, first)
    flow.leave(5, 6)
    flow.arrive(5, 6)
    for x in range(4):
        for side in range(2):
            there = slice(half * side + 96 * x, half * side + 96 * x + 96)
            for block in range(4):
                columns = slice(block * LANES, (block + 1) * LANES)
                ffn_in[there, columns] = tall_rows(info, part_b, "xy", block * 2 + side, x).astype(BF)
            conv_in[there, :] = tall_rows(info, part_a, "yx", side, x).astype(BF)
        for block in range(2):
            columns = slice(block * LANES, (block + 1) * LANES)
            conv_out[96 * x : 96 * x + 96, columns] = tall_rows(info, part_a, "yx", 2 + block, x).astype(BF)
    flow.leave(0)
    wide = ffn_in.shape[1]
    chunk = 512

    def second(index, unused):
        columns = pl.ds(pl.multiple_of(index * chunk, chunk), chunk)
        up = dot(hidden[...], ffn_in[:, columns]) + ffn_bias[0:1, columns]
        cumulative, density = erf_parts(up)
        activated[:, columns] = (up * cumulative).astype(BF)
        slope[:, columns] = (cumulative + up * density).astype(BF)
        return unused

    lax.fori_loop(0, wide // chunk, second, 0, unroll=True)
    flow.leave(7, 8)
    for x in range(4):
        for y in range(4):
            for block in range(2):
                indices = {"x": index_at(info, "x", x), "y": index_at(info, "y", y)}
                place = outer_inner("xy", indices)
                pieces = [part_b[place, 8 + z * 2 + block].astype(F32) for z in range(3)]
                pieces.append(part_a[outer_inner("yx", indices), 4 + block].astype(F32))
                row = 384 * x + 96 * y
                ffn_out[row : row + 96, block * LANES : (block + 1) * LANES] = jnp.concatenate(
                    pieces, axis=0
                ).astype(BF)
    flow.leave(1)
    part[...] = dot(activated[...], ffn_out[...]).astype(BF)


def tap_row(taps, info, batch, offset):
    choice = info[1 + batch]
    row = taps[11 + offset : 12 + offset, :]
    row = jnp.where(choice == 1, taps[5 + offset : 6 + offset, :] if abs(offset) < 3 else 0.0, row)
    return jnp.where(choice == 0, taps[1 + offset : 2 + offset, :] if abs(offset) < 2 else 0.0, row)


def fill_slots(info, padded, per_batch, batches):
    position = lax.broadcasted_iota(jnp.int32, (per_batch, 128), 0)
    outside = jnp.full((8, 128), -1, jnp.int32)
    for batch in range(batches):
        padded[batch, 0:8, :] = outside
        padded[batch, 8 : 8 + per_batch, :] = slots(position, info, batch)
        padded[batch, 8 + per_batch :, :] = outside


def clear_edges(padded, per_batch, batches):
    edge = jnp.zeros((8, padded.shape[2]), F32)
    for batch in range(batches):
        padded[batch, 0:8, :] = edge
        padded[batch, 8 + per_batch :, :] = edge


def convolution_kernel(
    flow, info, hidden, mine, theirs, rows, conv_in, taps, conv_out,
    phase_one, norm, inverse, mixed, gated, slope, part, slot_pad, mixed_pad,
):
    batches = slot_pad.shape[0]
    per_batch = hidden.shape[0] // batches
    half = conv_in.shape[1]

    def first(there):
        residual = (
            hidden[there, :].astype(F32)
            + (mine[there, :].astype(F32) + theirs[there, :].astype(F32))
            + rows[4:5, :]
        )
        unit, scale = normed(residual)
        norm[there, :] = unit
        inverse[there, :] = jnp.broadcast_to(scale, (scale.shape[0], 128))
        phase_one[there, :] = (unit * rows[10:11, :] + rows[5:6, :]).astype(BF)

    each(hidden.shape[0] // 64, 64, first)
    flow.leave(1, 2)
    fill_slots(info, slot_pad, per_batch, batches)
    clear_edges(mixed_pad, per_batch, batches)
    mixed[...] = dot(phase_one[...], conv_in[...]) + rows[14:15, :half]
    for batch in range(batches):
        there = slice(batch * per_batch, (batch + 1) * per_batch)
        mixed_pad[batch, 8 : 8 + per_batch, :] = mixed[there, :]
        for column in range(half // 128):
            columns = slice(column * 128, (column + 1) * 128)
            here = slot_pad[batch, 8 : 8 + per_batch, :]
            total = jnp.zeros((per_batch, 128), F32)
            for offset in range(-3, 4):
                same = slot_pad[batch, 8 + offset : 8 + offset + per_batch, :] == here
                moved = mixed_pad[batch, 8 + offset : 8 + offset + per_batch, columns]
                tap = tap_row(taps, info, batch, offset)[:, columns]
                total = total + jnp.where(same, moved, 0.0) * tap
            cumulative, density = erf_parts(total)
            gated[there, columns] = (total * cumulative).astype(BF)
            slope[there, columns] = cumulative + total * density
    part[...] = dot(gated[...], conv_out[...]).astype(BF)


def own(info, row):
    half = row.shape[1] // 2
    return jnp.where(info[0] == 0, row[:, :half], row[:, half:])


def convolution_back_kernel(
    flow, info, phase_one, mine, theirs, cotangent, rows, conv_in, taps, conv_out, mixed, gated, slope,
    result, grad_three, grad_low, grad_mixed, part, sums, d_taps,
    slot_pad, mixed_pad, grad_pad, wide_sums,
):
    batches = slot_pad.shape[0]
    per_batch = phase_one.shape[0] // batches
    half = conv_in.shape[1]
    fill_slots(info, slot_pad, per_batch, batches)
    clear_edges(mixed_pad, per_batch, batches)
    clear_edges(grad_pad, per_batch, batches)
    wide_sums[...] = jnp.zeros_like(wide_sums)
    flow.arrive()
    size = 64
    for batch in range(batches):

        def first(index, unused):
            inner = pl.multiple_of(index * size, size)
            there = pl.ds(pl.multiple_of(batch * per_batch + inner, size), size)
            residual = (
                phase_one[there, :].astype(F32)
                + (mine[there, :].astype(F32) + theirs[there, :].astype(F32))
                + rows[7:8, :]
            )
            unit, scale = normed(residual)
            ended = (unit * rows[11:12, :] + rows[8:9, :]).astype(BF)
            result[there, :] = jnp.where(info[0] == 0, phase_one[there, :], ended)
            valid = slot_pad[batch, pl.ds(pl.multiple_of(8 + inner, 8), size), :][:, :1] < SLOTS - 1
            masked = jnp.where(valid, cotangent[there, :].astype(F32), 0.0)
            grad = normed_back(masked, unit, scale, rows[11:12, :])
            grad_three[there, :] = grad
            low = grad.astype(BF)
            grad_low[there, :] = low
            wide_sums[0:1, :] += jnp.sum(low.astype(F32), axis=0, keepdims=True)
            wide_sums[1:2, :] += jnp.sum(masked, axis=0, keepdims=True)
            wide_sums[2:3, :] += jnp.sum(masked * unit, axis=0, keepdims=True)
            return unused

        lax.fori_loop(0, per_batch // size, first, 0, unroll=True)
    flow.leave(0)
    tap_sums = [[[] for offset in range(7)] for batch in range(batches)]
    for batch in range(batches):
        there = slice(batch * per_batch, (batch + 1) * per_batch)
        grad_pad[batch, 8 : 8 + per_batch, :] = (
            dot(grad_low[there, :], conv_out[...], 1, 1) * slope[there, :]
        )
        mixed_pad[batch, 8 : 8 + per_batch, :] = mixed[there, :]
        for column in range(half // 128):
            columns = slice(column * 128, (column + 1) * 128)
            here = slot_pad[batch, 8 : 8 + per_batch, :]
            grad = grad_pad[batch, 8 : 8 + per_batch, columns]
            total = jnp.zeros((per_batch, 128), F32)
            for offset in range(-3, 4):
                away = slice(8 + offset, 8 + offset + per_batch)
                same = slot_pad[batch, away, :] == here
                tap = tap_row(taps, info, batch, -offset)[:, columns]
                total = total + jnp.where(same, grad_pad[batch, away, columns], 0.0) * tap
                term = jnp.where(same, mixed_pad[batch, away, columns], 0.0) * grad
                tap_sums[batch][offset + 3].append(jnp.sum(term, axis=0, keepdims=True))
            grad_mixed[there, columns] = total.astype(BF)
    for choice in range(3):
        for offset in range(-choice - 1, choice + 2):
            row = choice * choice + 2 * choice + offset + choice + 1
            total = jnp.zeros((1, half), F32)
            for batch in range(batches):
                joined = jnp.concatenate(tap_sums[batch][offset + 3], axis=1)
                total = total + jnp.where(info[1 + batch] == choice, joined, 0.0)
            d_taps[row : row + 1, :] = total
    d_taps[15:16, :] = jnp.zeros((1, half), F32)
    part[...] = dot(grad_mixed[...], conv_in[...], 1, 1).astype(BF)
    sums[0:1, :] = jnp.sum(grad_mixed[...].astype(F32), axis=0, keepdims=True)
    for place in range(3):
        sums[place + 1 : place + 2, :] = own(info, wide_sums[place : place + 1, :])
    sums[4:8, :] = jnp.zeros((4, half), F32)


def convolution_sums_kernel(info, phase_one, gated, grad_low, grad_mixed, kept, sent, whole):
    half = gated.shape[1]
    for block in range(2):
        columns = slice(block * LANES, (block + 1) * LANES)
        whole[0:half, :] = dot(gated[...], grad_low[:, columns], 0, 0)
        pack_rows(info, whole, "xy", 2 + block, kept, sent, 0)
    whole[...] = dot(phase_one[...], grad_mixed[...], 0, 0)
    for side in range(2):
        pack_rows(info, whole, "xy", side, kept, sent, side * half)


def feed_back_kernel(
    flow, info, grad_three, mine, theirs, norm, inverse, rows, activated, slope, hidden, ffn_in, ffn_out,
    conv_kept, conv_sent,
    grad_phase_one, grad_two, b_kept, b_sent, c_kept, c_sent, part, sums, bias_sums,
    grad_low, grad_up, wide_sums, whole,
):
    wide_sums[...] = jnp.zeros_like(wide_sums)
    flow.arrive(4, 5)

    def first(there):
        arriving = grad_three[there, :] + (mine[there, :].astype(F32) + theirs[there, :].astype(F32))
        arriving = arriving.astype(BF)
        grad_phase_one[there, :] = arriving
        arriving = arriving.astype(F32)
        unit = norm[there, :]
        grad = normed_back(arriving, unit, inverse[there, :1], rows[10:11, :])
        grad_two[there, :] = grad
        low = grad.astype(BF)
        grad_low[there, :] = low
        wide_sums[0:1, :] += jnp.sum(low.astype(F32), axis=0, keepdims=True)
        wide_sums[1:2, :] += jnp.sum(arriving, axis=0, keepdims=True)
        wide_sums[2:3, :] += jnp.sum(arriving * unit, axis=0, keepdims=True)

    each(hidden.shape[0] // 64, 64, first)
    flow.leave(0)
    flow.arrive(7, 8, 10, 11)
    half = ffn_in.shape[0] // 2
    for block in range(ffn_in.shape[1] // LANES):
        columns = slice(block * LANES, (block + 1) * LANES)
        grad = dot(grad_low[...], ffn_out[columns, :], 1, 1) * slope[:, columns].astype(F32)
        low = grad.astype(BF)
        grad_up[:, columns] = low
        bias_sums[0:1, columns] = jnp.sum(low.astype(F32), axis=0, keepdims=True)
        whole[...] = dot(hidden[...], low, 0, 0)
        for side in range(2):
            pack_rows(info, whole, "xy", block * 2 + side, b_kept, b_sent, side * half)
    for place in range(8):
        for block in range(4):
            b_kept[place, 8 + block] = conv_kept[place, block]
            b_sent[place, 8 + block] = conv_sent[place, block]
    for step in range(4):
        x = coordinate_at(info, "x", step)
        there = pl.ds(pl.multiple_of(x * 384, 128), 384)
        for block in range(2):
            columns = slice(block * LANES, (block + 1) * LANES)
            whole[0:384, :] = dot(activated[:, there], grad_low[:, columns], 0, 0)
            for outer in range(4):
                for inner in range(4):
                    z, y = coordinate_at(info, "z", outer), coordinate_at(info, "y", inner)
                    piece = whole[pl.ds(pl.multiple_of(96 * y + 24 * z, 8), 24), :].astype(BF)
                    place = ((outer % 2) * 4 + step) * 4 + inner
                    (c_kept if outer < 2 else c_sent)[place, block] = piece
    part[...] = dot(grad_up[...], ffn_in[...], 1, 1).astype(BF)
    for place in range(3):
        sums[place : place + 1, :] = own(info, wide_sums[place : place + 1, :])
    sums[3:8, :] = jnp.zeros((5, sums.shape[1]), F32)


def attention_back_kernel(
    flow, info, grad_two, mine, theirs, norm, inverse, rows, tokens, qkv, attended, soft, weights,
    sums_two, sums_three, d_taps, bias_sums, order,
    grad_one, kept, sent, grad_qkv, grad_low, grad_attended, wide_sums, whole, sums,
):
    flow.arrive(4, 5)
    half, width = attended.shape[1], tokens.shape[1]
    out_w = weights.at[width:, 0:width]
    per_batch = soft.shape[1]
    wide_sums[...] = jnp.zeros_like(wide_sums)

    def first(there):
        arriving = grad_two[there, :] + (mine[there, :].astype(F32) + theirs[there, :].astype(F32))
        unit = norm[there, :]
        grad = normed_back(arriving, unit, inverse[there, :1], rows[9:10, :])
        grad_one[there, :] = grad
        low = grad.astype(BF)
        grad_low[there, :] = low
        wide_sums[0:1, :] += jnp.sum(low.astype(F32), axis=0, keepdims=True)
        wide_sums[1:2, :] += jnp.sum(arriving, axis=0, keepdims=True)
        wide_sums[2:3, :] += jnp.sum(arriving * unit, axis=0, keepdims=True)

    each(tokens.shape[0] // 64, 64, first)
    flow.leave(0)
    flow.arrive(7, 8, 9, 10, 11)
    for block in range(2):
        columns = slice(block * LANES, (block + 1) * LANES)
        whole[0:half, :] = dot(attended[...], grad_low[:, columns], 0, 0)
        pack_rows(info, whole, "yx", 6 + block, kept, sent, 0)
    grad_attended[...] = dot(grad_low[...], out_w[...], 1, 1).astype(BF)
    lane = lax.broadcasted_iota(jnp.int32, (per_batch, 128), 1)
    pairs = half // 128
    scale = HEAD_DIM ** (-0.5)
    for batch in range(tokens.shape[0] // per_batch):
        there = slice(batch * per_batch, (batch + 1) * per_batch)
        for pair in range(pairs):
            columns = [
                slice(third * half + pair * 128, third * half + (pair + 1) * 128) for third in range(3)
            ]
            query, key, value = (qkv[there, columns[third]] for third in range(3))
            grad = grad_attended[there, columns[0]]
            totals = [jnp.zeros((per_batch, 128), F32) for third in range(3)]
            for side in range(2):
                mine_lanes = (lane >= HEAD_DIM) if side else (lane < HEAD_DIM)

                def only(operand):
                    return jnp.where(mine_lanes, operand, jnp.zeros_like(operand))

                weight = soft[(batch * pairs + pair) * 2 + side]
                grad_side = only(grad)
                grad_soft = dot(grad_side, value, 1, 1)
                weight_wide = weight.astype(F32)
                inner = jnp.sum(grad_soft * weight_wide, axis=-1, keepdims=True)
                grad_scores = (weight_wide * (grad_soft - inner)).astype(BF)
                totals[0] = totals[0] + dot(grad_scores, only(key))
                totals[1] = totals[1] + dot(grad_scores, only(query), 0, 0)
                totals[2] = totals[2] + dot(weight, grad_side, 0, 0)
            grad_qkv[there, columns[0]] = (totals[0] * scale).astype(BF)
            grad_qkv[there, columns[1]] = (totals[1] * scale).astype(BF)
            grad_qkv[there, columns[2]] = totals[2].astype(BF)
    sums[...] = jnp.zeros_like(sums)
    for third in range(3):
        columns = slice(third * half, (third + 1) * half)
        whole[...] = dot(tokens[...], grad_qkv[:, columns], 0, 0)
        for side in range(2):
            pack_rows(info, whole, "yx", third * 2 + side, kept, sent, side * half)
        if third != 1:
            place = third // 2
            sums[place : place + 1, :] = jnp.sum(
                grad_qkv[:, columns].astype(F32), axis=0, keepdims=True
            )
    sums[2:3, :] = own(info, wide_sums[0:1, :])
    sums[3:4, :] = own(info, wide_sums[1:2, :])
    sums[4:6, :] = sums_two[0:2, :]
    sums[6:9, :] = sums_three[0:3, :]
    sums[9:10, :] = own(info, wide_sums[2:3, :])
    sums[10:11, :] = sums_two[2:3, :]
    sums[11:12, :] = sums_three[3:4, :]
    sums[12:27, :] = d_taps[0:15, :]
    spread = jnp.concatenate(
        [bias_sums[0:1, x * LANES : (x + 1) * LANES] for x in range(4)] + [jnp.zeros((4, half), F32)], axis=0
    )
    spread = dot(spread.astype(BF), order[...], 1, 1)
    for i in range(4):
        sums[27 + i : 28 + i, :] = jnp.concatenate(
            [spread[x : x + 1, 96 * i : 96 * i + 96] for x in range(4)], axis=1
        )
    whole[0:half, :] = jnp.zeros((half, LANES), F32)
    whole[0:half, 0:128] = jnp.transpose(sums[...])
    pack_rows(info, whole, "yx", 8, kept, sent, 0)


def tokens_back_kernel(flow, grad_qkv, weights, part):
    flow.arrive()
    part[...] = dot(grad_qkv[...], weights[0 : part.shape[1], :], 1, 1).astype(BF)


class Flow:
    def __init__(self):
        self.coming, self.going = {}, {}

    def arrive(self, *chosen):
        for which in chosen or tuple(self.coming):
            for copy in self.coming[which]:
                copy.wait()

    def leave(self, *chosen):
        for which in chosen:
            self.going[which].start()


def kernel_call(body, outputs, scratch, has_info, *operands, late=(), early=(), mib=4, gflop=0):
    vmem = pl.BlockSpec(memory_space=pltpu.VMEM)
    smem = pl.BlockSpec(memory_space=pltpu.SMEM)
    hbm = pl.BlockSpec(memory_space=pltpu.HBM)
    groups = [operand if isinstance(operand, tuple) else (operand,) for operand in operands]
    arrays = [array for group in groups for array in group]
    moves = sum(len(groups[which]) for which in late) + len(early)

    def with_copies(*refs):
        taken = 0
        operand_refs = []
        for group in groups:
            operand_refs.append(refs[taken : taken + len(group)])
            taken += len(group)
        output_refs = list(refs[taken : taken + len(outputs)])
        own = refs[taken + len(outputs) : taken + len(outputs) + len(scratch)]
        buffers = list(refs[taken + len(outputs) + len(scratch) : -1])
        flags, used = refs[-1], 0
        flow = Flow()
        for which in late:
            buffer = buffers.pop(0)
            first, flow.coming[which] = 0, []
            for source in operand_refs[which]:
                count = source.shape[0]
                target = buffer if len(groups[which]) == 1 else buffer.at[pl.ds(first, count)]
                copy = pltpu.make_async_copy(source, target, flags.at[used])
                copy.start()
                flow.coming[which].append(copy)
                first, used = first + count, used + 1
            operand_refs[which] = (buffer,)
        for which in early:
            buffer = buffers.pop(0)
            flow.going[which] = pltpu.make_async_copy(buffer, output_refs[which], flags.at[used])
            output_refs[which] = buffer
            used += 1
        body(flow, *(group[0] for group in operand_refs), *output_refs, *own)
        for which in early:
            flow.going[which].wait()

    specs = [smem if has_info and place == 0 else vmem for place in range(len(operands))]
    out_specs = [vmem] * len(outputs)
    memory = [pltpu.VMEM(shape, dtype) for shape, dtype in scratch]
    for which in late:
        specs[which] = hbm
        whole = sum(array.shape[0] for array in groups[which])
        memory.append(pltpu.VMEM((whole, *groups[which][0].shape[1:]), groups[which][0].dtype))
    for which in early:
        out_specs[which] = hbm
        memory.append(pltpu.VMEM(*outputs[which]))
    if moves:
        memory.append(pltpu.SemaphoreType.DMA((moves,)))
    return pl.pallas_call(
        with_copies if moves else body,
        out_shape=[jax.ShapeDtypeStruct(shape, dtype) for shape, dtype in outputs],
        in_specs=[spec for spec, group in zip(specs, groups) for array in group],
        out_specs=out_specs,
        scratch_shapes=memory,
        compiler_params=pltpu.CompilerParams(vmem_limit_bytes=mib * 1024 * 1024),
        cost_estimate=pl.CostEstimate(flops=int(gflop * 1e9), bytes_accessed=1 << 20, transcendentals=0),
    )(*arrays)


def gather_weights(info, masters):
    (qkv, out, ffn_in, ffn_bias, ffn_out, conv_in, conv_taps, conv_out, biases, gains) = masters
    mine, theirs = kernel_call(
        send_weights_kernel,
        [((128, LANES), BF), ((56, LANES), BF)],
        [((128, 128), F32), ((128, LANES), F32), ((56, LANES), F32)],
        True,
        lax.axis_index("phase").astype(jnp.int32).reshape(1), qkv, out, ffn_in, ffn_bias.reshape(1, -1), ffn_out,
        conv_in, conv_taps.T, conv_out, biases.T, gains,
        late=tuple(range(1, 11)),
        mib=60,
    )

    def together(*values):
        return lax.optimization_barrier(values)

    line = jnp.concatenate([mine, swap(theirs)])
    part_a, part_b = kernel_call(
        line_weights_kernel,
        [((1, 15, 24, LANES), BF), ((1, 14, 24, LANES), BF)],
        [((24, LANES), F32), ((4, 184, LANES), F32)],
        True,
        info, line, *(lax.ppermute(line, BOTH, across(mask)) for mask in (1, 2, 3)),
    )
    for step in range(2):
        part_a, part_b = together(grown(part_a, "x", step), grown(part_b, "y", step))
    came = lax.ppermute(part_a, BOTH, partners("y", 0))
    early, late, part_b = together(
        jnp.concatenate([part_a[:, :9], came[:, :9]]),
        jnp.concatenate([part_a[:, 9:], came[:, 9:]]),
        grown(part_b, "x", 0),
    )
    return (
        (early, lax.ppermute(early, BOTH, partners("y", 1))),
        (late, lax.ppermute(late, BOTH, partners("y", 1))),
        (part_b, lax.ppermute(part_b, BOTH, partners("x", 1))),
    )


def shards(
    tokens,
    cotangent,
    lengths,
    kernel_choice,
    *masters,
):
    batches = lengths.shape[0]
    rows, width = tokens.shape
    per_batch = rows // batches
    half = width // 2
    wide = masters[2].shape[1] // 2
    heads = half // HEAD_DIM
    info = info_of(lengths, kernel_choice)
    part_a, rest, part_b = gather_weights(info, masters)
    order = bias_order()
    low, full = ((rows, width), BF), ((rows, width), F32)
    narrow = ((rows, 128), F32)
    slot_pad = ((batches, per_batch + 16, 128), jnp.int32)
    row_pad = ((batches, per_batch + 16, half), F32)
    whole = ((width, LANES), F32)

    def halves(blocks):
        return [((8, blocks, 24, LANES), BF)] * 2

    weights, all_rows, taps, ffn_bias, qkv, attended, soft, part = kernel_call(
        attention_kernel,
        [
            ((width + half, 3 * half), BF), ((16, width), F32),
            ((16, half), F32), ((1, wide), F32), ((rows, 3 * half), BF), ((rows, half), BF),
            ((batches * heads, per_batch, per_batch), BF), low,
        ],
        [],
        True,
        info, tokens, part_a, order,
        late=(2,),
        early=(0, 4, 5, 6),
        gflop=5,
        mib=16,
    )
    ffn_in, ffn_out, conv_in, conv_out, hidden, norm_one, inverse_one, activated, slope_up, part_two = kernel_call(
        feed_kernel,
        [
            ((width, wide), BF), ((wide, width), BF), ((width, half), BF), ((half, width), BF), low, full, narrow, ((rows, wide), BF), ((rows, wide), BF), low,
        ],
        [],
        True,
        info, tokens, part, swap(part), all_rows, part_b, rest, ffn_bias,
        late=(5, 6),
        early=(0, 1, 5, 6, 7, 8),
        gflop=8,
        mib=24,
    )
    phase_one, norm_two, inverse_two, mixed, gated, slope, part_three = kernel_call(
        convolution_kernel,
        [low, full, narrow, ((rows, half), F32), ((rows, half), BF), ((rows, half), F32), low],
        [slot_pad, row_pad],
        True,
        info, hidden, part_two, swap(part_two), all_rows, conv_in, taps, conv_out,
        early=(1, 2),
        gflop=4,
        mib=8,
    )
    block_outputs, grad_three, grad_low, grad_mixed, part, sums_three, d_taps = kernel_call(
        convolution_back_kernel,
        [low, full, low, ((rows, half), BF), low, ((8, half), F32), ((16, half), F32)],
        [slot_pad, row_pad, row_pad, ((8, width), F32)],
        True,
        info, phase_one, part_three, swap(part_three), cotangent, all_rows, conv_in, taps, conv_out,
        mixed, gated, slope,
        late=(4,),
        early=(0,),
        gflop=8,
        mib=10,
    )
    conv_kept, conv_sent = kernel_call(
        convolution_sums_kernel,
        halves(4),
        [whole],
        True,
        info, phase_one, gated, grad_low, grad_mixed,
        gflop=2,
        mib=6,
    )
    grad_phase_one, grad_two, b_kept, b_sent, c_kept, c_sent, part, sums_two, d_ffn_bias = kernel_call(
        feed_back_kernel,
        [
            low, full, *halves(12), ((32, 2, 24, LANES), BF), ((32, 2, 24, LANES), BF), low,
            ((8, half), F32), ((1, wide), F32),
        ],
        [low, ((rows, wide), BF), ((8, width), F32), whole],
        True,
        info, grad_three, part, swap(part), norm_two, inverse_two, all_rows, activated, slope_up, hidden,
        ffn_in, ffn_out, conv_kept, conv_sent,
        late=(4, 5, 7, 8, 10, 11),
        early=(0,),
        gflop=10,
        mib=20,
    )
    grad_one, a_kept, a_sent, grad_qkv = kernel_call(
        attention_back_kernel,
        [full, *halves(9), ((rows, 3 * half), BF)],
        [low, ((rows, half), BF), ((8, width), F32), whole, ((128, half), F32)],
        True,
        info, grad_two, part, swap(part), norm_one, inverse_one, all_rows, tokens, qkv, attended, soft,
        weights, sums_two, sums_three, d_taps, d_ffn_bias, order,
        late=(4, 5, 7, 8, 9, 10, 11),
        early=(0,),
        gflop=10,
        mib=20,
    )
    (part,) = kernel_call(
        tokens_back_kernel, [low], [], False, grad_qkv, weights, late=(1,), gflop=1, mib=8
    )
    theirs = lax.ppermute(part, "phase", [(1, 0)])
    b_kept, b_sent = halved(b_kept, exchanged(b_sent, "x", 1))
    c_kept, c_sent = halved(c_kept, exchanged(c_sent, "z", 1))
    a_kept, a_sent = halved(after(a_kept, b_sent, c_sent, theirs), exchanged(a_sent, "y", 1))
    b_came = exchanged(b_sent, "x", 0)
    c_kept, c_sent = halved(after(c_kept, b_sent), exchanged(c_sent, "z", 0))
    c_kept, c_sent = halved(c_kept, exchanged(c_sent, "x", 1))
    a_kept, a_sent = halved(after(a_kept, b_came, c_sent), exchanged(a_sent, "y", 0))
    b_kept, b_sent = halved(after(b_kept, a_sent), b_came)
    c_kept, c_sent = halved(c_kept, exchanged(c_sent, "x", 0))
    b_kept, b_sent = (jnp.concatenate(pair, axis=1) for pair in ((b_kept, c_kept), (b_sent, c_sent)))
    b_came = exchanged(b_sent, "y", 1)
    a_kept, a_sent = halved(a_kept, exchanged(a_sent, "x", 1))
    b_kept, b_sent = halved(after(b_kept, a_sent), b_came)
    *pieces, ffn_out_share = kernel_call(
        send_sums_kernel,
        [*[((128, LANES), BF)] * 4, (masters[4].shape, F32)],
        [((24, LANES), F32), ((4, 128, LANES), F32)],
        True,
        info, a_kept, exchanged(a_sent, "x", 0), b_kept, exchanged(b_sent, "y", 0),
    )
    grad_one = after(grad_one, pieces[1])
    shapes = [master.shape for master in masters]
    shapes[3] = (1, shapes[3][0])
    for turned in (6, 8):
        shapes[turned] = shapes[turned][::-1]
    joined, swapped = (1, 3, 6, 7, 8, 9), (0, 2, 5)
    grad_tokens = (grad_one + (part.astype(F32) + theirs.astype(F32))).astype(BF)
    input_grads = jnp.where(lax.axis_index("phase") == 0, grad_tokens, grad_phase_one)
    held, other, *done = kernel_call(
        join_sums_kernel,
        [((8, 6, LANES), F32), ((8, 6, LANES), BF), *((shapes[place], F32) for place in joined)],
        [((128, 128), F32), ((128, LANES), F32)],
        True,
        info, after(pieces[0], input_grads), *(lax.ppermute(pieces[mask], BOTH, across(mask)) for mask in (1, 2, 3)),
    )
    done += kernel_call(
        shares_kernel, [(shapes[place], F32) for place in swapped], [], True, info, held, swap(other)
    )
    shares = dict(zip(joined + swapped, done))
    shares[4] = ffn_out_share
    shares[3] = shares[3].reshape(-1)
    for turned in (6, 8):
        shares[turned] = shares[turned].T
    shares = [shares[place] for place in range(10)]
    return (block_outputs[None], input_grads[None], *shares)


def solution(mesh):
    sharded, columns = P(BOTH, None), P(None, BOTH)
    weights = (sharded, sharded, sharded, P(BOTH), sharded, sharded, columns, sharded, columns, columns)
    return jax.shard_map(
        shards,
        mesh=mesh,
        in_specs=(P("dp", None), P("dp", None), P("dp", None), P("dp"), *weights),
        out_specs=(P("phase", "dp", None), P("phase", "dp", None), *weights),
        check_vma=False,
    )
```

```python
import math

import jax
import jax.numpy as jnp
import numpy as np
from jax import lax
from jax.experimental import pallas as pl
from jax.experimental.pallas import tpu as pltpu
from jax.sharding import PartitionSpec as P

HEAD_DIM = 64
EPSILON = 1e-05
BOTH = ("phase", "dp")
STRIDE = {"x": 16, "y": 4, "z": 1}
AXES = "xyz"
LANES = 384
SLOTS = 6
SWAP = [(0, 1), (1, 0)]
BF = jnp.bfloat16
F32 = jnp.float32


def partners(axis, step):
    pairs = []
    for core in range(2):
        mask = (1, 3)[(core + step) % 2]
        for chip in range(64):
            coordinate = (chip // STRIDE[axis]) % 4
            target = chip + ((coordinate ^ mask) - coordinate) * STRIDE[axis]
            pairs.append((core * 64 + chip, core * 64 + target))
    return pairs


def across(mask):
    return [(device, device + (((device % 4) ^ mask) - device % 4)) for device in range(128)]


def grown(held, axis, step):
    return jnp.concatenate([held, lax.ppermute(held, BOTH, partners(axis, step))])


def exchanged(sent, axis, step):
    return lax.ppermute(sent, BOTH, partners(axis, step))


def halved(kept, came):
    count = kept.shape[0] // 2
    return tuple(
        (kept[there].astype(F32) + came[there].astype(F32)).astype(BF)
        for there in (slice(0, count), slice(count, 2 * count))
    )


def after(value, *others):
    return lax.optimization_barrier((value, *others))[0]


def swap(part):
    return lax.ppermute(part, "phase", SWAP)


def bias_order():
    table = np.zeros((LANES, LANES), np.float32)
    for i in range(4):
        for d in range(16):
            for j in range(6):
                table[96 * i + 6 * d + j, 24 * d + 6 * i + j] = 1.0
    return jnp.asarray(table, BF)


def info_of(lengths, kernel_choice):
    core = lax.axis_index("phase").astype(jnp.int32)
    chip = lax.axis_index("dp").astype(jnp.int32)
    return jnp.concatenate(
        [
            core[None],
            kernel_choice,
            jnp.zeros((3 - kernel_choice.shape[0],), jnp.int32),
            jnp.cumsum(lengths, axis=-1).reshape(-1),
            jnp.stack([(chip // STRIDE[axis]) % 4 for axis in AXES]),
            jnp.stack([1 + 2 * core, 3 - 2 * core]),
        ]
    )


def coordinate_at(info, axis, index):
    here = info[16 + AXES.index(axis)]
    return here ^ (0, info[19], info[20], 2)[index]


def index_at(info, axis, coordinate):
    apart = info[16 + AXES.index(axis)] ^ coordinate
    return jnp.where(
        apart == 0, 0, jnp.where(apart == info[19], 1, jnp.where(apart == info[20], 2, 3))
    )


def outer_inner(order, indices):
    place = 0
    for axis in order:
        place = place * 4 + indices[axis]
    return place


def tall_rows(info, part, order, block, x):
    pieces = []
    for y in range(4):
        place = outer_inner(order, {"x": index_at(info, "x", x), "y": index_at(info, "y", y)})
        pieces.append(part[place, block].astype(F32))
    return jnp.concatenate(pieces, axis=0)


def pack_rows(info, source, order, block, kept, sent, first_row):
    for outer in range(4):
        for inner in range(4):
            place = {order[0]: coordinate_at(info, order[0], outer)}
            place[order[1]] = coordinate_at(info, order[1], inner)
            row = pl.multiple_of(first_row + 96 * place["x"] + 24 * place["y"], 8)
            piece = source[pl.ds(row, 24), :].astype(BF)
            (kept if outer < 2 else sent)[(outer % 2) * 4 + inner, block] = piece


def send_weights_kernel(
    flow, core, qkv, out, ffn_in, ffn_bias, ffn_out, conv_in, conv_taps, conv_out, biases, gains,
    mine, theirs, turned, mine_rows, their_rows,
):
    width = out.shape[1]
    half, wide = width // 2, ffn_in.shape[1] // 2
    turned[...] = jnp.zeros_like(turned)
    flow.arrive()
    turned[9:12, 0:6] = gains[...]
    for i in range(4):
        turned[27 + i : 28 + i, 0:6] = ffn_bias[0:1, 6 * i : 6 * i + 6]
    turned[0:8, :] = jnp.transpose(turned[...])[0:8, :]
    turned[0:6, 0:9] = biases[...]
    turned[0:6, 12:27] = conv_taps[...]
    small = turned[0:6, :]
    blank = jnp.zeros((6, LANES - 128), F32)
    small = jnp.concatenate([small, blank], axis=1)
    mine_rows[120:128, :] = jnp.zeros((8, LANES), F32)
    their_rows[48:56, :] = jnp.zeros((8, LANES), F32)

    def put(target, place, block):
        target[6 * place : 6 * place + 6, :] = block

    def pair(source, first, apart):
        return (source[:, first : first + LANES], source[:, first + apart : first + apart + LANES])

    places = [pair(qkv, third * width, half) for third in range(3)]
    places += [pair(ffn_in, block * LANES, wide) for block in range(4)]
    places.append(pair(conv_in, 0, half))
    for place, (low, high) in enumerate(places):
        put(mine_rows, place, jnp.where(core[0] == 0, low, high))
        put(their_rows, place, jnp.where(core[0] == 0, high, low))
    put(mine_rows, 8, small)
    put(their_rows, 8, small)
    for block in range(2):
        columns = slice(block * LANES, (block + 1) * LANES)
        put(mine_rows, 9 + block, out[:, columns])
        put(mine_rows, 11 + block, conv_out[:, columns])
        for part in range(4):
            put(mine_rows, 13 + block * 4 + part, ffn_out[6 * part : 6 * part + 6, columns])
    mine[...] = mine_rows[...].astype(BF)
    theirs[...] = their_rows[...].astype(BF)


def line_weights_kernel(info, own_rows, first, second, third, part_a, part_b, rows, lines):
    core = info[0]

    for mask, source in enumerate((own_rows, first, second, third)):
        lines[mask] = source[...].astype(F32)

    def piece(z, place):
        row = 6 * place if place < 21 else 128 + 6 * (place - 21)
        return lines[info[18] ^ z, row : row + 6, :]

    def whole(place):
        for z in range(4):
            rows[6 * z : 6 * z + 6, :] = piece(z, place)
        return rows[...]

    for block in range(3):
        part_a[0, block * 2 + core] = whole(block).astype(BF)
        part_a[0, block * 2 + 1 - core] = whole(21 + block).astype(BF)
    for block in range(2):
        part_a[0, 6 + block] = whole(9 + block).astype(BF)
        part_a[0, 11 + block] = whole(11 + block).astype(BF)
    mine = whole(8)[:, :128]
    theirs = whole(29)[:, :128]
    part_a[0, 8] = jnp.concatenate([mine, theirs, jnp.zeros_like(mine)], axis=1).astype(BF)
    part_a[0, 9 + core] = whole(7).astype(BF)
    part_a[0, 10 - core] = whole(28).astype(BF)
    for block in range(4):
        part_b[0, block * 2 + core] = whole(3 + block).astype(BF)
        part_b[0, block * 2 + 1 - core] = whole(24 + block).astype(BF)
    for z in range(4):
        for block in range(2):
            for part in range(4):
                rows[6 * part : 6 * part + 6, :] = piece(z, 13 + block * 4 + part)
            if z < 3:
                part_b[0, 8 + z * 2 + block] = rows[...].astype(BF)
            else:
                part_a[0, 13 + block] = rows[...].astype(BF)


def send_sums_kernel(
    info, a_kept, a_came, b_kept, b_came, kept, first, second, third, ffn_out, rows, lines
):
    core = info[0]
    lines[:, 120:128, :] = jnp.zeros((4, 8, LANES), F32)

    def spread(near, came, place, block):
        rows[...] = near[0, place].astype(F32) + came[0, place].astype(F32)
        pieces = [rows[6 * z : 6 * z + 6, :] for z in range(4)]
        for mask in range(4):
            z = info[18] ^ mask
            low = jnp.where(z % 2 == 0, pieces[0], pieces[1])
            high = jnp.where(z % 2 == 0, pieces[2], pieces[3])
            lines[mask, 6 * block : 6 * block + 6, :] = jnp.where(z < 2, low, high)

    for side, place in ((core, 0), (1 - core, 13)):
        for block in range(3):
            spread(a_kept, a_came, block * 2 + side, place + block)
        for block in range(5):
            spread(b_kept, b_came, block * 2 + side, place + 3 + block)
    spread(a_kept, a_came, 8, 8)
    for block in range(2):
        spread(a_kept, a_came, 6 + block, 9 + block)
        spread(b_kept, b_came, 10 + block, 11 + block)
        ffn_out[:, block * LANES : (block + 1) * LANES] = (
            b_kept[0, 12 + block].astype(F32) + b_came[0, 12 + block].astype(F32)
        )
    for mask, target in enumerate((kept, first, second, third)):
        target[...] = lines[mask].astype(BF)


def join_sums_kernel(
    info, kept, first, second, third,
    held, other, out, ffn_bias, conv_taps, conv_out, biases, gains, turned, lines,
):
    pieces = [source[...].astype(F32) for source in (kept, first, second, third)]
    lines[...] = (pieces[0] + pieces[1]) + (pieces[2] + pieces[3])

    def total(place):
        return lines[6 * place : 6 * place + 6, :]

    for place in range(8):
        held[place] = total(place)
        other[place] = total(13 + place).astype(BF)
    for block in range(2):
        columns = slice(block * LANES, (block + 1) * LANES)
        out[:, columns] = total(9 + block)
        conv_out[:, columns] = total(11 + block)
    turned[...] = jnp.zeros_like(turned)
    turned[0:6, :] = total(8)[:, :128]
    biases[...] = turned[0:6, 0:9]
    conv_taps[...] = turned[0:6, 12:27]
    small = jnp.transpose(turned[...])
    gains[...] = small[9:12, 0:6]
    for i in range(4):
        ffn_bias[0:1, 6 * i : 6 * i + 6] = small[27 + i : 28 + i, 0:6]


def shares_kernel(info, held, came, qkv, ffn_in, conv_in):
    width = conv_in.shape[1]
    half, wide = width // 2, ffn_in.shape[1] // 2

    def put(target, first, apart, place):
        own_columns, other = held[place], came[place].astype(F32)
        target[:, first : first + LANES] = jnp.where(info[0] == 0, own_columns, other)
        target[:, first + apart : first + apart + LANES] = jnp.where(info[0] == 0, other, own_columns)

    for third in range(3):
        put(qkv, third * width, half, third)
    for block in range(4):
        put(ffn_in, block * LANES, wide, 3 + block)
    put(conv_in, 0, half, 7)


def erf_parts(operand):
    cumulative = 0.5 * (1.0 + lax.erf(operand * (0.5**0.5)))
    density = jnp.exp(-0.5 * operand * operand) * (0.5 / math.pi) ** 0.5
    return (cumulative, density)


def dot(left_side, right_side, left_dim=1, right_dim=0):
    return lax.dot_general(
        left_side, right_side, (((left_dim,), (right_dim,)), ((), ())), preferred_element_type=F32
    )


def normed(residual):
    centered = residual - jnp.mean(residual, axis=-1, keepdims=True)
    inverse = lax.rsqrt(jnp.mean(centered * centered, axis=-1, keepdims=True) + EPSILON)
    return (centered * inverse, inverse)


def normed_back(grad, norm, inverse, gain_row):
    scaled = grad * gain_row
    return inverse * (
        scaled
        - jnp.mean(scaled, axis=-1, keepdims=True)
        - norm * jnp.mean(scaled * norm, axis=-1, keepdims=True)
    )


def each(count, size, body):
    def step(index, unused):
        body(pl.ds(pl.multiple_of(index * size, size), size))
        return unused

    lax.fori_loop(0, count, step, 0, unroll=True)


def slots(position, ends, batch):
    number = jnp.zeros(position.shape, jnp.int32)
    for place in range(SLOTS):
        number = number + (position >= ends[4 + SLOTS * batch + place]).astype(jnp.int32)
    return number


def attention_kernel(
    flow, info, tokens, part_a, order, weights, rows, taps, ffn_bias, qkv, attended, soft, part
):
    half, width = attended.shape[1], tokens.shape[1]
    per_batch = soft.shape[1]
    qkv_w, out_w = weights.at[0:width, :], weights.at[width:, 0:width]
    weights[width:, width:] = jnp.zeros((half, half), BF)
    flow.arrive()
    for x in range(4):
        there = slice(96 * x, 96 * x + 96)
        for block in range(3):
            columns = slice(block * LANES, (block + 1) * LANES)
            qkv_w[there, columns] = tall_rows(info, part_a, "yx", block * 2, x).astype(BF)
            below = slice(half + 96 * x, half + 96 * x + 96)
            qkv_w[below, columns] = tall_rows(info, part_a, "yx", block * 2 + 1, x).astype(BF)
        for block in range(2):
            columns = slice(block * LANES, (block + 1) * LANES)
            out_w[there, columns] = tall_rows(info, part_a, "yx", 6 + block, x).astype(BF)
    flow.leave(0)
    small = jnp.concatenate([tall_rows(info, part_a, "yx", 8, x) for x in range(4)], axis=0)
    mine = jnp.transpose(small[:, 0:128])
    theirs = jnp.transpose(small[:, 128:256])
    rows[...] = jnp.zeros_like(rows)
    left, right = jnp.where(info[0] == 0, mine, theirs), jnp.where(info[0] == 0, theirs, mine)
    rows[0:12, :half] = left[0:12, :]
    rows[0:12, half:] = right[0:12, :]
    rows[12:14, :half] = mine[0:2, :]
    rows[14:15, :half] = mine[6:7, :]
    taps[...] = jnp.zeros_like(taps)
    taps[0:15, :] = mine[12:27, :]
    spread = jnp.concatenate(
        [
            jnp.concatenate([mine[27 + i : 28 + i, 96 * x : 96 * x + 96] for i in range(4)], axis=1)
            for x in range(4)
        ]
        + [jnp.zeros((4, half), F32)],
        axis=0,
    )
    spread = dot(spread.astype(BF), order[...])
    for x in range(4):
        ffn_bias[0:1, x * LANES : (x + 1) * LANES] = spread[x : x + 1, :]
    for third in range(3):
        columns = slice(third * half, (third + 1) * half)
        block = dot(tokens[...], qkv_w[:, columns])
        if third != 1:
            block = block + rows[12 + third // 2 : 13 + third // 2, :half]
        qkv[:, columns] = block.astype(BF)
    square = (per_batch, per_batch)
    down = lax.broadcasted_iota(jnp.int32, square, 0)
    across = lax.broadcasted_iota(jnp.int32, square, 1)
    lane = lax.broadcasted_iota(jnp.int32, (per_batch, 128), 1)
    pairs = half // 128
    for batch in range(tokens.shape[0] // per_batch):
        there = slice(batch * per_batch, (batch + 1) * per_batch)
        slot_down, slot_across = slots(down, info, batch), slots(across, info, batch)
        allowed = (slot_down == slot_across) & ((slot_across < SLOTS - 1) | (down == across))
        forbidden = jnp.where(allowed, 0.0, -1e9)
        for pair in range(pairs):
            columns = slice(pair * 128, (pair + 1) * 128)
            query = qkv[there, columns]
            key = qkv[there, half + pair * 128 : half + (pair + 1) * 128]
            value = qkv[there, 2 * half + pair * 128 : 2 * half + (pair + 1) * 128]
            result = jnp.zeros((per_batch, 128), F32)
            for side in range(2):
                mine = (lane >= HEAD_DIM) if side else (lane < HEAD_DIM)
                scores = dot(jnp.where(mine, query, jnp.zeros_like(query)), key, 1, 1)
                scores = scores * HEAD_DIM ** (-0.5) + forbidden
                exponent = jnp.exp(scores - jnp.max(scores, axis=-1, keepdims=True))
                weight = (exponent * (1.0 / jnp.sum(exponent, axis=-1, keepdims=True))).astype(BF)
                soft[(batch * pairs + pair) * 2 + side] = weight
                result = result + dot(weight, jnp.where(mine, value, jnp.zeros_like(value)))
            attended[there, columns] = result.astype(BF)
    flow.leave(4, 5, 6)
    part[...] = dot(attended[...], out_w[...]).astype(BF)


def feed_kernel(
    flow, info, tokens, mine, theirs, rows, part_b, part_a, ffn_bias,
    ffn_in, ffn_out, conv_in, conv_out, hidden, norm, inverse, activated, slope, part,
):
    half = conv_in.shape[1]

    def first(there):
        residual = (
            tokens[there, :].astype(F32)
            + (mine[there, :].astype(F32) + theirs[there, :].astype(F32))
            + rows[2:3, :]
        )
        unit, scale = normed(residual)
        norm[there, :] = unit
        inverse[there, :] = jnp.broadcast_to(scale, (scale.shape[0], 128))
        hidden[there, :] = (unit * rows[9:10, :] + rows[3:4, :]).astype(BF)

    each(tokens.shape[0] // 64, 64, first)
    flow.leave(5, 6)
    flow.arrive(5, 6)
    for x in range(4):
        for side in range(2):
            there = slice(half * side + 96 * x, half * side + 96 * x + 96)
            for block in range(4):
                columns = slice(block * LANES, (block + 1) * LANES)
                ffn_in[there, columns] = tall_rows(info, part_b, "xy", block * 2 + side, x).astype(BF)
            conv_in[there, :] = tall_rows(info, part_a, "yx", side, x).astype(BF)
        for block in range(2):
            columns = slice(block * LANES, (block + 1) * LANES)
            conv_out[96 * x : 96 * x + 96, columns] = tall_rows(info, part_a, "yx", 2 + block, x).astype(BF)
    flow.leave(0)
    wide = ffn_in.shape[1]
    chunk = 512

    def second(index, unused):
        columns = pl.ds(pl.multiple_of(index * chunk, chunk), chunk)
        up = dot(hidden[...], ffn_in[:, columns]) + ffn_bias[0:1, columns]
        cumulative, density = erf_parts(up)
        activated[:, columns] = (up * cumulative).astype(BF)
        slope[:, columns] = (cumulative + up * density).astype(BF)
        return unused

    lax.fori_loop(0, wide // chunk, second, 0, unroll=True)
    flow.leave(7, 8)
    for x in range(4):
        for y in range(4):
            for block in range(2):
                indices = {"x": index_at(info, "x", x), "y": index_at(info, "y", y)}
                place = outer_inner("xy", indices)
                pieces = [part_b[place, 8 + z * 2 + block].astype(F32) for z in range(3)]
                pieces.append(part_a[outer_inner("yx", indices), 4 + block].astype(F32))
                row = 384 * x + 96 * y
                ffn_out[row : row + 96, block * LANES : (block + 1) * LANES] = jnp.concatenate(
                    pieces, axis=0
                ).astype(BF)
    flow.leave(1)
    part[...] = dot(activated[...], ffn_out[...]).astype(BF)


def tap_row(taps, info, batch, offset):
    choice = info[1 + batch]
    row = taps[11 + offset : 12 + offset, :]
    row = jnp.where(choice == 1, taps[5 + offset : 6 + offset, :] if abs(offset) < 3 else 0.0, row)
    return jnp.where(choice == 0, taps[1 + offset : 2 + offset, :] if abs(offset) < 2 else 0.0, row)


def fill_slots(info, padded, per_batch, batches):
    position = lax.broadcasted_iota(jnp.int32, (per_batch, 128), 0)
    outside = jnp.full((8, 128), -1, jnp.int32)
    for batch in range(batches):
        padded[batch, 0:8, :] = outside
        padded[batch, 8 : 8 + per_batch, :] = slots(position, info, batch)
        padded[batch, 8 + per_batch :, :] = outside


def clear_edges(padded, per_batch, batches):
    edge = jnp.zeros((8, padded.shape[2]), F32)
    for batch in range(batches):
        padded[batch, 0:8, :] = edge
        padded[batch, 8 + per_batch :, :] = edge


def convolution_kernel(
    flow, info, hidden, mine, theirs, rows, conv_in, taps, conv_out,
    phase_one, norm, inverse, mixed, gated, slope, part, slot_pad, mixed_pad,
):
    batches = slot_pad.shape[0]
    per_batch = hidden.shape[0] // batches
    half = conv_in.shape[1]

    def first(there):
        residual = (
            hidden[there, :].astype(F32)
            + (mine[there, :].astype(F32) + theirs[there, :].astype(F32))
            + rows[4:5, :]
        )
        unit, scale = normed(residual)
        norm[there, :] = unit
        inverse[there, :] = jnp.broadcast_to(scale, (scale.shape[0], 128))
        phase_one[there, :] = (unit * rows[10:11, :] + rows[5:6, :]).astype(BF)

    each(hidden.shape[0] // 64, 64, first)
    flow.leave(1, 2)
    fill_slots(info, slot_pad, per_batch, batches)
    clear_edges(mixed_pad, per_batch, batches)
    mixed[...] = dot(phase_one[...], conv_in[...]) + rows[14:15, :half]
    for batch in range(batches):
        there = slice(batch * per_batch, (batch + 1) * per_batch)
        mixed_pad[batch, 8 : 8 + per_batch, :] = mixed[there, :]
        for column in range(half // 128):
            columns = slice(column * 128, (column + 1) * 128)
            here = slot_pad[batch, 8 : 8 + per_batch, :]
            total = jnp.zeros((per_batch, 128), F32)
            for offset in range(-3, 4):
                same = slot_pad[batch, 8 + offset : 8 + offset + per_batch, :] == here
                moved = mixed_pad[batch, 8 + offset : 8 + offset + per_batch, columns]
                tap = tap_row(taps, info, batch, offset)[:, columns]
                total = total + jnp.where(same, moved, 0.0) * tap
            cumulative, density = erf_parts(total)
            gated[there, columns] = (total * cumulative).astype(BF)
            slope[there, columns] = cumulative + total * density
    part[...] = dot(gated[...], conv_out[...]).astype(BF)


def own(info, row):
    half = row.shape[1] // 2
    return jnp.where(info[0] == 0, row[:, :half], row[:, half:])


def convolution_back_kernel(
    flow, info, phase_one, mine, theirs, cotangent, rows, conv_in, taps, conv_out, mixed, gated, slope,
    result, grad_three, grad_low, grad_mixed, part, sums, d_taps,
    slot_pad, mixed_pad, grad_pad, wide_sums,
):
    batches = slot_pad.shape[0]
    per_batch = phase_one.shape[0] // batches
    half = conv_in.shape[1]
    fill_slots(info, slot_pad, per_batch, batches)
    clear_edges(mixed_pad, per_batch, batches)
    clear_edges(grad_pad, per_batch, batches)
    wide_sums[...] = jnp.zeros_like(wide_sums)
    flow.arrive()
    size = 64
    for batch in range(batches):

        def first(index, unused):
            inner = pl.multiple_of(index * size, size)
            there = pl.ds(pl.multiple_of(batch * per_batch + inner, size), size)
            residual = (
                phase_one[there, :].astype(F32)
                + (mine[there, :].astype(F32) + theirs[there, :].astype(F32))
                + rows[7:8, :]
            )
            unit, scale = normed(residual)
            ended = (unit * rows[11:12, :] + rows[8:9, :]).astype(BF)
            result[there, :] = jnp.where(info[0] == 0, phase_one[there, :], ended)
            valid = slot_pad[batch, pl.ds(pl.multiple_of(8 + inner, 8), size), :][:, :1] < SLOTS - 1
            masked = jnp.where(valid, cotangent[there, :].astype(F32), 0.0)
            grad = normed_back(masked, unit, scale, rows[11:12, :])
            grad_three[there, :] = grad
            low = grad.astype(BF)
            grad_low[there, :] = low
            wide_sums[0:1, :] += jnp.sum(low.astype(F32), axis=0, keepdims=True)
            wide_sums[1:2, :] += jnp.sum(masked, axis=0, keepdims=True)
            wide_sums[2:3, :] += jnp.sum(masked * unit, axis=0, keepdims=True)
            return unused

        lax.fori_loop(0, per_batch // size, first, 0, unroll=True)
    flow.leave(0)
    tap_sums = [[[] for offset in range(7)] for batch in range(batches)]
    for batch in range(batches):
        there = slice(batch * per_batch, (batch + 1) * per_batch)
        grad_pad[batch, 8 : 8 + per_batch, :] = (
            dot(grad_low[there, :], conv_out[...], 1, 1) * slope[there, :]
        )
        mixed_pad[batch, 8 : 8 + per_batch, :] = mixed[there, :]
        for column in range(half // 128):
            columns = slice(column * 128, (column + 1) * 128)
            here = slot_pad[batch, 8 : 8 + per_batch, :]
            grad = grad_pad[batch, 8 : 8 + per_batch, columns]
            total = jnp.zeros((per_batch, 128), F32)
            for offset in range(-3, 4):
                away = slice(8 + offset, 8 + offset + per_batch)
                same = slot_pad[batch, away, :] == here
                tap = tap_row(taps, info, batch, -offset)[:, columns]
                total = total + jnp.where(same, grad_pad[batch, away, columns], 0.0) * tap
                term = jnp.where(same, mixed_pad[batch, away, columns], 0.0) * grad
                tap_sums[batch][offset + 3].append(jnp.sum(term, axis=0, keepdims=True))
            grad_mixed[there, columns] = total.astype(BF)
    for choice in range(3):
        for offset in range(-choice - 1, choice + 2):
            row = choice * choice + 2 * choice + offset + choice + 1
            total = jnp.zeros((1, half), F32)
            for batch in range(batches):
                joined = jnp.concatenate(tap_sums[batch][offset + 3], axis=1)
                total = total + jnp.where(info[1 + batch] == choice, joined, 0.0)
            d_taps[row : row + 1, :] = total
    d_taps[15:16, :] = jnp.zeros((1, half), F32)
    part[...] = dot(grad_mixed[...], conv_in[...], 1, 1).astype(BF)
    sums[0:1, :] = jnp.sum(grad_mixed[...].astype(F32), axis=0, keepdims=True)
    for place in range(3):
        sums[place + 1 : place + 2, :] = own(info, wide_sums[place : place + 1, :])
    sums[4:8, :] = jnp.zeros((4, half), F32)


def convolution_sums_kernel(info, phase_one, gated, grad_low, grad_mixed, kept, sent, whole):
    half = gated.shape[1]
    for block in range(2):
        columns = slice(block * LANES, (block + 1) * LANES)
        whole[0:half, :] = dot(gated[...], grad_low[:, columns], 0, 0)
        pack_rows(info, whole, "xy", 2 + block, kept, sent, 0)
    whole[...] = dot(phase_one[...], grad_mixed[...], 0, 0)
    for side in range(2):
        pack_rows(info, whole, "xy", side, kept, sent, side * half)


def feed_back_kernel(
    flow, info, grad_three, mine, theirs, norm, inverse, rows, activated, slope, hidden, ffn_in, ffn_out,
    conv_kept, conv_sent,
    grad_phase_one, grad_two, b_kept, b_sent, c_kept, c_sent, part, sums, bias_sums,
    grad_low, grad_up, wide_sums, whole,
):
    wide_sums[...] = jnp.zeros_like(wide_sums)
    flow.arrive(4, 5)

    def first(there):
        arriving = grad_three[there, :] + (mine[there, :].astype(F32) + theirs[there, :].astype(F32))
        arriving = arriving.astype(BF)
        grad_phase_one[there, :] = arriving
        arriving = arriving.astype(F32)
        unit = norm[there, :]
        grad = normed_back(arriving, unit, inverse[there, :1], rows[10:11, :])
        grad_two[there, :] = grad
        low = grad.astype(BF)
        grad_low[there, :] = low
        wide_sums[0:1, :] += jnp.sum(low.astype(F32), axis=0, keepdims=True)
        wide_sums[1:2, :] += jnp.sum(arriving, axis=0, keepdims=True)
        wide_sums[2:3, :] += jnp.sum(arriving * unit, axis=0, keepdims=True)

    each(hidden.shape[0] // 64, 64, first)
    flow.leave(0)
    flow.arrive(7, 8, 10, 11)
    half = ffn_in.shape[0] // 2
    for block in range(ffn_in.shape[1] // LANES):
        columns = slice(block * LANES, (block + 1) * LANES)
        grad = dot(grad_low[...], ffn_out[columns, :], 1, 1) * slope[:, columns].astype(F32)
        low = grad.astype(BF)
        grad_up[:, columns] = low
        bias_sums[0:1, columns] = jnp.sum(low.astype(F32), axis=0, keepdims=True)
        whole[...] = dot(hidden[...], low, 0, 0)
        for side in range(2):
            pack_rows(info, whole, "xy", block * 2 + side, b_kept, b_sent, side * half)
    for place in range(8):
        for block in range(4):
            b_kept[place, 8 + block] = conv_kept[place, block]
            b_sent[place, 8 + block] = conv_sent[place, block]
    for step in range(4):
        x = coordinate_at(info, "x", step)
        there = pl.ds(pl.multiple_of(x * 384, 128), 384)
        for block in range(2):
            columns = slice(block * LANES, (block + 1) * LANES)
            whole[0:384, :] = dot(activated[:, there], grad_low[:, columns], 0, 0)
            for outer in range(4):
                for inner in range(4):
                    z, y = coordinate_at(info, "z", outer), coordinate_at(info, "y", inner)
                    piece = whole[pl.ds(pl.multiple_of(96 * y + 24 * z, 8), 24), :].astype(BF)
                    place = ((outer % 2) * 4 + step) * 4 + inner
                    (c_kept if outer < 2 else c_sent)[place, block] = piece
    part[...] = dot(grad_up[...], ffn_in[...], 1, 1).astype(BF)
    for place in range(3):
        sums[place : place + 1, :] = own(info, wide_sums[place : place + 1, :])
    sums[3:8, :] = jnp.zeros((5, sums.shape[1]), F32)


def attention_back_kernel(
    flow, info, grad_two, mine, theirs, norm, inverse, rows, tokens, qkv, attended, soft, weights,
    sums_two, sums_three, d_taps, bias_sums, order,
    grad_one, kept, sent, grad_qkv, grad_low, grad_attended, wide_sums, whole, sums,
):
    flow.arrive(4, 5)
    half, width = attended.shape[1], tokens.shape[1]
    out_w = weights.at[width:, 0:width]
    per_batch = soft.shape[1]
    wide_sums[...] = jnp.zeros_like(wide_sums)

    def first(there):
        arriving = grad_two[there, :] + (mine[there, :].astype(F32) + theirs[there, :].astype(F32))
        unit = norm[there, :]
        grad = normed_back(arriving, unit, inverse[there, :1], rows[9:10, :])
        grad_one[there, :] = grad
        low = grad.astype(BF)
        grad_low[there, :] = low
        wide_sums[0:1, :] += jnp.sum(low.astype(F32), axis=0, keepdims=True)
        wide_sums[1:2, :] += jnp.sum(arriving, axis=0, keepdims=True)
        wide_sums[2:3, :] += jnp.sum(arriving * unit, axis=0, keepdims=True)

    each(tokens.shape[0] // 64, 64, first)
    flow.leave(0)
    flow.arrive(7, 8, 9, 10, 11)
    for block in range(2):
        columns = slice(block * LANES, (block + 1) * LANES)
        whole[0:half, :] = dot(attended[...], grad_low[:, columns], 0, 0)
        pack_rows(info, whole, "yx", 6 + block, kept, sent, 0)
    grad_attended[...] = dot(grad_low[...], out_w[...], 1, 1).astype(BF)
    lane = lax.broadcasted_iota(jnp.int32, (per_batch, 128), 1)
    pairs = half // 128
    scale = HEAD_DIM ** (-0.5)
    for batch in range(tokens.shape[0] // per_batch):
        there = slice(batch * per_batch, (batch + 1) * per_batch)
        for pair in range(pairs):
            columns = [
                slice(third * half + pair * 128, third * half + (pair + 1) * 128) for third in range(3)
            ]
            query, key, value = (qkv[there, columns[third]] for third in range(3))
            grad = grad_attended[there, columns[0]]
            totals = [jnp.zeros((per_batch, 128), F32) for third in range(3)]
            for side in range(2):
                mine_lanes = (lane >= HEAD_DIM) if side else (lane < HEAD_DIM)

                def only(operand):
                    return jnp.where(mine_lanes, operand, jnp.zeros_like(operand))

                weight = soft[(batch * pairs + pair) * 2 + side]
                grad_side = only(grad)
                grad_soft = dot(grad_side, value, 1, 1)
                weight_wide = weight.astype(F32)
                inner = jnp.sum(grad_soft * weight_wide, axis=-1, keepdims=True)
                grad_scores = (weight_wide * (grad_soft - inner)).astype(BF)
                totals[0] = totals[0] + dot(grad_scores, only(key))
                totals[1] = totals[1] + dot(grad_scores, only(query), 0, 0)
                totals[2] = totals[2] + dot(weight, grad_side, 0, 0)
            grad_qkv[there, columns[0]] = (totals[0] * scale).astype(BF)
            grad_qkv[there, columns[1]] = (totals[1] * scale).astype(BF)
            grad_qkv[there, columns[2]] = totals[2].astype(BF)
    sums[...] = jnp.zeros_like(sums)
    for third in range(3):
        columns = slice(third * half, (third + 1) * half)
        whole[...] = dot(tokens[...], grad_qkv[:, columns], 0, 0)
        for side in range(2):
            pack_rows(info, whole, "yx", third * 2 + side, kept, sent, side * half)
        if third != 1:
            place = third // 2
            sums[place : place + 1, :] = jnp.sum(
                grad_qkv[:, columns].astype(F32), axis=0, keepdims=True
            )
    sums[2:3, :] = own(info, wide_sums[0:1, :])
    sums[3:4, :] = own(info, wide_sums[1:2, :])
    sums[4:6, :] = sums_two[0:2, :]
    sums[6:9, :] = sums_three[0:3, :]
    sums[9:10, :] = own(info, wide_sums[2:3, :])
    sums[10:11, :] = sums_two[2:3, :]
    sums[11:12, :] = sums_three[3:4, :]
    sums[12:27, :] = d_taps[0:15, :]
    spread = jnp.concatenate(
        [bias_sums[0:1, x * LANES : (x + 1) * LANES] for x in range(4)] + [jnp.zeros((4, half), F32)], axis=0
    )
    spread = dot(spread.astype(BF), order[...], 1, 1)
    for i in range(4):
        sums[27 + i : 28 + i, :] = jnp.concatenate(
            [spread[x : x + 1, 96 * i : 96 * i + 96] for x in range(4)], axis=1
        )
    whole[0:half, :] = jnp.zeros((half, LANES), F32)
    whole[0:half, 0:128] = jnp.transpose(sums[...])
    pack_rows(info, whole, "yx", 8, kept, sent, 0)


def tokens_back_kernel(flow, grad_qkv, weights, part):
    flow.arrive()
    part[...] = dot(grad_qkv[...], weights[0 : part.shape[1], :], 1, 1).astype(BF)


class Flow:
    def __init__(self):
        self.coming, self.going = {}, {}

    def arrive(self, *chosen):
        for which in chosen or tuple(self.coming):
            for copy in self.coming[which]:
                copy.wait()

    def leave(self, *chosen):
        for which in chosen:
            self.going[which].start()


def kernel_call(body, outputs, scratch, has_info, *operands, late=(), early=(), mib=4, gflop=0):
    vmem = pl.BlockSpec(memory_space=pltpu.VMEM)
    smem = pl.BlockSpec(memory_space=pltpu.SMEM)
    hbm = pl.BlockSpec(memory_space=pltpu.HBM)
    groups = [operand if isinstance(operand, tuple) else (operand,) for operand in operands]
    arrays = [array for group in groups for array in group]
    moves = sum(len(groups[which]) for which in late) + len(early)

    def with_copies(*refs):
        taken = 0
        operand_refs = []
        for group in groups:
            operand_refs.append(refs[taken : taken + len(group)])
            taken += len(group)
        output_refs = list(refs[taken : taken + len(outputs)])
        own = refs[taken + len(outputs) : taken + len(outputs) + len(scratch)]
        buffers = list(refs[taken + len(outputs) + len(scratch) : -1])
        flags, used = refs[-1], 0
        flow = Flow()
        for which in late:
            buffer = buffers.pop(0)
            first, flow.coming[which] = 0, []
            for source in operand_refs[which]:
                count = source.shape[0]
                target = buffer if len(groups[which]) == 1 else buffer.at[pl.ds(first, count)]
                copy = pltpu.make_async_copy(source, target, flags.at[used])
                copy.start()
                flow.coming[which].append(copy)
                first, used = first + count, used + 1
            operand_refs[which] = (buffer,)
        for which in early:
            buffer = buffers.pop(0)
            flow.going[which] = pltpu.make_async_copy(buffer, output_refs[which], flags.at[used])
            output_refs[which] = buffer
            used += 1
        body(flow, *(group[0] for group in operand_refs), *output_refs, *own)
        for which in early:
            flow.going[which].wait()

    specs = [smem if has_info and place == 0 else vmem for place in range(len(operands))]
    out_specs = [vmem] * len(outputs)
    memory = [pltpu.VMEM(shape, dtype) for shape, dtype in scratch]
    for which in late:
        specs[which] = hbm
        whole = sum(array.shape[0] for array in groups[which])
        memory.append(pltpu.VMEM((whole, *groups[which][0].shape[1:]), groups[which][0].dtype))
    for which in early:
        out_specs[which] = hbm
        memory.append(pltpu.VMEM(*outputs[which]))
    if moves:
        memory.append(pltpu.SemaphoreType.DMA((moves,)))
    return pl.pallas_call(
        with_copies if moves else body,
        out_shape=[jax.ShapeDtypeStruct(shape, dtype) for shape, dtype in outputs],
        in_specs=[spec for spec, group in zip(specs, groups) for array in group],
        out_specs=out_specs,
        scratch_shapes=memory,
        compiler_params=pltpu.CompilerParams(vmem_limit_bytes=mib * 1024 * 1024),
        cost_estimate=pl.CostEstimate(flops=int(gflop * 1e9), bytes_accessed=1 << 20, transcendentals=0),
    )(*arrays)


def gather_weights(info, masters):
    (qkv, out, ffn_in, ffn_bias, ffn_out, conv_in, conv_taps, conv_out, biases, gains) = masters
    mine, theirs = kernel_call(
        send_weights_kernel,
        [((128, LANES), BF), ((56, LANES), BF)],
        [((128, 128), F32), ((128, LANES), F32), ((56, LANES), F32)],
        True,
        lax.axis_index("phase").astype(jnp.int32).reshape(1), qkv, out, ffn_in, ffn_bias.reshape(1, -1), ffn_out,
        conv_in, conv_taps.T, conv_out, biases.T, gains,
        late=tuple(range(1, 11)),
        mib=60,
    )

    def together(*values):
        return lax.optimization_barrier(values)

    line = jnp.concatenate([mine, swap(theirs)])
    part_a, part_b = kernel_call(
        line_weights_kernel,
        [((1, 15, 24, LANES), BF), ((1, 14, 24, LANES), BF)],
        [((24, LANES), F32), ((4, 184, LANES), F32)],
        True,
        info, line, *(lax.ppermute(line, BOTH, across(mask)) for mask in (1, 2, 3)),
    )
    for step in range(2):
        part_a, part_b = together(grown(part_a, "x", step), grown(part_b, "y", step))
    came = lax.ppermute(part_a, BOTH, partners("y", 0))
    early, late, part_b = together(
        jnp.concatenate([part_a[:, :9], came[:, :9]]),
        jnp.concatenate([part_a[:, 9:], came[:, 9:]]),
        grown(part_b, "x", 0),
    )
    return (
        (early, lax.ppermute(early, BOTH, partners("y", 1))),
        (late, lax.ppermute(late, BOTH, partners("y", 1))),
        (part_b, lax.ppermute(part_b, BOTH, partners("x", 1))),
    )


def shards(
    tokens,
    cotangent,
    lengths,
    kernel_choice,
    *masters,
):
    batches = lengths.shape[0]
    rows, width = tokens.shape
    per_batch = rows // batches
    half = width // 2
    wide = masters[2].shape[1] // 2
    heads = half // HEAD_DIM
    info = info_of(lengths, kernel_choice)
    part_a, rest, part_b = gather_weights(info, masters)
    order = bias_order()
    low, full = ((rows, width), BF), ((rows, width), F32)
    narrow = ((rows, 128), F32)
    slot_pad = ((batches, per_batch + 16, 128), jnp.int32)
    row_pad = ((batches, per_batch + 16, half), F32)
    whole = ((width, LANES), F32)

    def halves(blocks):
        return [((8, blocks, 24, LANES), BF)] * 2

    weights, all_rows, taps, ffn_bias, qkv, attended, soft, part = kernel_call(
        attention_kernel,
        [
            ((width + half, 3 * half), BF), ((16, width), F32),
            ((16, half), F32), ((1, wide), F32), ((rows, 3 * half), BF), ((rows, half), BF),
            ((batches * heads, per_batch, per_batch), BF), low,
        ],
        [],
        True,
        info, tokens, part_a, order,
        late=(2,),
        early=(0, 4, 5, 6),
        gflop=5,
        mib=16,
    )
    ffn_in, ffn_out, conv_in, conv_out, hidden, norm_one, inverse_one, activated, slope_up, part_two = kernel_call(
        feed_kernel,
        [
            ((width, wide), BF), ((wide, width), BF), ((width, half), BF), ((half, width), BF), low, full, narrow, ((rows, wide), BF), ((rows, wide), BF), low,
        ],
        [],
        True,
        info, tokens, part, swap(part), all_rows, part_b, rest, ffn_bias,
        late=(5, 6),
        early=(0, 1, 5, 6, 7, 8),
        gflop=8,
        mib=24,
    )
    phase_one, norm_two, inverse_two, mixed, gated, slope, part_three = kernel_call(
        convolution_kernel,
        [low, full, narrow, ((rows, half), F32), ((rows, half), BF), ((rows, half), F32), low],
        [slot_pad, row_pad],
        True,
        info, hidden, part_two, swap(part_two), all_rows, conv_in, taps, conv_out,
        early=(1, 2),
        gflop=4,
        mib=8,
    )
    block_outputs, grad_three, grad_low, grad_mixed, part, sums_three, d_taps = kernel_call(
        convolution_back_kernel,
        [low, full, low, ((rows, half), BF), low, ((8, half), F32), ((16, half), F32)],
        [slot_pad, row_pad, row_pad, ((8, width), F32)],
        True,
        info, phase_one, part_three, swap(part_three), cotangent, all_rows, conv_in, taps, conv_out,
        mixed, gated, slope,
        late=(4,),
        early=(0,),
        gflop=8,
        mib=10,
    )
    conv_kept, conv_sent = kernel_call(
        convolution_sums_kernel,
        halves(4),
        [whole],
        True,
        info, phase_one, gated, grad_low, grad_mixed,
        gflop=2,
        mib=6,
    )
    grad_phase_one, grad_two, b_kept, b_sent, c_kept, c_sent, part, sums_two, d_ffn_bias = kernel_call(
        feed_back_kernel,
        [
            low, full, *halves(12), ((32, 2, 24, LANES), BF), ((32, 2, 24, LANES), BF), low,
            ((8, half), F32), ((1, wide), F32),
        ],
        [low, ((rows, wide), BF), ((8, width), F32), whole],
        True,
        info, grad_three, part, swap(part), norm_two, inverse_two, all_rows, activated, slope_up, hidden,
        ffn_in, ffn_out, conv_kept, conv_sent,
        late=(4, 5, 7, 8, 10, 11),
        early=(0,),
        gflop=10,
        mib=20,
    )
    grad_one, a_kept, a_sent, grad_qkv = kernel_call(
        attention_back_kernel,
        [full, *halves(9), ((rows, 3 * half), BF)],
        [low, ((rows, half), BF), ((8, width), F32), whole, ((128, half), F32)],
        True,
        info, grad_two, part, swap(part), norm_one, inverse_one, all_rows, tokens, qkv, attended, soft,
        weights, sums_two, sums_three, d_taps, d_ffn_bias, order,
        late=(4, 5, 7, 8, 9, 10, 11),
        early=(0,),
        gflop=10,
        mib=20,
    )
    (part,) = kernel_call(
        tokens_back_kernel, [low], [], False, grad_qkv, weights, late=(1,), gflop=1, mib=8
    )
    theirs = lax.ppermute(part, "phase", [(1, 0)])
    b_kept, b_sent = halved(b_kept, exchanged(b_sent, "x", 1))
    c_kept, c_sent = halved(c_kept, exchanged(after(c_sent, a_sent), "z", 1))
    a_kept, a_sent = halved(after(a_kept, b_sent, c_sent, theirs), exchanged(a_sent, "y", 1))
    b_came = exchanged(b_sent, "x", 0)
    c_kept, c_sent = halved(after(c_kept, b_sent), exchanged(c_sent, "z", 0))
    c_kept, c_sent = halved(c_kept, exchanged(c_sent, "x", 1))
    a_kept, a_sent = halved(after(a_kept, b_came, c_sent), exchanged(a_sent, "y", 0))
    b_kept, b_sent = halved(after(b_kept, a_sent), b_came)
    c_kept, c_sent = halved(c_kept, exchanged(c_sent, "x", 0))
    b_kept, b_sent = (jnp.concatenate(pair, axis=1) for pair in ((b_kept, c_kept), (b_sent, c_sent)))
    b_came = exchanged(b_sent, "y", 1)
    a_kept, a_sent = halved(a_kept, exchanged(a_sent, "x", 1))
    b_kept, b_sent = halved(after(b_kept, a_sent), b_came)
    *pieces, ffn_out_share = kernel_call(
        send_sums_kernel,
        [*[((128, LANES), BF)] * 4, (masters[4].shape, F32)],
        [((24, LANES), F32), ((4, 128, LANES), F32)],
        True,
        info, a_kept, exchanged(a_sent, "x", 0), b_kept, exchanged(b_sent, "y", 0),
    )
    grad_one = after(grad_one, pieces[1])
    shapes = [master.shape for master in masters]
    shapes[3] = (1, shapes[3][0])
    for turned in (6, 8):
        shapes[turned] = shapes[turned][::-1]
    joined, swapped = (1, 3, 6, 7, 8, 9), (0, 2, 5)
    held, other, *done = kernel_call(
        join_sums_kernel,
        [((8, 6, LANES), F32), ((8, 6, LANES), BF), *((shapes[place], F32) for place in joined)],
        [((128, 128), F32), ((128, LANES), F32)],
        True,
        info, pieces[0], *(lax.ppermute(pieces[mask], BOTH, across(mask)) for mask in (1, 2, 3)),
    )
    done += kernel_call(
        shares_kernel, [(shapes[place], F32) for place in swapped], [], True, info, held, swap(other)
    )
    shares = dict(zip(joined + swapped, done))
    shares[4] = ffn_out_share
    shares[3] = shares[3].reshape(-1)
    for turned in (6, 8):
        shares[turned] = shares[turned].T
    shares = [shares[place] for place in range(10)]
    grad_tokens = (grad_one + (part.astype(F32) + theirs.astype(F32))).astype(BF)
    input_grads = jnp.where(lax.axis_index("phase") == 0, grad_tokens, grad_phase_one)
    return (block_outputs[None], input_grads[None], *shares)


def solution(mesh):
    sharded, columns = P(BOTH, None), P(None, BOTH)
    weights = (sharded, sharded, sharded, P(BOTH), sharded, sharded, columns, sharded, columns, columns)
    return jax.shard_map(
        shards,
        mesh=mesh,
        in_specs=(P("dp", None), P("dp", None), P("dp", None), P("dp"), *weights),
        out_specs=(P("phase", "dp", None), P("phase", "dp", None), *weights),
        check_vma=False,
    )
```
